32 devices in a mesh: gx: 8 (over z, y), gy: 2 (over x), depth: 2 (over core).
Axes of the slice: x: 2, y: 2, z: 4, core: 2. Of those that a mesh axis runs over, the one named last changes fastest.
Arguments:
- adjoint: float32 [19, 24, 32, 1024], P(None, 'depth', 'gy', 'gx'), may hold values from -6 to 6
- momentum: float32 [3, 24, 32, 1024], P(None, 'depth', 'gy', 'gx'), may hold values from -4 to 4
- design: float32 [32, 1024], P('gy', 'gx'), may hold values from 0 to 1
- solid_mask: int32 [24, 32, 1024], P('depth', 'gy', 'gx'), may hold values 0 or 1
- port_label: int32 [24, 32, 1024], P('depth', 'gy', 'gx'), may hold values from 0 to 2, as said below
Outputs:
- new_adjoint: float32 [19, 24, 32, 1024], P(None, 'depth', 'gy', 'gx')
- sensitivity: float32 [32, 1024], P('gy', 'gx')
The draws below stay inside these ranges and needn't reach their ends.
Inputs may be any that keep to these rules, and one draw needn't show every extreme that they name: `solid_mask`: 1 marks a solid cell, 0 a fluid one. `port_label`: 0 marks an ordinary cell, 1 an inlet cell, 2 an outlet cell.
All inputs are finite; a program needn't handle non-finite values. No bound on the sum of `solid_mask` on one device may be relied on, other than what follows from the above.
Results may differ from the reference program's by a relative error of at most 0.00012.
Values sent between devices are 32-bit elements; how exact they have to be, the bound alone decides.
No kernel may reach another device: no remote copies, remote signals or barrier semaphores. Data moves between devices by JAX's collectives and lax.ppermute only.
A program may use at most 128 MiB of HBM per device.

```python
import math
import jax
import jax.numpy as jnp
from jax import lax

VELOCITIES = 19
NX = 1024
NY = 32
NZ = 24


def draw_port_label(key, part):
    picks = jax.random.randint(key, (NZ, NY, NX), 0, 16)
    return jnp.where(picks == 0, 1, jnp.where(picks == 1, 2, 0)).astype(jnp.int32)


def set_ends(entries, own_key, low, top_value):
    shape = entries.shape
    place = [jax.random.randint(jax.random.fold_in(own_key, axis), (), 0, shape[axis]) for axis in range(len(shape))]
    entries = entries.at[tuple(place)].set(low)
    longest = shape.index(max(shape))
    place[longest] = (place[longest] + 1) % shape[longest]
    return entries.at[tuple(place)].set(top_value)


def block_scale(rng, dims, shards, low, top_value):
    gain = 1.0
    for dim, parts in shards:
        steps = jax.random.uniform(jax.random.fold_in(jax.random.fold_in(rng, 6), dim), (parts,), jnp.float32, low / len(shards), top_value / len(shards))
        gain = gain * jnp.repeat(jnp.exp(steps), dims[dim] // parts).reshape((-1,) + (1,) * (len(dims) - 1 - dim))
    return gain


def centred(key, shape, spread, reach, shards=(), dtype=jnp.bfloat16):
    array = jax.random.normal(key, shape, jnp.float32) * spread
    if len(shards) > 0:
        array = block_scale(key, shape, shards, -0.22, 0.18) * array
    return jnp.clip(array, min=-reach, max=reach).astype(dtype)


def setup_inputs(seed: int = 0) -> dict:
    arg_keys = jax.random.split(jax.random.key(seed), 6)
    adjoint = centred(arg_keys[0], (VELOCITIES, NZ, NY, NX), 1.0, 6.0, ((1, 2), (2, 2), (3, 8)), jnp.float32)
    momentum = centred(arg_keys[1], (3, NZ, NY, NX), 0.5, 4.0, ((1, 2), (2, 2), (3, 8)), jnp.float32)
    design = jnp.clip(1.0 * jax.random.uniform(arg_keys[2], (NY, NX), jnp.float32) ** block_scale(arg_keys[2], (NY, NX), ((0, 2), (1, 8)), -0.2, 0.2), 0.0, 1.0)
    solid_mask = set_ends((jax.random.randint(arg_keys[3], (NZ, NY, NX), 0, 8) < 1).astype(jnp.int32), jax.random.fold_in(arg_keys[3], 1), 0, 1)
    port_label = draw_port_label(jax.random.fold_in(arg_keys[5], 71), 0)
    return {"adjoint": adjoint, "momentum": momentum, "design": design, "solid_mask": solid_mask, "port_label": port_label}


velocities = ((0, 0, 0), (1, 0, 0), (-1, 0, 0), (0, 1, 0), (0, -1, 0), (0, 0, 1), (0, 0, -1), (1, 1, 0), (-1, -1, 0), (1, -1, 0), (-1, 1, 0), (1, 0, 1), (-1, 0, -1), (1, 0, -1), (-1, 0, 1), (0, 1, 1), (0, -1, -1), (0, 1, -1), (0, -1, 1))
lattice_weights = (1.0 / 3.0,) + (1.0 / 18.0,) * 6 + (1.0 / 36.0,) * 12
opposite = (0, 2, 1, 4, 3, 6, 5, 8, 7, 10, 9, 12, 11, 14, 13, 16, 15, 18, 17)
relax_rate = 1.25
damp_top = 0.5
cone_radius = 5.0
filter_reach = 4

def stream_pull(adjoint):
    depth_cells, band_cells, span_cells = adjoint.shape[1:]
    padded = jnp.pad(adjoint, ((0, 0), (1, 1), (1, 1), (1, 1)))
    pulled = []
    for number, vector in enumerate(velocities):
        pulled.append(padded[number, 1 + vector[2]:1 + vector[2] + depth_cells, 1 + vector[1]:1 + vector[1] + band_cells, 1 + vector[0]:1 + vector[0] + span_cells])
    return pulled

def collide(pulled, momentum, damping, solid_mask, port_label):
    zeroth = jnp.zeros_like(pulled[0])
    moment_x = jnp.zeros_like(pulled[0])
    moment_y = jnp.zeros_like(pulled[0])
    moment_z = jnp.zeros_like(pulled[0])
    for number, vector in enumerate(velocities):
        weighted = lattice_weights[number] * pulled[number]
        zeroth = zeroth + weighted
        if vector[0] != 0:
            moment_x = moment_x + vector[0] * weighted
        if vector[1] != 0:
            moment_y = moment_y + vector[1] * weighted
        if vector[2] != 0:
            moment_z = moment_z + vector[2] * weighted
    local_sens = -3.0 * (moment_x * momentum[0] + moment_y * momentum[1] + moment_z * momentum[2])
    fluid_cell = solid_mask == 0
    inlet_cell = port_label == 1
    outlet_cell = port_label == 2
    results = []
    for number, vector in enumerate(velocities):
        projected = 3.0 * (vector[0] * moment_x + vector[1] * moment_y + vector[2] * moment_z)
        relaxed = (1.0 - relax_rate) * pulled[number] + relax_rate * (zeroth + projected) - damping * projected
        updated = jnp.where(fluid_cell, relaxed, pulled[opposite[number]])
        updated = jnp.where(inlet_cell, 0.0, updated) + jnp.where(outlet_cell, float(vector[0]), 0.0)
        results.append(updated)
    kept_sens = jnp.where(fluid_cell & jnp.logical_not(inlet_cell), local_sens, 0.0)
    return (jnp.stack(results), kept_sens)

def cone_filter(column):
    band_cells, span_cells = column.shape
    padded = jnp.pad(column, filter_reach)
    ones_padded = jnp.pad(jnp.ones_like(column), filter_reach)
    numerator = jnp.zeros_like(column)
    denominator = jnp.zeros_like(column)
    for offset_y in range(-filter_reach, filter_reach + 1):
        for offset_x in range(-filter_reach, filter_reach + 1):
            weight = max(0.0, cone_radius - math.sqrt(offset_y * offset_y + offset_x * offset_x))
            if weight > 0.0:
                top = filter_reach + offset_y
                left = filter_reach + offset_x
                numerator = numerator + weight * padded[top:top + band_cells, left:left + span_cells]
                denominator = denominator + weight * ones_padded[top:top + band_cells, left:left + span_cells]
    return numerator / denominator

def reference(adjoint, momentum, design, solid_mask, port_label):
    damping = damp_top * (1.0 - design) / (1.0 + design)
    design_slope = -2.0 * damp_top / ((1.0 + design) * (1.0 + design))
    pulled = stream_pull(adjoint)
    new_adjoint, kept_sens = collide(pulled, momentum, damping, solid_mask, port_label)
    column = lax.optimization_barrier(jnp.sum(kept_sens, axis=0)) * design_slope
    return (new_adjoint, cone_filter(column))
```

```python
import functools
import math

import jax
import jax.numpy as jnp
from jax import lax
from jax.experimental import pallas as pl
from jax.experimental.pallas import tpu as pltpu
from jax.sharding import PartitionSpec as P

velocities = (
    (0, 0, 0),
    (1, 0, 0),
    (-1, 0, 0),
    (0, 1, 0),
    (0, -1, 0),
    (0, 0, 1),
    (0, 0, -1),
    (1, 1, 0),
    (-1, -1, 0),
    (1, -1, 0),
    (-1, 1, 0),
    (1, 0, 1),
    (-1, 0, -1),
    (1, 0, -1),
    (-1, 0, 1),
    (0, 1, 1),
    (0, -1, -1),
    (0, 1, -1),
    (0, -1, 1),
)
lattice_weights = (1.0 / 3.0,) + (1.0 / 18.0,) * 6 + (1.0 / 36.0,) * 12
opposite = (0, 2, 1, 4, 3, 6, 5, 8, 7, 10, 9, 12, 11, 14, 13, 16, 15, 18, 17)
relax_rate = 1.25
damp_top = 0.5
cone_radius = 5.0
filter_reach = 4
wide = filter_reach + 1
tile = 8
laterals = ((0, 0), (1, 0), (-1, 0), (0, 1), (0, -1))
lateral_weights = (1.0 / 18.0,) + (1.0 / 36.0,) * 4
kinds = len(laterals) + 3


def crossing(axis, sign):
    others = [other for other in range(3) if other != axis]
    return [
        next(
            number
            for number, vector in enumerate(velocities)
            if vector[axis] == sign and (vector[others[0]], vector[others[1]]) == lateral
        )
        for lateral in laterals
    ]


def cone(offset_y, offset_x):
    return max(0.0, cone_radius - math.sqrt(offset_y * offset_y + offset_x * offset_x))


def pairings(axis):
    return range(min(lax.axis_size(axis) - 1, 2))


def swap(array, axis, pairing):
    pairs = []
    for low in range(pairing, lax.axis_size(axis) - 1, 2):
        pairs += [(low, low + 1), (low + 1, low)]
    return lax.ppermute(array, axis, pairs)


def partner_after(axis, pairing):
    return lax.rem(lax.axis_index(axis) + pairing, 2) == 0


def pick(flag, yes, no):
    return lax.select(flag, yes, no)


def turn(array, shift, axis):
    shift = shift % array.shape[axis]
    return array if shift == 0 else pltpu.roll(array, shift, axis)


def lanes_of(shape):
    return lax.broadcasted_iota(jnp.int32, shape, len(shape) - 1)


def rows_of(shape):
    return lax.broadcasted_iota(jnp.int32, shape, len(shape) - 2)


def halves(axis, arrays):
    before, after = 0.0, 0.0
    for pairing, array in enumerate(arrays):
        flag = partner_after(axis, pairing)
        none = jnp.zeros_like(array)
        before = before + pick(flag, none, array)
        after = after + pick(flag, array, none)
    return (before, after)


def depth_plane(adjoint, halo, number, level):
    levels = adjoint.shape[1]
    if 0 <= level < levels:
        return adjoint[number, level]
    sign = 1 if level == levels else -1
    side = halo[1] if sign > 0 else halo[0]
    return side[crossing(2, sign).index(number)]


def gain_of(momentum, scale, solid, port, level):
    kept = (solid[level] == 0) & (port[level] != 1)
    factor = jnp.where(kept, scale, 0.0)
    return [factor * momentum[part, level] for part in range(3)]


def along_x(plane, step):
    lane = lanes_of(plane.shape)
    edge = plane.shape[-1] - 1 if step > 0 else 0
    return jnp.where(lane == edge, 0.0, turn(plane, -step, 1))


def along_y(plane, step):
    row = rows_of(plane.shape)
    edge = plane.shape[-2] - 1 if step > 0 else 0
    return jnp.where(row == edge, 0.0, turn(plane, -step, 0))


def own_moment(take):
    heavy, light = (1.0 / 18.0, 1.0 / 36.0)
    p = {
        number: take(number, vector[2]) for number, vector in enumerate(velocities) if number != 0
    }
    for number in (7, 8, 9, 10):
        p[number] = along_y(p[number], velocities[number][1])
    right_x = along_x(heavy * p[1] + light * ((p[7] + p[9]) + (p[11] + p[13])), 1)
    left_x = along_x(heavy * p[2] + light * ((p[8] + p[10]) + (p[12] + p[14])), -1)
    right_y = along_x(light * (p[7] - p[9]), 1)
    left_y = along_x(light * (p[10] - p[8]), -1)
    right_z = along_x(light * (p[11] - p[13]), 1)
    left_z = along_x(light * (p[14] - p[12]), -1)
    lower_y = along_y(heavy * p[3] + light * (p[15] + p[17]), 1)
    upper_y = along_y(heavy * p[4] + light * (p[16] + p[18]), -1)
    lower_z = along_y(light * (p[15] - p[17]), 1)
    upper_z = along_y(light * (p[18] - p[16]), -1)
    moment_x = right_x - left_x
    moment_y = (lower_y - upper_y) + (right_y + left_y)
    moment_z = heavy * (p[5] - p[6]) + ((right_z + left_z) + (lower_z + upper_z))
    return (moment_x, moment_y, moment_z)


def pack_kernel(counts, adjoint, momentum, design, solid, port, *refs):
    x_pairs, y_pairs, z_pairs = counts
    z_got = refs[:z_pairs]
    x_out = refs[z_pairs : z_pairs + x_pairs]
    y_out = refs[z_pairs + x_pairs : z_pairs + x_pairs + y_pairs]
    own_out = refs[z_pairs + x_pairs + y_pairs]
    levels, rows, lanes = adjoint.shape[1:]
    slots = lanes // tile
    assert levels + 3 <= slots
    halo = halves("depth", [got[...] for got in z_got])
    scale = 6.0 * damp_top / ((1.0 + design[...]) * (1.0 + design[...]))
    lane = lanes_of((rows, lanes))
    for pairing in range(y_pairs):
        after = partner_after("gy", pairing)
        y_out[pairing][...] = jnp.zeros(y_out[pairing].shape, jnp.float32)
        for kind in range(len(laterals)):
            last, first = (crossing(1, -1)[kind], crossing(1, 1)[kind])
            y_out[pairing][kind * slots : kind * slots + levels, :] = pick(
                after, adjoint[last, :, rows - 1, :], adjoint[first, :, 0, :]
            )
        for kind, level in ((3, levels), (4, -1)):
            last, first = (crossing(1, -1)[kind], crossing(1, 1)[kind])
            place = kind * slots + level % slots
            y_out[pairing][place : place + 1, :] = pick(
                after,
                depth_plane(adjoint, halo, last, level)[rows - 1 : rows],
                depth_plane(adjoint, halo, first, level)[0:1],
            )
    total = jnp.zeros((rows, lanes), jnp.float32)
    first_pack = jnp.zeros((rows, lanes), jnp.float32)
    last_pack = jnp.zeros((rows, lanes), jnp.float32)
    for level in range(-1, levels + 1):
        inside = 0 <= level < levels
        first, last = ([], [])
        for kind, lateral in enumerate(laterals):
            if inside or lateral[1] == (1 if level == levels else -1):
                first.append((kind, depth_plane(adjoint, halo, crossing(0, 1)[kind], level)))
                last.append((kind, depth_plane(adjoint, halo, crossing(0, -1)[kind], level)))
        if inside:
            gain = gain_of(momentum, scale, solid, port, level)
            moment = own_moment(
                lambda number, step: depth_plane(adjoint, halo, number, level + step)
            )
            total = total + (gain[0] * moment[0] + gain[1] * moment[1] + gain[2] * moment[2])
            first += [(len(laterals) + part, gain[part]) for part in range(3)]
            last += [(len(laterals) + part, gain[part]) for part in range(3)]
            for pairing in range(y_pairs):
                after = partner_after("gy", pairing)
                for part in range(3):
                    place = (len(laterals) + part) * slots + level
                    y_out[pairing][place : place + 1, :] = pick(
                        after, gain[part][rows - 1 : rows], gain[part][0:1]
                    )
        for kind, plane in first:
            place = (level % slots) * tile + kind
            first_pack = jnp.where(lane == place, turn(plane, place, 1), first_pack)
        for kind, plane in last:
            place = (level % slots) * tile + kind
            last_pack = jnp.where(lane == place, turn(plane, place + 1, 1), last_pack)
    own_out[...] = total
    spare = (levels + 1) * tile
    chosen = (lane >= spare) & (lane < spare + filter_reach)
    first_pack = jnp.where(chosen, turn(total, spare, 1), first_pack)
    last_pack = jnp.where(chosen, turn(total, spare + filter_reach, 1), last_pack)
    first_ends = jnp.zeros((slots, lanes), jnp.float32)
    last_ends = jnp.zeros((slots, lanes), jnp.float32)
    lane = lanes_of((slots, lanes))
    for pairing in range(y_pairs):
        for kind in range(kinds):
            line = y_out[pairing][kind * slots : (kind + 1) * slots, :]
            place = (pairing * kinds + kind) * wide
            chosen = (lane >= place) & (lane < place + wide)
            first_ends = jnp.where(chosen, turn(line, place, 1), first_ends)
            last_ends = jnp.where(chosen, turn(line, place + wide, 1), last_ends)
    for pairing in range(x_pairs):
        after = partner_after("gx", pairing)
        x_out[pairing][0:rows, :] = pick(after, last_pack, first_pack)
        x_out[pairing][rows : rows + slots, :] = pick(after, last_ends, first_ends)


def cross_x(levels, faces, gains, sign):
    rows, lanes = faces.shape
    lane, row = (lanes_of(faces.shape), rows_of(faces.shape))
    gain = [turn(gains, -(len(laterals) + part), 1) for part in range(3)]
    total = jnp.zeros_like(faces)
    for kind, (step_y, step_z) in enumerate(laterals):
        source = turn(faces, -kind - tile * step_z, 1)
        pull = sign * gain[0]
        if step_y != 0:
            edge = rows - 1 if step_y > 0 else 0
            source = jnp.where(row == edge, 0.0, turn(source, -step_y, 0))
            pull = pull + step_y * gain[1]
        if step_z != 0:
            pull = pull + step_z * gain[2]
        total = total + lateral_weights[kind] * source * pull
    used = (lane % tile == 0) & (lane < tile * levels)
    return jnp.sum(jnp.where(used, total, 0.0), axis=1, keepdims=True)


def middle_kernel(counts, levels, *refs):
    x_pairs, y_pairs = counts
    x_got, refs = (refs[:x_pairs], refs[x_pairs:])
    x_sent, refs = (refs[:x_pairs], refs[x_pairs:])
    y_rows, refs = (refs[:y_pairs], refs[y_pairs:])
    own, refs = (refs[0], refs[1:])
    y_out, middle = (refs[:y_pairs], refs[y_pairs])
    rows, lanes = own.shape
    slots = lanes // tile
    lane = lanes_of((rows, lanes))
    main = own[...]
    side = jnp.zeros((rows, lanes), jnp.float32)
    spare = (levels + 1) * tile
    for pairing in range(x_pairs):
        after = partner_after("gx", pairing)
        sign = jnp.where(after, 1.0, -1.0)
        got, sent = (x_got[pairing][0:rows, :], x_sent[pairing][0:rows, :])
        there = cross_x(levels, sent, got, -sign)
        here = cross_x(levels, got, sent, sign)
        right = jnp.where(lane < filter_reach, turn(got, -spare, 1), 0.0)
        right = right + jnp.where(lane == 0, there, 0.0)
        left = jnp.where(lane >= lanes - filter_reach, turn(got, -spare - filter_reach, 1), 0.0)
        left = left + jnp.where(lane == lanes - 1, there, 0.0)
        side = side + pick(after, right, left)
        edge = jnp.where(after, lanes - 1, 0)
        main = main + jnp.where(lane == edge, here, 0.0)
    middle[0] = main
    middle[1] = side
    left_ends, right_ends = halves("gx", [got[rows : rows + slots, :] for got in x_got])
    lane = lanes_of((slots, lanes))
    size = kinds * wide
    for pairing in range(y_pairs):
        after = partner_after("gy", pairing)
        out = y_out[pairing]
        out[0 : kinds * slots, :] = y_rows[pairing][...]
        ends = jnp.zeros((slots, lanes), jnp.float32)
        if x_pairs:
            ends = jnp.where(lane < size, turn(left_ends, -pairing * size, 1), ends)
            ends = jnp.where(
                (lane >= size) & (lane < 2 * size), turn(right_ends, size - pairing * size, 1), ends
            )
        base = kinds * slots
        out[base : base + slots, :] = ends
        for number, part in enumerate((main, side)):
            place = base + slots + number * tile
            out[place : place + tile, :] = pick(after, part[rows - tile :], part[0:tile])


def spread_ends(ends, kind, lanes):
    lane = lanes_of(ends.shape)
    size = kinds * wide
    right = jnp.where(lane < wide, turn(ends, -size - kind * wide, 1), 0.0)
    return jnp.where(lane >= lanes - wide, turn(ends, -wide - kind * wide, 1), right)


def step_x(main, side, step):
    if step == 0:
        return (main, side)
    lane = lanes_of(main.shape)
    edge = lane == (main.shape[-1] - 1 if step > 0 else 0)
    main, side = (turn(main, -step, 1), turn(side, -step, 1))
    return (jnp.where(edge, side, main), jnp.where(edge, main, side))


def cross_y(faces, gains, sign):
    total_main, total_side = (0.0, 0.0)
    for kind, (lateral_x, lateral_z) in enumerate(laterals):
        main, side = step_x(*faces[kind], lateral_x)
        main, side = (turn(main, -lateral_z, 0), turn(side, -lateral_z, 0))
        pull_main, pull_side = (sign * gains[1][0], sign * gains[1][1])
        if lateral_x != 0:
            pull_main = pull_main + lateral_x * gains[0][0]
            pull_side = pull_side + lateral_x * gains[0][1]
        if lateral_z != 0:
            pull_main = pull_main + lateral_z * gains[2][0]
            pull_side = pull_side + lateral_z * gains[2][1]
        total_main = total_main + lateral_weights[kind] * main * pull_main
        total_side = total_side + lateral_weights[kind] * side * pull_side
    return (
        jnp.sum(total_main, axis=0, keepdims=True),
        jnp.sum(total_side, axis=0, keepdims=True),
    )


def face_lines(packed, slots, lanes):
    ends = packed[kinds * slots : (kinds + 1) * slots, :]
    return [
        (packed[kind * slots : (kind + 1) * slots, :], spread_ends(ends, kind, lanes))
        for kind in range(kinds)
    ]


def extend_kernel(y_pairs, *refs):
    y_got, refs = (refs[:y_pairs], refs[y_pairs:])
    y_sent, refs = (refs[:y_pairs], refs[y_pairs:])
    middle, out = refs
    rows, lanes = middle.shape[1:]
    slots = lanes // tile
    row, row_tile = (rows_of((rows, lanes)), rows_of((tile, lanes)))
    own = [middle[0], middle[1]]
    before = [jnp.zeros((tile, lanes), jnp.float32) for part in range(2)]
    after = [jnp.zeros((tile, lanes), jnp.float32) for part in range(2)]
    for pairing in range(y_pairs):
        flag = partner_after("gy", pairing)
        sign = jnp.where(flag, 1.0, -1.0)
        got = face_lines(y_got[pairing], slots, lanes)
        sent = face_lines(y_sent[pairing], slots, lanes)
        there = cross_y(sent[:5], got[5:], -sign)
        here = cross_y(got[:5], sent[5:], sign)
        edge_here = jnp.where(flag, rows - 1, 0)
        edge_there = jnp.where(flag, 0, tile - 1)
        for part in range(2):
            place = (kinds + 1) * slots + part * tile
            sums = y_got[pairing][place : place + tile, :]
            sums = sums + jnp.where(row_tile == edge_there, there[part], 0.0)
            none = jnp.zeros_like(sums)
            before[part] = before[part] + pick(flag, none, sums)
            after[part] = after[part] + pick(flag, sums, none)
            own[part] = own[part] + jnp.where(row == edge_here, here[part], 0.0)
    for part in range(2):
        out[part, 0:tile, :] = before[part]
        out[part, tile : tile + rows, :] = own[part]
        out[part, tile + rows :, :] = after[part]


def cone_sum(main, side, rows):
    lanes = main.shape[-1]
    lane = lanes_of(main.shape)
    pairs = [main]
    for offset in range(1, filter_reach + 1):
        up = jnp.where(lane < lanes - offset, turn(main, -offset, 1), turn(side, -offset, 1))
        down = jnp.where(lane >= offset, turn(main, offset, 1), turn(side, offset, 1))
        pairs.append(up + down)
    total = jnp.zeros((rows, lanes), jnp.float32)
    for offset in range(filter_reach + 1):
        weighted = jnp.zeros_like(main)
        for distance, pair in enumerate(pairs):
            weight = cone(offset, distance)
            if weight > 0.0:
                weighted = weighted + weight * pair
        for step in sorted({offset, -offset}):
            total = total + turn(weighted, -step, 0)[tile : tile + rows]
    return total


def filter_kernel(mine, other, out):
    rows, lanes = out.shape
    main, side = (mine[0] + other[0], mine[1] + other[1])
    row, lane = (rows_of(main.shape), lanes_of(main.shape))
    place = lax.axis_index("gy") * rows + row - tile
    inside = jnp.where((place >= 0) & (place < lax.axis_size("gy") * rows), 1.0, 0.0)
    left = (lax.axis_index("gx") > 0).astype(jnp.float32)
    right = (lax.axis_index("gx") < lax.axis_size("gx") - 1).astype(jnp.float32)
    beside = inside * jnp.where(lane < lanes // 2, right, left)
    out[...] = cone_sum(main, side, rows) / cone_sum(inside, beside, rows)


def collide_kernel(counts, adjoint, design, solid, port, *refs):
    x_pairs, y_pairs, z_pairs = counts
    x_got, refs = (refs[:x_pairs], refs[x_pairs:])
    y_got, refs = (refs[:y_pairs], refs[y_pairs:])
    z_got, refs = (refs[:z_pairs], refs[z_pairs:])
    out = refs[0]
    levels, rows, lanes = adjoint.shape[1:]
    slots = lanes // tile
    halo_z = halves("depth", [got[...] for got in z_got])
    halo_x = halves("gx", [got[0:rows, :] for got in x_got])
    halo_y = ([], [])
    for kind, (lateral_x, lateral_z) in enumerate(laterals):
        lines = []
        for got in y_got:
            ends = got[kinds * slots : (kinds + 1) * slots, :]
            main = got[kind * slots : (kind + 1) * slots, :]
            if lateral_x != 0:
                main = step_x(main, spread_ends(ends, kind, lanes), lateral_x)[0]
            lines.append(main)
        for part, line in zip(halo_y, halves("gy", lines)):
            part.append(line)
    damping = damp_top * (1.0 - design[...]) / (1.0 + design[...])
    rate = 3.0 * (relax_rate - damping)
    row, lane = (rows_of((rows, lanes)), lanes_of((rows, lanes)))
    for level in range(levels):
        pulled = []
        for number, (step_x_, step_y_, step_z_) in enumerate(velocities):
            source = level + step_z_
            plane = depth_plane(adjoint, halo_z, number, source)
            if step_x_ != 0:
                edge = lanes - 1 if step_x_ > 0 else 0
                plane = turn(plane, -step_x_, 1)
                if x_pairs:
                    kind = crossing(0, step_x_).index(number)
                    place = (source % slots) * tile + kind
                    column = turn(halo_x[1 if step_x_ > 0 else 0], edge - place, 1)
                    plane = jnp.where(lane == edge, column, plane)
                else:
                    plane = jnp.where(lane == edge, 0.0, plane)
            if step_y_ != 0:
                edge = rows - 1 if step_y_ > 0 else 0
                plane = turn(plane, -step_y_, 0)
                if y_pairs:
                    kind = crossing(1, step_y_).index(number)
                    line = halo_y[1 if step_y_ > 0 else 0][kind]
                    place = source % slots
                    plane = jnp.where(row == edge, line[place : place + 1], plane)
                else:
                    plane = jnp.where(row == edge, 0.0, plane)
            pulled.append(plane)
        total = {}
        for number in range(1, len(velocities), 2):
            total[number] = pulled[number] + pulled[number + 1]
        heavy = (total[1] + total[3]) + total[5]
        light = ((total[7] + total[9]) + (total[11] + total[13])) + (total[15] + total[17])
        zeroth = (
            lattice_weights[0] * pulled[0] + lattice_weights[1] * heavy + lattice_weights[7] * light
        )
        moment = []
        for axis in range(3):
            strong, weak = (0.0, 0.0)
            for number in range(1, len(velocities), 2):
                component = velocities[number][axis]
                if component != 0:
                    gap = component * (pulled[number] - pulled[number + 1])
                    if number < 7:
                        strong = strong + gap
                    else:
                        weak = weak + gap
            moment.append(lattice_weights[1] * strong + lattice_weights[7] * weak)
        fluid = solid[level] == 0
        inlet = port[level] == 1
        outflow = jnp.where(port[level] == 2, 1.0, 0.0)
        base = relax_rate * zeroth
        scaled = [rate * part for part in moment]
        updated = base + (1.0 - relax_rate) * pulled[0]
        updated = jnp.where(fluid, updated, pulled[0])
        out[0, level] = jnp.where(inlet, 0.0, updated)
        for number in range(1, len(velocities), 2):
            projected = 0.0
            for axis in range(3):
                component = velocities[number][axis]
                if component != 0:
                    projected = projected + component * scaled[axis]
            for mine, other, value in (
                (number, number + 1, base + projected),
                (number + 1, number, base - projected),
            ):
                updated = value + (1.0 - relax_rate) * pulled[mine]
                updated = jnp.where(fluid, updated, pulled[other])
                updated = jnp.where(inlet, 0.0, updated)
                if velocities[mine][0] > 0:
                    updated = updated + outflow
                if velocities[mine][0] < 0:
                    updated = updated - outflow
                out[mine, level] = updated


def local_call(body, name, out_shapes, *operands):
    spec = pl.BlockSpec(memory_space=pltpu.VMEM)
    shapes = [jax.ShapeDtypeStruct(shape, jnp.float32) for shape in out_shapes]
    return pl.pallas_call(
        body,
        out_shape=shapes,
        in_specs=[spec] * len(operands),
        out_specs=[spec] * len(shapes),
        compiler_params=pltpu.CompilerParams(vmem_limit_bytes=40 * 1024 * 1024),
        name=name,
    )(*operands)


def on_device(adjoint, momentum, design, solid_mask, port_label):
    levels, rows, lanes = adjoint.shape[1:]
    slots = lanes // tile
    x_pairs, y_pairs, z_pairs = (len(pairings(axis)) for axis in ("gx", "gy", "depth"))
    z_got = []
    for pairing in range(z_pairs):
        last = jnp.stack([adjoint[number, levels - 1] for number in crossing(2, -1)])
        first = jnp.stack([adjoint[number, 0] for number in crossing(2, 1)])
        face = jnp.where(partner_after("depth", pairing), last, first)
        z_got.append(swap(face, "depth", pairing))
    packed = local_call(
        functools.partial(pack_kernel, (x_pairs, y_pairs, z_pairs)),
        "pack_faces",
        [(rows + slots, lanes)] * x_pairs + [(kinds * slots, lanes)] * y_pairs + [(rows, lanes)],
        adjoint,
        momentum,
        design,
        solid_mask,
        port_label,
        *z_got,
    )
    x_sent, y_rows, own = (
        packed[:x_pairs],
        packed[x_pairs : x_pairs + y_pairs],
        packed[x_pairs + y_pairs],
    )
    x_got = [None] * x_pairs
    for pairing in reversed(range(x_pairs)):
        x_got[pairing] = swap(x_sent[pairing], "gx", pairing)
    merged = local_call(
        functools.partial(middle_kernel, (x_pairs, y_pairs), levels),
        "add_x_faces",
        [((kinds + 1) * slots + 2 * tile, lanes)] * y_pairs + [(2, rows, lanes)],
        *x_got,
        *x_sent,
        *y_rows,
        own,
    )
    y_sent, middle = (merged[:y_pairs], merged[y_pairs])
    y_got = [swap(y_sent[pairing], "gy", pairing) for pairing in range(y_pairs)]
    (column,) = local_call(
        functools.partial(extend_kernel, y_pairs),
        "add_y_faces",
        [(2, rows + 2 * tile, lanes)],
        *y_got,
        *y_sent,
        middle,
    )
    if z_pairs == 1:
        other = swap(column, "depth", 0)
    else:
        other = lax.psum(column, "depth") - column
    (new_adjoint,) = local_call(
        functools.partial(collide_kernel, (x_pairs, y_pairs, z_pairs)),
        "collide",
        [adjoint.shape],
        adjoint,
        design,
        solid_mask,
        port_label,
        *x_got,
        *y_got,
        *z_got,
    )
    (sensitivity,) = local_call(filter_kernel, "cone_filter", [(rows, lanes)], column, other)
    return (new_adjoint, sensitivity)


def solution(mesh):
    in_specs = (
        P(None, "depth", "gy", "gx"),
        P(None, "depth", "gy", "gx"),
        P("gy", "gx"),
        P("depth", "gy", "gx"),
        P("depth", "gy", "gx"),
    )
    out_specs = (P(None, "depth", "gy", "gx"), P("gy", "gx"))
    return jax.shard_map(
        on_device, mesh=mesh, in_specs=in_specs, out_specs=out_specs, check_vma=False
    )
```

```python
import functools
import math

import jax
import jax.numpy as jnp
from jax import lax
from jax.experimental import pallas as pl
from jax.experimental.pallas import tpu as pltpu
from jax.sharding import PartitionSpec as P

velocities = (
    (0, 0, 0),
    (1, 0, 0),
    (-1, 0, 0),
    (0, 1, 0),
    (0, -1, 0),
    (0, 0, 1),
    (0, 0, -1),
    (1, 1, 0),
    (-1, -1, 0),
    (1, -1, 0),
    (-1, 1, 0),
    (1, 0, 1),
    (-1, 0, -1),
    (1, 0, -1),
    (-1, 0, 1),
    (0, 1, 1),
    (0, -1, -1),
    (0, 1, -1),
    (0, -1, 1),
)
lattice_weights = (1.0 / 3.0,) + (1.0 / 18.0,) * 6 + (1.0 / 36.0,) * 12
opposite = (0, 2, 1, 4, 3, 6, 5, 8, 7, 10, 9, 12, 11, 14, 13, 16, 15, 18, 17)
relax_rate = 1.25
damp_top = 0.5
cone_radius = 5.0
filter_reach = 4
wide = filter_reach + 1
tile = 8
level_group = 3
laterals = ((0, 0), (1, 0), (-1, 0), (0, 1), (0, -1))
lateral_weights = (1.0 / 18.0,) + (1.0 / 36.0,) * 4
kinds = len(laterals) + 3


def crossing(axis, sign):
    others = [other for other in range(3) if other != axis]
    return [
        next(
            number
            for number, vector in enumerate(velocities)
            if vector[axis] == sign and (vector[others[0]], vector[others[1]]) == lateral
        )
        for lateral in laterals
    ]


def cone(offset_y, offset_x):
    return max(0.0, cone_radius - math.sqrt(offset_y * offset_y + offset_x * offset_x))


def pairings(axis):
    return range(min(lax.axis_size(axis) - 1, 2))


def swap(array, axis, pairing):
    pairs = []
    for low in range(pairing, lax.axis_size(axis) - 1, 2):
        pairs += [(low, low + 1), (low + 1, low)]
    return lax.ppermute(array, axis, pairs)


def partner_after(axis, pairing):
    return lax.rem(lax.axis_index(axis) + pairing, 2) == 0


def pick(flag, yes, no):
    return lax.select(flag, yes, no)


def turn(array, shift, axis):
    shift = shift % array.shape[axis]
    return array if shift == 0 else pltpu.roll(array, shift, axis)


def lanes_of(shape):
    return lax.broadcasted_iota(jnp.int32, shape, len(shape) - 1)


def rows_of(shape):
    return lax.broadcasted_iota(jnp.int32, shape, len(shape) - 2)


def halves(axis, arrays):
    before, after = 0.0, 0.0
    for pairing, array in enumerate(arrays):
        flag = partner_after(axis, pairing)
        none = jnp.zeros_like(array)
        before = before + pick(flag, none, array)
        after = after + pick(flag, array, none)
    return (before, after)


def depth_plane(adjoint, halo, number, level):
    levels = adjoint.shape[1]
    if 0 <= level < levels:
        return adjoint[number, level]
    sign = 1 if level == levels else -1
    side = halo[1] if sign > 0 else halo[0]
    return side[crossing(2, sign).index(number)]


def gain_of(momentum, scale, solid, port, level):
    kept = (solid[level] == 0) & (port[level] != 1)
    factor = jnp.where(kept, scale, 0.0)
    return [factor * momentum[part, level] for part in range(3)]


def along_x(plane, step):
    lane = lanes_of(plane.shape)
    edge = plane.shape[-1] - 1 if step > 0 else 0
    return jnp.where(lane == edge, 0.0, turn(plane, -step, 1))


def along_y(plane, step):
    row = rows_of(plane.shape)
    edge = plane.shape[-2] - 1 if step > 0 else 0
    return jnp.where(row == edge, 0.0, turn(plane, -step, 0))


def own_moment(take):
    heavy, light = (1.0 / 18.0, 1.0 / 36.0)
    p = {
        number: take(number, vector[2]) for number, vector in enumerate(velocities) if number != 0
    }
    for number in (7, 8, 9, 10):
        p[number] = along_y(p[number], velocities[number][1])
    right_x = along_x(heavy * p[1] + light * ((p[7] + p[9]) + (p[11] + p[13])), 1)
    left_x = along_x(heavy * p[2] + light * ((p[8] + p[10]) + (p[12] + p[14])), -1)
    right_y = along_x(light * (p[7] - p[9]), 1)
    left_y = along_x(light * (p[10] - p[8]), -1)
    right_z = along_x(light * (p[11] - p[13]), 1)
    left_z = along_x(light * (p[14] - p[12]), -1)
    lower_y = along_y(heavy * p[3] + light * (p[15] + p[17]), 1)
    upper_y = along_y(heavy * p[4] + light * (p[16] + p[18]), -1)
    lower_z = along_y(light * (p[15] - p[17]), 1)
    upper_z = along_y(light * (p[18] - p[16]), -1)
    moment_x = right_x - left_x
    moment_y = (lower_y - upper_y) + (right_y + left_y)
    moment_z = heavy * (p[5] - p[6]) + ((right_z + left_z) + (lower_z + upper_z))
    return (moment_x, moment_y, moment_z)


def groups_of(levels):
    return [(low, min(low + level_group, levels)) for low in range(0, levels, level_group)]


def face_kernel(z_pairs, adjoint, *refs):
    outs, sems = (refs[:z_pairs], refs[z_pairs])
    levels = adjoint.shape[1]
    copies = []
    for pairing in range(z_pairs):
        after = partner_after("depth", pairing)
        level = jnp.where(after, levels - 1, 0)
        for kind, numbers in enumerate(zip(crossing(2, -1), crossing(2, 1))):
            number = jnp.where(after, numbers[0], numbers[1])
            copies.append(
                pltpu.make_async_copy(
                    adjoint.at[number, level],
                    outs[pairing].at[kind],
                    sems.at[pairing * len(laterals) + kind],
                )
            )
    for copy in copies:
        copy.start()
    for copy in copies:
        copy.wait()


def pack_kernel(counts, adjoint_far, momentum_far, design_far, solid_far, port_far, *refs):
    x_pairs, y_pairs = counts
    adjoint, design, solid, port, refs = (*refs[:4], refs[4:])
    x_out, refs = (refs[:x_pairs], refs[x_pairs:])
    y_out, refs = (refs[:y_pairs], refs[y_pairs:])
    own_out, edge_gain, momentum, sems = refs
    levels, rows, lanes = adjoint.shape[1:]
    slots = lanes // tile
    assert levels + 3 <= slots
    pairs = [(design_far, design), (solid_far, solid), (port_far, port), (momentum_far, momentum)]
    pairs += [
        (adjoint_far.at[:, low:high], adjoint.at[:, low:high]) for low, high in groups_of(levels)
    ]
    copies = [
        pltpu.make_async_copy(far, near, sems.at[place]) for place, (far, near) in enumerate(pairs)
    ]
    for copy in copies:
        copy.start()
    for copy in copies[:4]:
        copy.wait()
    loads = dict(zip([low for low, high in groups_of(levels)], copies[4:]))
    scale = 6.0 * damp_top / ((1.0 + design[...]) * (1.0 + design[...]))
    lane = lanes_of((rows, lanes))
    for pairing in range(y_pairs):
        y_out[pairing][...] = jnp.zeros(y_out[pairing].shape, jnp.float32)
    total = jnp.zeros((rows, lanes), jnp.float32)
    first_pack = jnp.zeros((rows, lanes), jnp.float32)
    last_pack = jnp.zeros((rows, lanes), jnp.float32)
    loads.pop(0).wait()
    for level in range(levels):
        if level + 1 in loads:
            loads.pop(level + 1).wait()
        gain = gain_of(momentum, scale, solid, port, level)
        moment = own_moment(
            lambda number, step: adjoint[number, level + step]
            if 0 <= level + step < levels
            else jnp.zeros((rows, lanes), jnp.float32)
        )
        total = total + (gain[0] * moment[0] + gain[1] * moment[1] + gain[2] * moment[2])
        for side, edge in enumerate((0, levels - 1)):
            if level == edge:
                for part in range(3):
                    edge_gain[side, part] = gain[part]
        for pairing in range(y_pairs):
            after = partner_after("gy", pairing)
            for part in range(3):
                place = (len(laterals) + part) * slots + level
                y_out[pairing][place : place + 1, :] = pick(
                    after, gain[part][rows - 1 : rows], gain[part][0:1]
                )
        for kind in range(kinds):
            if kind < len(laterals):
                first = adjoint[crossing(0, 1)[kind], level]
                last = adjoint[crossing(0, -1)[kind], level]
            else:
                first = last = gain[kind - len(laterals)]
            place = level * tile + kind
            first_pack = jnp.where(lane == place, turn(first, place, 1), first_pack)
            last_pack = jnp.where(lane == place, turn(last, place + 1, 1), last_pack)
    for pairing in range(y_pairs):
        after = partner_after("gy", pairing)
        for kind in range(len(laterals)):
            last, first = (crossing(1, -1)[kind], crossing(1, 1)[kind])
            y_out[pairing][kind * slots : kind * slots + levels, :] = pick(
                after, adjoint[last, :, rows - 1, :], adjoint[first, :, 0, :]
            )
    own_out[...] = total
    for pairing in range(x_pairs):
        x_out[pairing][...] = pick(partner_after("gx", pairing), last_pack, first_pack)


def depth_kernel(counts, levels, *refs):
    x_pairs, y_pairs, z_pairs = counts
    z_got, refs = (refs[:z_pairs], refs[z_pairs:])
    x_pack, refs = (refs[:x_pairs], refs[x_pairs:])
    y_pack, refs = (refs[:y_pairs], refs[y_pairs:])
    own, edge_gain, refs = (*refs[:2], refs[2:])
    x_out, refs = (refs[:x_pairs], refs[x_pairs:])
    y_out, own_out = (refs[:y_pairs], refs[y_pairs])
    rows, lanes = own.shape
    slots = lanes // tile
    halo = halves("depth", [got[...] for got in z_got])
    lane = lanes_of((rows, lanes))
    total = own[...]
    if z_pairs:
        for side, sign in enumerate((-1, 1)):
            gain = [edge_gain[side, part] for part in range(3)]
            for kind, (step_x_, step_y_) in enumerate(laterals):
                plane = halo[side][kind]
                pull = sign * gain[2]
                if step_x_ != 0:
                    plane = along_x(plane, step_x_)
                    pull = pull + step_x_ * gain[0]
                if step_y_ != 0:
                    plane = along_y(plane, step_y_)
                    pull = pull + step_y_ * gain[1]
                total = total + lateral_weights[kind] * plane * pull
    own_out[...] = total
    beyond = ((3, levels, 1), (4, -1, 0))
    for pairing in range(y_pairs):
        after = partner_after("gy", pairing)
        y_out[pairing][...] = y_pack[pairing][...]
        if z_pairs:
            for kind, level, side in beyond:
                planes = crossing(2, 1 if side else -1)
                last, first = (
                    halo[side][planes.index(crossing(1, sign)[kind])] for sign in (-1, 1)
                )
                place = kind * slots + level % slots
                y_out[pairing][place : place + 1, :] = pick(
                    after, last[rows - 1 : rows], first[0:1]
                )
    spare = (levels + 1) * tile
    chosen = (lane >= spare) & (lane < spare + filter_reach)
    packs = []
    for edge_shift, sign, sums in ((0, 1, 0), (1, -1, filter_reach)):
        pack = jnp.where(chosen, turn(total, spare + sums, 1), 0.0)
        if z_pairs:
            for kind, level, side in beyond:
                planes = crossing(2, 1 if side else -1)
                plane = halo[side][planes.index(crossing(0, sign)[kind])]
                place = (level % slots) * tile + kind
                pack = jnp.where(lane == place, turn(plane, place + edge_shift, 1), pack)
        packs.append(pack)
    ends = [jnp.zeros((slots, lanes), jnp.float32) for side in range(2)]
    lane = lanes_of((slots, lanes))
    for pairing in range(y_pairs):
        for kind in range(kinds):
            line = y_out[pairing][kind * slots : (kind + 1) * slots, :]
            place = (pairing * kinds + kind) * wide
            chosen = (lane >= place) & (lane < place + wide)
            ends[0] = jnp.where(chosen, turn(line, place, 1), ends[0])
            ends[1] = jnp.where(chosen, turn(line, place + wide, 1), ends[1])
    for pairing in range(x_pairs):
        after = partner_after("gx", pairing)
        x_out[pairing][0:rows, :] = x_pack[pairing][...] + pick(after, packs[1], packs[0])
        x_out[pairing][rows : rows + slots, :] = pick(after, ends[1], ends[0])


def cross_x(levels, faces, gains, sign):
    rows, lanes = faces.shape
    lane, row = (lanes_of(faces.shape), rows_of(faces.shape))
    gain = [turn(gains, -(len(laterals) + part), 1) for part in range(3)]
    total = jnp.zeros_like(faces)
    for kind, (step_y, step_z) in enumerate(laterals):
        source = turn(faces, -kind - tile * step_z, 1)
        pull = sign * gain[0]
        if step_y != 0:
            edge = rows - 1 if step_y > 0 else 0
            source = jnp.where(row == edge, 0.0, turn(source, -step_y, 0))
            pull = pull + step_y * gain[1]
        if step_z != 0:
            pull = pull + step_z * gain[2]
        total = total + lateral_weights[kind] * source * pull
    used = (lane % tile == 0) & (lane < tile * levels)
    return jnp.sum(jnp.where(used, total, 0.0), axis=1, keepdims=True)


def middle_kernel(counts, levels, *refs):
    x_pairs, y_pairs = counts
    x_got, refs = (refs[:x_pairs], refs[x_pairs:])
    x_sent, refs = (refs[:x_pairs], refs[x_pairs:])
    y_rows, refs = (refs[:y_pairs], refs[y_pairs:])
    own, refs = (refs[0], refs[1:])
    y_out, middle = (refs[:y_pairs], refs[y_pairs])
    rows, lanes = own.shape
    slots = lanes // tile
    lane = lanes_of((rows, lanes))
    main = own[...]
    side = jnp.zeros((rows, lanes), jnp.float32)
    spare = (levels + 1) * tile
    for pairing in range(x_pairs):
        after = partner_after("gx", pairing)
        sign = jnp.where(after, 1.0, -1.0)
        got, sent = (x_got[pairing][0:rows, :], x_sent[pairing][0:rows, :])
        there = cross_x(levels, sent, got, -sign)
        here = cross_x(levels, got, sent, sign)
        right = jnp.where(lane < filter_reach, turn(got, -spare, 1), 0.0)
        right = right + jnp.where(lane == 0, there, 0.0)
        left = jnp.where(lane >= lanes - filter_reach, turn(got, -spare - filter_reach, 1), 0.0)
        left = left + jnp.where(lane == lanes - 1, there, 0.0)
        side = side + pick(after, right, left)
        edge = jnp.where(after, lanes - 1, 0)
        main = main + jnp.where(lane == edge, here, 0.0)
    middle[0] = main
    middle[1] = side
    left_ends, right_ends = halves("gx", [got[rows : rows + slots, :] for got in x_got])
    lane = lanes_of((slots, lanes))
    size = kinds * wide
    for pairing in range(y_pairs):
        after = partner_after("gy", pairing)
        out = y_out[pairing]
        out[0 : kinds * slots, :] = y_rows[pairing][...]
        ends = jnp.zeros((slots, lanes), jnp.float32)
        if x_pairs:
            ends = jnp.where(lane < size, turn(left_ends, -pairing * size, 1), ends)
            ends = jnp.where(
                (lane >= size) & (lane < 2 * size), turn(right_ends, size - pairing * size, 1), ends
            )
        base = kinds * slots
        out[base : base + slots, :] = ends
        for number, part in enumerate((main, side)):
            place = base + slots + number * tile
            out[place : place + tile, :] = pick(after, part[rows - tile :], part[0:tile])


def spread_ends(ends, kind, lanes):
    lane = lanes_of(ends.shape)
    size = kinds * wide
    right = jnp.where(lane < wide, turn(ends, -size - kind * wide, 1), 0.0)
    return jnp.where(lane >= lanes - wide, turn(ends, -wide - kind * wide, 1), right)


def step_x(main, side, step):
    if step == 0:
        return (main, side)
    lane = lanes_of(main.shape)
    edge = lane == (main.shape[-1] - 1 if step > 0 else 0)
    main, side = (turn(main, -step, 1), turn(side, -step, 1))
    return (jnp.where(edge, side, main), jnp.where(edge, main, side))


def cross_y(faces, gains, sign):
    total_main, total_side = (0.0, 0.0)
    for kind, (lateral_x, lateral_z) in enumerate(laterals):
        main, side = step_x(*faces[kind], lateral_x)
        main, side = (turn(main, -lateral_z, 0), turn(side, -lateral_z, 0))
        pull_main, pull_side = (sign * gains[1][0], sign * gains[1][1])
        if lateral_x != 0:
            pull_main = pull_main + lateral_x * gains[0][0]
            pull_side = pull_side + lateral_x * gains[0][1]
        if lateral_z != 0:
            pull_main = pull_main + lateral_z * gains[2][0]
            pull_side = pull_side + lateral_z * gains[2][1]
        total_main = total_main + lateral_weights[kind] * main * pull_main
        total_side = total_side + lateral_weights[kind] * side * pull_side
    return (
        jnp.sum(total_main, axis=0, keepdims=True),
        jnp.sum(total_side, axis=0, keepdims=True),
    )


def face_lines(packed, slots, lanes):
    ends = packed[kinds * slots : (kinds + 1) * slots, :]
    return [
        (packed[kind * slots : (kind + 1) * slots, :], spread_ends(ends, kind, lanes))
        for kind in range(kinds)
    ]


def extend_kernel(y_pairs, *refs):
    y_got, refs = (refs[:y_pairs], refs[y_pairs:])
    y_sent, refs = (refs[:y_pairs], refs[y_pairs:])
    middle, out = refs
    rows, lanes = middle.shape[1:]
    slots = lanes // tile
    row, row_tile = (rows_of((rows, lanes)), rows_of((tile, lanes)))
    own = [middle[0], middle[1]]
    before = [jnp.zeros((tile, lanes), jnp.float32) for part in range(2)]
    after = [jnp.zeros((tile, lanes), jnp.float32) for part in range(2)]
    for pairing in range(y_pairs):
        flag = partner_after("gy", pairing)
        sign = jnp.where(flag, 1.0, -1.0)
        got = face_lines(y_got[pairing], slots, lanes)
        sent = face_lines(y_sent[pairing], slots, lanes)
        there = cross_y(sent[:5], got[5:], -sign)
        here = cross_y(got[:5], sent[5:], sign)
        edge_here = jnp.where(flag, rows - 1, 0)
        edge_there = jnp.where(flag, 0, tile - 1)
        for part in range(2):
            place = (kinds + 1) * slots + part * tile
            sums = y_got[pairing][place : place + tile, :]
            sums = sums + jnp.where(row_tile == edge_there, there[part], 0.0)
            none = jnp.zeros_like(sums)
            before[part] = before[part] + pick(flag, none, sums)
            after[part] = after[part] + pick(flag, sums, none)
            own[part] = own[part] + jnp.where(row == edge_here, here[part], 0.0)
    for part in range(2):
        out[part, 0:tile, :] = before[part]
        out[part, tile : tile + rows, :] = own[part]
        out[part, tile + rows :, :] = after[part]


def cone_sum(main, side, rows):
    lanes = main.shape[-1]
    lane = lanes_of(main.shape)
    pairs = [main]
    for offset in range(1, filter_reach + 1):
        up = jnp.where(lane < lanes - offset, turn(main, -offset, 1), turn(side, -offset, 1))
        down = jnp.where(lane >= offset, turn(main, offset, 1), turn(side, offset, 1))
        pairs.append(up + down)
    total = jnp.zeros((rows, lanes), jnp.float32)
    for offset in range(filter_reach + 1):
        weighted = jnp.zeros_like(main)
        for distance, pair in enumerate(pairs):
            weight = cone(offset, distance)
            if weight > 0.0:
                weighted = weighted + weight * pair
        for step in sorted({offset, -offset}):
            total = total + turn(weighted, -step, 0)[tile : tile + rows]
    return total


def filter_kernel(mine, other, norm, out):
    rows = out.shape[0]
    out[...] = cone_sum(mine[0] + other[0], mine[1] + other[1], rows) * norm[...]


def filter_norm(rows, lanes):
    shape = (rows + 2 * tile, lanes)
    row, lane = (rows_of(shape), lanes_of(shape))
    place = lax.axis_index("gy") * rows + row - tile
    inside = jnp.where((place >= 0) & (place < lax.axis_size("gy") * rows), 1.0, 0.0)
    left = (lax.axis_index("gx") > 0).astype(jnp.float32)
    right = (lax.axis_index("gx") < lax.axis_size("gx") - 1).astype(jnp.float32)
    beside = inside * jnp.where(lane < lanes // 2, right, left)
    return 1.0 / cone_sum(inside, beside, rows)


def collide_kernel(counts, adjoint, design, solid, port, *refs):
    x_pairs, y_pairs, z_pairs = counts
    x_got, refs = (refs[:x_pairs], refs[x_pairs:])
    z_got, refs = (refs[:z_pairs], refs[z_pairs:])
    far, edge_rows, norm, out, sems = refs
    levels, rows, lanes = adjoint.shape[1:]
    slots = lanes // tile
    halo_z = halves("depth", [got[...] for got in z_got])
    halo_x = halves("gx", [got[0:rows, :] for got in x_got])
    damping = damp_top * (1.0 - design[...]) / (1.0 + design[...])
    rate = 3.0 * (relax_rate - damping)
    lane = lanes_of((rows, lanes))
    copies = []
    for level in range(levels):
        pulled = []
        for number, (step_x_, step_y_, step_z_) in enumerate(velocities):
            source = level + step_z_
            if z_pairs or 0 <= source < levels:
                plane = depth_plane(adjoint, halo_z, number, source)
            else:
                plane = jnp.zeros((rows, lanes), jnp.float32)
            if step_x_ != 0:
                edge = lanes - 1 if step_x_ > 0 else 0
                column = 0.0
                if x_pairs:
                    kind = crossing(0, step_x_).index(number)
                    place = (source % slots) * tile + kind
                    column = turn(halo_x[1 if step_x_ > 0 else 0], edge - place, 1)
                plane = jnp.where(lane == edge, column, turn(plane, -step_x_, 1))
            if step_y_ != 0:
                plane = along_y(plane, step_y_)
            pulled.append(plane)
        zeroth, moment = sums_of(pulled)
        base = relax_rate * zeroth
        scaled = [rate * part for part in moment]
        fluid, inlet = (solid[level] == 0, port[level] == 1)
        outflow = jnp.where(port[level] == 2, 1.0, 0.0)
        for number, vector in enumerate(velocities):
            updated = base + (1.0 - relax_rate) * pulled[number]
            if number > 0:
                updated = updated + along(vector, scaled)
            updated = jnp.where(fluid, updated, pulled[opposite[number]])
            updated = jnp.where(inlet, 0.0, updated)
            if vector[0] != 0:
                updated = updated + vector[0] * outflow
            out[number, level] = updated
        for place, (low, high) in enumerate(groups_of(levels)):
            if level == high - 1:
                copy = pltpu.make_async_copy(
                    out.at[:, low:high], far.at[:, low:high], sems.at[place]
                )
                copy.start()
                copies.append(copy)
    for pairing in range(y_pairs):
        after = partner_after("gy", pairing)
        for number in range(len(velocities)):
            edge_rows[pairing, number] = pick(after, out[number, :, rows - 1, :], out[number, :, 0, :])
    norm[...] = filter_norm(rows, lanes)
    for copy in copies:
        copy.wait()


def along(vector, parts):
    total = 0.0
    for component, part in zip(vector, parts):
        if component > 0:
            total = total + part
        if component < 0:
            total = total - part
    return total


def sums_of(pulled):
    heavy, light = (lattice_weights[1], lattice_weights[7])
    both, gap = ({}, {})
    for number in range(1, len(velocities), 2):
        both[number] = pulled[number] + pulled[number + 1]
        gap[number] = pulled[number] - pulled[number + 1]
    zeroth = lattice_weights[0] * pulled[0] + heavy * ((both[1] + both[3]) + both[5])
    zeroth = zeroth + light * (((both[7] + both[9]) + (both[11] + both[13])) + (both[15] + both[17]))
    moment = (
        heavy * gap[1] + light * ((gap[7] + gap[9]) + (gap[11] + gap[13])),
        heavy * gap[3] + light * ((gap[7] - gap[9]) + (gap[15] + gap[17])),
        heavy * gap[5] + light * ((gap[11] - gap[13]) + (gap[15] - gap[17])),
    )
    return (zeroth, moment)


def row_kernel(y_pairs, new, edge_rows, design, solid, port, *refs):
    y_got, (far, out, sems) = (refs[:y_pairs], refs[y_pairs:])
    levels, rows, lanes = solid.shape
    slots = lanes // tile
    copies = []
    for pairing in range(y_pairs):
        after = partner_after("gy", pairing)
        sign = jnp.where(after, 1.0, -1.0)
        got = y_got[pairing]
        ends = got[kinds * slots : (kinds + 1) * slots, :]
        extra, moment = ({}, [0.0, 0.0, 0.0])
        zeroth = 0.0
        for kind, (lateral_x, lateral_z) in enumerate(laterals):
            line = got[kind * slots : (kind + 1) * slots, :]
            if lateral_x != 0:
                line = step_x(line, spread_ends(ends, kind, lanes), lateral_x)[0]
            line = turn(line, -lateral_z, 0)[0:levels]
            none = jnp.zeros_like(line)
            extra[crossing(1, 1)[kind]] = pick(after, line, none)
            extra[crossing(1, -1)[kind]] = pick(after, none, line)
            weighted = lateral_weights[kind] * line
            zeroth = zeroth + weighted
            moment[0] = moment[0] + lateral_x * weighted
            moment[2] = moment[2] + lateral_z * weighted
        moment[1] = sign * zeroth
        edge_design = pick(after, design[rows - 1 : rows, :], design[0:1, :])
        damping = damp_top * (1.0 - edge_design) / (1.0 + edge_design)
        rate = 3.0 * (relax_rate - damping)
        fluid = pick(after, solid[:, rows - 1, :], solid[:, 0, :]) == 0
        inlet = pick(after, port[:, rows - 1, :], port[:, 0, :]) == 1
        scaled = [rate * part for part in moment]
        base = relax_rate * zeroth
        for number, vector in enumerate(velocities):
            added = base
            if number > 0:
                added = added + along(vector, scaled)
            if number in extra:
                added = added + (1.0 - relax_rate) * extra[number]
            added = jnp.where(fluid, added, extra.get(opposite[number], 0.0))
            added = jnp.where(inlet, 0.0, added)
            out[pairing, number, :, 0, :] = edge_rows[pairing, number] + added
        place = jnp.where(after, rows - 1, 0)
        copies.append(
            pltpu.make_async_copy(
                out.at[pairing, :, :, 0:1, :], far.at[:, :, pl.ds(place, 1), :], sems.at[pairing]
            )
        )
        copies[-1].start()
    for copy in copies:
        copy.wait()


def local_call(body, name, operands, out_shapes, scratch=(), far=(), far_out=(), aliases=None):
    near_spec = pl.BlockSpec(memory_space=pltpu.VMEM)
    far_spec = pl.BlockSpec(memory_space=pltpu.HBM)
    shapes = [
        shape if isinstance(shape, jax.ShapeDtypeStruct) else jax.ShapeDtypeStruct(shape, jnp.float32)
        for shape in out_shapes
    ]
    return pl.pallas_call(
        body,
        out_shape=shapes,
        in_specs=[far_spec if place in far else near_spec for place in range(len(operands))],
        out_specs=[far_spec if place in far_out else near_spec for place in range(len(shapes))],
        scratch_shapes=list(scratch),
        input_output_aliases=aliases or {},
        compiler_params=pltpu.CompilerParams(vmem_limit_bytes=16 * 1024 * 1024),
        name=name,
    )(*operands)


def on_device(adjoint, momentum, design, solid_mask, port_label):
    levels, rows, lanes = adjoint.shape[1:]
    slots = lanes // tile
    groups = len(groups_of(levels))
    x_pairs, y_pairs, z_pairs = (len(pairings(axis)) for axis in ("gx", "gy", "depth"))
    z_got = []
    if z_pairs:
        faces = local_call(
            functools.partial(face_kernel, z_pairs),
            "depth_faces",
            [adjoint],
            [(len(laterals), rows, lanes)] * z_pairs,
            scratch=[pltpu.SemaphoreType.DMA((z_pairs * len(laterals),))],
            far=(0,),
        )
        z_got = [swap(face, "depth", pairing) for pairing, face in enumerate(faces)]
    packed = local_call(
        functools.partial(pack_kernel, (x_pairs, y_pairs)),
        "pack_faces",
        [adjoint, momentum, design, solid_mask, port_label],
        [adjoint.shape, (rows, lanes)]
        + [jax.ShapeDtypeStruct(solid_mask.shape, jnp.int32)] * 2
        + [(rows, lanes)] * x_pairs
        + [(kinds * slots, lanes)] * y_pairs
        + [(rows, lanes), (2, 3, rows, lanes)],
        scratch=[
            pltpu.VMEM(momentum.shape, jnp.float32),
            pltpu.SemaphoreType.DMA((4 + groups,)),
        ],
        far=range(5),
    )
    adjoint, design, solid_mask, port_label = packed[:4]
    packed = packed[4:]
    filled = local_call(
        functools.partial(depth_kernel, (x_pairs, y_pairs, z_pairs), levels),
        "add_z_faces",
        [*z_got, *packed],
        [(rows + slots, lanes)] * x_pairs + [(kinds * slots, lanes)] * y_pairs + [(rows, lanes)],
    )
    x_sent, y_rows, own = (
        filled[:x_pairs],
        filled[x_pairs : x_pairs + y_pairs],
        filled[x_pairs + y_pairs],
    )
    x_got = [swap(x_sent[pairing], "gx", pairing) for pairing in range(x_pairs)]
    merged = local_call(
        functools.partial(middle_kernel, (x_pairs, y_pairs), levels),
        "add_x_faces",
        [*x_got, *x_sent, *y_rows, own],
        [((kinds + 1) * slots + 2 * tile, lanes)] * y_pairs + [(2, rows, lanes)],
    )
    y_sent, middle = (merged[:y_pairs], merged[y_pairs])
    y_got = [swap(y_sent[pairing], "gy", pairing) for pairing in range(y_pairs)]
    (column,) = local_call(
        functools.partial(extend_kernel, y_pairs),
        "add_y_faces",
        [*y_got, *y_sent, middle],
        [(2, rows + 2 * tile, lanes)],
    )
    if z_pairs == 1:
        other = swap(column, "depth", 0)
    else:
        other = lax.psum(column, "depth") - column
    new_adjoint, edge_rows, norm = local_call(
        functools.partial(collide_kernel, (x_pairs, y_pairs, z_pairs)),
        "collide",
        [adjoint, design, solid_mask, port_label, *x_got, *z_got],
        [adjoint.shape, (max(y_pairs, 1), len(velocities), levels, lanes), (rows, lanes)],
        scratch=[pltpu.VMEM(adjoint.shape, jnp.float32), pltpu.SemaphoreType.DMA((groups,))],
        far_out=(0,),
    )
    if y_pairs:
        (new_adjoint,) = local_call(
            functools.partial(row_kernel, y_pairs),
            "add_y_rows",
            [new_adjoint, edge_rows, design, solid_mask, port_label, *y_got],
            [adjoint.shape],
            scratch=[
                pltpu.VMEM((y_pairs, len(velocities), levels, tile, lanes), jnp.float32),
                pltpu.SemaphoreType.DMA((y_pairs,)),
            ],
            far=(0,),
            far_out=(0,),
            aliases={0: 0},
        )
    (sensitivity,) = local_call(
        filter_kernel, "cone_filter", [column, other, norm], [(rows, lanes)]
    )
    return (new_adjoint, sensitivity)


def solution(mesh):
    in_specs = (
        P(None, "depth", "gy", "gx"),
        P(None, "depth", "gy", "gx"),
        P("gy", "gx"),
        P("depth", "gy", "gx"),
        P("depth", "gy", "gx"),
    )
    out_specs = (P(None, "depth", "gy", "gx"), P("gy", "gx"))
    return jax.shard_map(
        on_device, mesh=mesh, in_specs=in_specs, out_specs=out_specs, check_vma=False
    )
```

```python
import functools
import math

import jax
import jax.numpy as jnp
from jax import lax
from jax.experimental import pallas as pl
from jax.experimental.pallas import tpu as pltpu
from jax.sharding import PartitionSpec as P

velocities = (
    (0, 0, 0),
    (1, 0, 0),
    (-1, 0, 0),
    (0, 1, 0),
    (0, -1, 0),
    (0, 0, 1),
    (0, 0, -1),
    (1, 1, 0),
    (-1, -1, 0),
    (1, -1, 0),
    (-1, 1, 0),
    (1, 0, 1),
    (-1, 0, -1),
    (1, 0, -1),
    (-1, 0, 1),
    (0, 1, 1),
    (0, -1, -1),
    (0, 1, -1),
    (0, -1, 1),
)
lattice_weights = (1.0 / 3.0,) + (1.0 / 18.0,) * 6 + (1.0 / 36.0,) * 12
opposite = (0, 2, 1, 4, 3, 6, 5, 8, 7, 10, 9, 12, 11, 14, 13, 16, 15, 18, 17)
relax_rate = 1.25
damp_top = 0.5
cone_radius = 5.0
filter_reach = 4
wide = filter_reach + 1
tile = 8
level_group = 3
laterals = ((0, 0), (1, 0), (-1, 0), (0, 1), (0, -1))
lateral_weights = (1.0 / 18.0,) + (1.0 / 36.0,) * 4
kinds = len(laterals) + 3


def crossing(axis, sign):
    others = [other for other in range(3) if other != axis]
    return [
        next(
            number
            for number, vector in enumerate(velocities)
            if vector[axis] == sign and (vector[others[0]], vector[others[1]]) == lateral
        )
        for lateral in laterals
    ]


def cone(offset_y, offset_x):
    return max(0.0, cone_radius - math.sqrt(offset_y * offset_y + offset_x * offset_x))


def pairings(axis):
    return range(min(lax.axis_size(axis) - 1, 2))


def swap(array, axis, pairing):
    size, cores = (lax.axis_size(axis), lax.axis_size("depth"))
    pairs = []
    for low in range(pairing, size - 1, 2):
        pairs += [(low, low + 1), (low + 1, low)]
    alone = [place for place in range(size) if place not in dict(pairs)]
    if axis == "depth" or cores % 2 != 0 or not alone:
        return lax.ppermute(array, axis, pairs)
    full = [(a * cores + core, b * cores + core) for a, b in pairs for core in range(cores)]
    for place in alone:
        full += [(place * cores + core, place * cores + (core ^ 1)) for core in range(cores)]
    return lax.ppermute(array, (axis, "depth"), full)


def partner_after(axis, pairing):
    return lax.rem(lax.axis_index(axis) + pairing, 2) == 0


def partners(axis, pairing):
    place, after = (lax.axis_index(axis), partner_after(axis, pairing))
    none_before, none_after = (place == 0, place == lax.axis_size(axis) - 1)
    return (
        jnp.logical_not(jnp.logical_or(after, none_before)),
        jnp.logical_and(after, jnp.logical_not(none_after)),
    )


def present(axis, pairing, array):
    before, after = partners(axis, pairing)
    return pick(jnp.logical_or(before, after), array, jnp.zeros_like(array))


def pick(flag, yes, no):
    return lax.select(flag, yes, no)


def turn(array, shift, axis):
    shift = shift % array.shape[axis]
    return array if shift == 0 else pltpu.roll(array, shift, axis)


def lanes_of(shape):
    return lax.broadcasted_iota(jnp.int32, shape, len(shape) - 1)


def rows_of(shape):
    return lax.broadcasted_iota(jnp.int32, shape, len(shape) - 2)


def halves(axis, arrays):
    before, after = 0.0, 0.0
    for pairing, array in enumerate(arrays):
        is_before, is_after = partners(axis, pairing)
        none = jnp.zeros_like(array)
        before = before + pick(is_before, array, none)
        after = after + pick(is_after, array, none)
    return (before, after)


def depth_plane(adjoint, halo, number, level):
    levels = adjoint.shape[1]
    if 0 <= level < levels:
        return adjoint[number, level]
    sign = 1 if level == levels else -1
    side = halo[1] if sign > 0 else halo[0]
    return side[crossing(2, sign).index(number)]


def gain_of(momentum, scale, solid, port, level):
    kept = (solid[level] == 0) & (port[level] != 1)
    factor = jnp.where(kept, scale, 0.0)
    return [factor * momentum[part, level] for part in range(3)]


def along_x(plane, step):
    lane = lanes_of(plane.shape)
    edge = plane.shape[-1] - 1 if step > 0 else 0
    return jnp.where(lane == edge, 0.0, turn(plane, -step, 1))


def along_y(plane, step):
    row = rows_of(plane.shape)
    edge = plane.shape[-2] - 1 if step > 0 else 0
    return jnp.where(row == edge, 0.0, turn(plane, -step, 0))


def own_moment(take):
    heavy, light = (1.0 / 18.0, 1.0 / 36.0)
    p = {
        number: take(number, vector[2]) for number, vector in enumerate(velocities) if number != 0
    }
    for number in (7, 8, 9, 10):
        p[number] = along_y(p[number], velocities[number][1])
    right_x = along_x(heavy * p[1] + light * ((p[7] + p[9]) + (p[11] + p[13])), 1)
    left_x = along_x(heavy * p[2] + light * ((p[8] + p[10]) + (p[12] + p[14])), -1)
    right_y = along_x(light * (p[7] - p[9]), 1)
    left_y = along_x(light * (p[10] - p[8]), -1)
    right_z = along_x(light * (p[11] - p[13]), 1)
    left_z = along_x(light * (p[14] - p[12]), -1)
    lower_y = along_y(heavy * p[3] + light * (p[15] + p[17]), 1)
    upper_y = along_y(heavy * p[4] + light * (p[16] + p[18]), -1)
    lower_z = along_y(light * (p[15] - p[17]), 1)
    upper_z = along_y(light * (p[18] - p[16]), -1)
    moment_x = right_x - left_x
    moment_y = (lower_y - upper_y) + (right_y + left_y)
    moment_z = heavy * (p[5] - p[6]) + ((right_z + left_z) + (lower_z + upper_z))
    return (moment_x, moment_y, moment_z)


def groups_of(levels):
    return [(low, min(low + level_group, levels)) for low in range(0, levels, level_group)]


def load_kernel(z_pairs, adjoint, momentum, design, solid, port, *refs):
    near, outs, sems = (refs[:4], refs[4 : 4 + z_pairs], refs[4 + z_pairs])
    levels = adjoint.shape[1]
    pairs = []
    for pairing in range(z_pairs):
        after = partner_after("depth", pairing)
        level = jnp.where(after, levels - 1, 0)
        for kind, numbers in enumerate(zip(crossing(2, -1), crossing(2, 1))):
            number = jnp.where(after, numbers[0], numbers[1])
            pairs.append((adjoint.at[number, level], outs[pairing].at[kind]))
    pairs += zip((momentum, design, solid, port), near)
    copies = [
        pltpu.make_async_copy(source, target, sems.at[place])
        for place, (source, target) in enumerate(pairs)
    ]
    for copy in copies:
        copy.start()
    for copy in copies:
        copy.wait()


def pack_kernel(counts, adjoint, momentum, design, solid, port, *refs):
    x_pairs, y_pairs = counts
    x_out, refs = (refs[:x_pairs], refs[x_pairs:])
    y_out, refs = (refs[:y_pairs], refs[y_pairs:])
    own_out, edge_gain = refs
    levels, rows, lanes = adjoint.shape[1:]
    slots = lanes // tile
    assert levels + 3 <= slots
    scale = 6.0 * damp_top / ((1.0 + design[...]) * (1.0 + design[...]))
    lane = lanes_of((rows, lanes))
    for pairing in range(y_pairs):
        y_out[pairing][...] = jnp.zeros(y_out[pairing].shape, jnp.float32)
    total = jnp.zeros((rows, lanes), jnp.float32)
    first_pack = jnp.zeros((rows, lanes), jnp.float32)
    last_pack = jnp.zeros((rows, lanes), jnp.float32)
    for level in range(levels):
        gain = gain_of(momentum, scale, solid, port, level)
        moment = own_moment(
            lambda number, step: adjoint[number, level + step]
            if 0 <= level + step < levels
            else jnp.zeros((rows, lanes), jnp.float32)
        )
        total = total + (gain[0] * moment[0] + gain[1] * moment[1] + gain[2] * moment[2])
        for side, edge in enumerate((0, levels - 1)):
            if level == edge:
                for part in range(3):
                    edge_gain[side, part] = gain[part]
        for pairing in range(y_pairs):
            after = partner_after("gy", pairing)
            for part in range(3):
                place = (len(laterals) + part) * slots + level
                y_out[pairing][place : place + 1, :] = pick(
                    after, gain[part][rows - 1 : rows], gain[part][0:1]
                )
        for kind in range(kinds):
            if kind < len(laterals):
                first = adjoint[crossing(0, 1)[kind], level]
                last = adjoint[crossing(0, -1)[kind], level]
            else:
                first = last = gain[kind - len(laterals)]
            place = level * tile + kind
            first_pack = jnp.where(lane == place, turn(first, place, 1), first_pack)
            last_pack = jnp.where(lane == place, turn(last, place + 1, 1), last_pack)
    for pairing in range(y_pairs):
        after = partner_after("gy", pairing)
        for kind in range(len(laterals)):
            last, first = (crossing(1, -1)[kind], crossing(1, 1)[kind])
            y_out[pairing][kind * slots : kind * slots + levels, :] = pick(
                after, adjoint[last, :, rows - 1, :], adjoint[first, :, 0, :]
            )
    own_out[...] = total
    for pairing in range(x_pairs):
        x_out[pairing][...] = pick(partner_after("gx", pairing), last_pack, first_pack)


def depth_kernel(counts, levels, *refs):
    x_pairs, y_pairs, z_pairs = counts
    z_got, refs = (refs[:z_pairs], refs[z_pairs:])
    x_pack, refs = (refs[:x_pairs], refs[x_pairs:])
    y_pack, refs = (refs[:y_pairs], refs[y_pairs:])
    own, edge_gain, refs = (*refs[:2], refs[2:])
    x_out, refs = (refs[:x_pairs], refs[x_pairs:])
    y_out, own_out = (refs[:y_pairs], refs[y_pairs])
    rows, lanes = own.shape
    slots = lanes // tile
    halo = halves("depth", [got[...] for got in z_got])
    lane = lanes_of((rows, lanes))
    total = own[...]
    if z_pairs:
        for side, sign in enumerate((-1, 1)):
            gain = [edge_gain[side, part] for part in range(3)]
            for kind, (step_x_, step_y_) in enumerate(laterals):
                plane = halo[side][kind]
                pull = sign * gain[2]
                if step_x_ != 0:
                    plane = along_x(plane, step_x_)
                    pull = pull + step_x_ * gain[0]
                if step_y_ != 0:
                    plane = along_y(plane, step_y_)
                    pull = pull + step_y_ * gain[1]
                total = total + lateral_weights[kind] * plane * pull
    own_out[...] = total
    beyond = ((3, levels, 1), (4, -1, 0))
    for pairing in range(y_pairs):
        after = partner_after("gy", pairing)
        y_out[pairing][...] = y_pack[pairing][...]
        if z_pairs:
            for kind, level, side in beyond:
                planes = crossing(2, 1 if side else -1)
                last, first = (
                    halo[side][planes.index(crossing(1, sign)[kind])] for sign in (-1, 1)
                )
                place = kind * slots + level % slots
                y_out[pairing][place : place + 1, :] = pick(
                    after, last[rows - 1 : rows], first[0:1]
                )
    spare = (levels + 1) * tile
    chosen = (lane >= spare) & (lane < spare + filter_reach)
    packs = []
    for edge_shift, sign, sums in ((0, 1, 0), (1, -1, filter_reach)):
        pack = jnp.where(chosen, turn(total, spare + sums, 1), 0.0)
        if z_pairs:
            for kind, level, side in beyond:
                planes = crossing(2, 1 if side else -1)
                plane = halo[side][planes.index(crossing(0, sign)[kind])]
                place = (level % slots) * tile + kind
                pack = jnp.where(lane == place, turn(plane, place + edge_shift, 1), pack)
        packs.append(pack)
    ends = [jnp.zeros((slots, lanes), jnp.float32) for side in range(2)]
    lane = lanes_of((slots, lanes))
    for pairing in range(y_pairs):
        for kind in range(kinds):
            line = y_out[pairing][kind * slots : (kind + 1) * slots, :]
            place = (pairing * kinds + kind) * wide
            chosen = (lane >= place) & (lane < place + wide)
            ends[0] = jnp.where(chosen, turn(line, place, 1), ends[0])
            ends[1] = jnp.where(chosen, turn(line, place + wide, 1), ends[1])
    for pairing in range(x_pairs):
        after = partner_after("gx", pairing)
        x_out[pairing][0:rows, :] = x_pack[pairing][...] + pick(after, packs[1], packs[0])
        x_out[pairing][rows : rows + slots, :] = pick(after, ends[1], ends[0])


def cross_x(levels, faces, gains, sign):
    rows, lanes = faces.shape
    lane, row = (lanes_of(faces.shape), rows_of(faces.shape))
    gain = [turn(gains, -(len(laterals) + part), 1) for part in range(3)]
    total = jnp.zeros_like(faces)
    for kind, (step_y, step_z) in enumerate(laterals):
        source = turn(faces, -kind - tile * step_z, 1)
        pull = sign * gain[0]
        if step_y != 0:
            edge = rows - 1 if step_y > 0 else 0
            source = jnp.where(row == edge, 0.0, turn(source, -step_y, 0))
            pull = pull + step_y * gain[1]
        if step_z != 0:
            pull = pull + step_z * gain[2]
        total = total + lateral_weights[kind] * source * pull
    used = (lane % tile == 0) & (lane < tile * levels)
    return jnp.sum(jnp.where(used, total, 0.0), axis=1, keepdims=True)


def middle_kernel(counts, levels, *refs):
    x_pairs, y_pairs = counts
    x_got, refs = (refs[:x_pairs][::-1], refs[x_pairs:])
    x_sent, refs = (refs[:x_pairs], refs[x_pairs:])
    own, refs = (refs[0], refs[1:])
    y_out, middle = (refs[:y_pairs], refs[y_pairs])
    rows, lanes = own.shape
    slots = lanes // tile
    lane = lanes_of((rows, lanes))
    main = own[...]
    side = jnp.zeros((rows, lanes), jnp.float32)
    spare = (levels + 1) * tile
    for pairing in range(x_pairs):
        after = partner_after("gx", pairing)
        sign = jnp.where(after, 1.0, -1.0)
        got = present("gx", pairing, x_got[pairing][0:rows, :])
        sent = x_sent[pairing][0:rows, :]
        there = cross_x(levels, sent, got, -sign)
        here = cross_x(levels, got, sent, sign)
        right = jnp.where(lane < filter_reach, turn(got, -spare, 1), 0.0)
        right = right + jnp.where(lane == 0, there, 0.0)
        left = jnp.where(lane >= lanes - filter_reach, turn(got, -spare - filter_reach, 1), 0.0)
        left = left + jnp.where(lane == lanes - 1, there, 0.0)
        side = side + pick(after, right, left)
        edge = jnp.where(after, lanes - 1, 0)
        main = main + jnp.where(lane == edge, here, 0.0)
    middle[0] = main
    middle[1] = side
    left_ends, right_ends = halves("gx", [got[rows : rows + slots, :] for got in x_got])
    lane = lanes_of((slots, lanes))
    size = kinds * wide
    for pairing in range(y_pairs):
        after = partner_after("gy", pairing)
        out = y_out[pairing]
        ends = jnp.zeros((slots, lanes), jnp.float32)
        if x_pairs:
            ends = jnp.where(lane < size, turn(left_ends, -pairing * size, 1), ends)
            ends = jnp.where(
                (lane >= size) & (lane < 2 * size), turn(right_ends, size - pairing * size, 1), ends
            )
        out[0:slots, :] = ends
        for number, part in enumerate((main, side)):
            place = slots + number * tile
            out[place : place + tile, :] = pick(after, part[rows - tile :], part[0:tile])


def spread_ends(ends, kind, lanes):
    lane = lanes_of(ends.shape)
    size = kinds * wide
    right = jnp.where(lane < wide, turn(ends, -size - kind * wide, 1), 0.0)
    return jnp.where(lane >= lanes - wide, turn(ends, -wide - kind * wide, 1), right)


def step_x(main, side, step):
    if step == 0:
        return (main, side)
    lane = lanes_of(main.shape)
    edge = lane == (main.shape[-1] - 1 if step > 0 else 0)
    main, side = (turn(main, -step, 1), turn(side, -step, 1))
    return (jnp.where(edge, side, main), jnp.where(edge, main, side))


def cross_y(faces, gains, sign):
    total_main, total_side = (0.0, 0.0)
    for kind, (lateral_x, lateral_z) in enumerate(laterals):
        main, side = step_x(*faces[kind], lateral_x)
        main, side = (turn(main, -lateral_z, 0), turn(side, -lateral_z, 0))
        pull_main, pull_side = (sign * gains[1][0], sign * gains[1][1])
        if lateral_x != 0:
            pull_main = pull_main + lateral_x * gains[0][0]
            pull_side = pull_side + lateral_x * gains[0][1]
        if lateral_z != 0:
            pull_main = pull_main + lateral_z * gains[2][0]
            pull_side = pull_side + lateral_z * gains[2][1]
        total_main = total_main + lateral_weights[kind] * main * pull_main
        total_side = total_side + lateral_weights[kind] * side * pull_side
    return (
        jnp.sum(total_main, axis=0, keepdims=True),
        jnp.sum(total_side, axis=0, keepdims=True),
    )


def face_lines(lines, ends, slots, lanes):
    return [
        (lines[kind * slots : (kind + 1) * slots], spread_ends(ends[0:slots], kind, lanes))
        for kind in range(kinds)
    ]


def extend_kernel(y_pairs, *refs):
    y_got, refs = (refs[:y_pairs], refs[y_pairs:])
    y_sent, refs = (refs[:y_pairs], refs[y_pairs:])
    ends_got, refs = (refs[:y_pairs], refs[y_pairs:])
    ends_sent, refs = (refs[:y_pairs], refs[y_pairs:])
    middle, norm, out = refs
    rows, lanes = middle.shape[1:]
    slots = lanes // tile
    row, row_tile = (rows_of((rows, lanes)), rows_of((tile, lanes)))
    own = [middle[0], middle[1]]
    before = [jnp.zeros((tile, lanes), jnp.float32) for part in range(2)]
    after = [jnp.zeros((tile, lanes), jnp.float32) for part in range(2)]
    for pairing in range(y_pairs):
        flag = partner_after("gy", pairing)
        sign = jnp.where(flag, 1.0, -1.0)
        got_lines = present("gy", pairing, y_got[pairing][...])
        got_ends = present("gy", pairing, ends_got[pairing][...])
        got = face_lines(got_lines, got_ends, slots, lanes)
        sent = face_lines(y_sent[pairing][...], ends_sent[pairing][...], slots, lanes)
        there = cross_y(sent[:5], got[5:], -sign)
        here = cross_y(got[:5], sent[5:], sign)
        edge_here = jnp.where(flag, rows - 1, 0)
        edge_there = jnp.where(flag, 0, tile - 1)
        for part in range(2):
            place = slots + part * tile
            sums = got_ends[place : place + tile]
            sums = sums + jnp.where(row_tile == edge_there, there[part], 0.0)
            none = jnp.zeros_like(sums)
            before[part] = before[part] + pick(flag, none, sums)
            after[part] = after[part] + pick(flag, sums, none)
            own[part] = own[part] + jnp.where(row == edge_here, here[part], 0.0)
    for part in range(2):
        out[part, 0:tile, :] = before[part]
        out[part, tile : tile + rows, :] = own[part]
        out[part, tile + rows :, :] = after[part]


def cone_sum(main, side, rows):
    lanes = main.shape[-1]
    lane = lanes_of(main.shape)
    pairs = [main]
    for offset in range(1, filter_reach + 1):
        up = jnp.where(lane < lanes - offset, turn(main, -offset, 1), turn(side, -offset, 1))
        down = jnp.where(lane >= offset, turn(main, offset, 1), turn(side, offset, 1))
        pairs.append(up + down)
    total = jnp.zeros((rows, lanes), jnp.float32)
    for offset in range(filter_reach + 1):
        weighted = jnp.zeros_like(main)
        for distance, pair in enumerate(pairs):
            weight = cone(offset, distance)
            if weight > 0.0:
                weighted = weighted + weight * pair
        for step in sorted({offset, -offset}):
            total = total + turn(weighted, -step, 0)[tile : tile + rows]
    return total


def filter_kernel(mine, other, norm, out):
    rows = out.shape[0]
    out[...] = cone_sum(mine[0] + other[0], mine[1] + other[1], rows) * norm[...]


def filter_norm(rows, lanes):
    shape = (rows + 2 * tile, lanes)
    row, lane = (rows_of(shape), lanes_of(shape))
    place = lax.axis_index("gy") * rows + row - tile
    inside = jnp.where((place >= 0) & (place < lax.axis_size("gy") * rows), 1.0, 0.0)
    left = (lax.axis_index("gx") > 0).astype(jnp.float32)
    right = (lax.axis_index("gx") < lax.axis_size("gx") - 1).astype(jnp.float32)
    beside = inside * jnp.where(lane < lanes // 2, right, left)
    return 1.0 / cone_sum(inside, beside, rows)


def collide_kernel(counts, adjoint, design, solid, port, *refs):
    x_pairs, y_pairs, z_pairs = counts
    x_got, refs = (refs[:x_pairs][::-1], refs[x_pairs:])
    z_got, refs = (refs[:z_pairs], refs[z_pairs:])
    far, edge_rows, norm, out, sems = refs
    levels, rows, lanes = adjoint.shape[1:]
    slots = lanes // tile
    halo_z = halves("depth", [got[...] for got in z_got])
    halo_x = halves("gx", [got[0:rows, :] for got in x_got])
    damping = damp_top * (1.0 - design[...]) / (1.0 + design[...])
    rate = 3.0 * (relax_rate - damping)
    lane = lanes_of((rows, lanes))
    copies = []
    for level in range(levels):
        pulled = []
        for number, (step_x_, step_y_, step_z_) in enumerate(velocities):
            source = level + step_z_
            if z_pairs or 0 <= source < levels:
                plane = depth_plane(adjoint, halo_z, number, source)
            else:
                plane = jnp.zeros((rows, lanes), jnp.float32)
            if step_x_ != 0:
                edge = lanes - 1 if step_x_ > 0 else 0
                column = 0.0
                if x_pairs:
                    kind = crossing(0, step_x_).index(number)
                    place = (source % slots) * tile + kind
                    column = turn(halo_x[1 if step_x_ > 0 else 0], edge - place, 1)
                plane = jnp.where(lane == edge, column, turn(plane, -step_x_, 1))
            if step_y_ != 0:
                plane = along_y(plane, step_y_)
            pulled.append(plane)
        zeroth, moment = sums_of(pulled)
        base = relax_rate * zeroth
        scaled = [rate * part for part in moment]
        fluid, inlet = (solid[level] == 0, port[level] == 1)
        outflow = jnp.where(port[level] == 2, 1.0, 0.0)
        for number, vector in enumerate(velocities):
            updated = base + (1.0 - relax_rate) * pulled[number]
            if number > 0:
                updated = updated + along(vector, scaled)
            updated = jnp.where(fluid, updated, pulled[opposite[number]])
            updated = jnp.where(inlet, 0.0, updated)
            if vector[0] != 0:
                updated = updated + vector[0] * outflow
            out[number, level] = updated
        for place, (low, high) in enumerate(groups_of(levels)):
            if level == high - 1:
                copy = pltpu.make_async_copy(
                    out.at[:, low:high], far.at[:, low:high], sems.at[place]
                )
                copy.start()
                copies.append(copy)
    for pairing in range(y_pairs):
        after = partner_after("gy", pairing)
        for number in range(len(velocities)):
            edge_rows[pairing, number] = pick(after, out[number, :, rows - 1, :], out[number, :, 0, :])
    norm[...] = filter_norm(rows, lanes)
    for copy in copies:
        copy.wait()


def along(vector, parts):
    total = 0.0
    for component, part in zip(vector, parts):
        if component > 0:
            total = total + part
        if component < 0:
            total = total - part
    return total


def sums_of(pulled):
    heavy, light = (lattice_weights[1], lattice_weights[7])
    both, gap = ({}, {})
    for number in range(1, len(velocities), 2):
        both[number] = pulled[number] + pulled[number + 1]
        gap[number] = pulled[number] - pulled[number + 1]
    zeroth = lattice_weights[0] * pulled[0] + heavy * ((both[1] + both[3]) + both[5])
    zeroth = zeroth + light * (((both[7] + both[9]) + (both[11] + both[13])) + (both[15] + both[17]))
    moment = (
        heavy * gap[1] + light * ((gap[7] + gap[9]) + (gap[11] + gap[13])),
        heavy * gap[3] + light * ((gap[7] - gap[9]) + (gap[15] + gap[17])),
        heavy * gap[5] + light * ((gap[11] - gap[13]) + (gap[15] - gap[17])),
    )
    return (zeroth, moment)


def row_kernel(y_pairs, new, edge_rows, design, solid, port, *refs):
    y_got, refs = (refs[:y_pairs], refs[y_pairs:])
    ends_got, (far, out, sems) = (refs[:y_pairs], refs[y_pairs:])
    levels, rows, lanes = solid.shape
    slots = lanes // tile
    copies = []
    for pairing in range(y_pairs):
        after = partner_after("gy", pairing)
        sign = jnp.where(after, 1.0, -1.0)
        got = present("gy", pairing, y_got[pairing][...])
        ends = present("gy", pairing, ends_got[pairing][0:slots, :])
        extra, moment = ({}, [0.0, 0.0, 0.0])
        zeroth = 0.0
        for kind, (lateral_x, lateral_z) in enumerate(laterals):
            line = got[kind * slots : (kind + 1) * slots]
            if lateral_x != 0:
                line = step_x(line, spread_ends(ends, kind, lanes), lateral_x)[0]
            line = turn(line, -lateral_z, 0)[0:levels]
            none = jnp.zeros_like(line)
            extra[crossing(1, 1)[kind]] = pick(after, line, none)
            extra[crossing(1, -1)[kind]] = pick(after, none, line)
            weighted = lateral_weights[kind] * line
            zeroth = zeroth + weighted
            moment[0] = moment[0] + lateral_x * weighted
            moment[2] = moment[2] + lateral_z * weighted
        moment[1] = sign * zeroth
        edge_design = pick(after, design[rows - 1 : rows, :], design[0:1, :])
        damping = damp_top * (1.0 - edge_design) / (1.0 + edge_design)
        rate = 3.0 * (relax_rate - damping)
        fluid = pick(after, solid[:, rows - 1, :], solid[:, 0, :]) == 0
        inlet = pick(after, port[:, rows - 1, :], port[:, 0, :]) == 1
        scaled = [rate * part for part in moment]
        base = relax_rate * zeroth
        for number, vector in enumerate(velocities):
            added = base
            if number > 0:
                added = added + along(vector, scaled)
            if number in extra:
                added = added + (1.0 - relax_rate) * extra[number]
            added = jnp.where(fluid, added, extra.get(opposite[number], 0.0))
            added = jnp.where(inlet, 0.0, added)
            out[pairing, number, :, 0, :] = edge_rows[pairing, number] + added
        place = jnp.where(after, rows - 1, 0)
        copies.append(
            pltpu.make_async_copy(
                out.at[pairing, :, :, 0:1, :], far.at[:, :, pl.ds(place, 1), :], sems.at[pairing]
            )
        )
        copies[-1].start()
    for copy in copies:
        copy.wait()


def local_call(body, name, operands, out_shapes, scratch=(), far=(), far_out=(), aliases=None, room=16):
    near_spec = pl.BlockSpec(memory_space=pltpu.VMEM)
    far_spec = pl.BlockSpec(memory_space=pltpu.HBM)
    shapes = [
        jax.ShapeDtypeStruct(shape, jnp.float32) if isinstance(shape, tuple) else shape
        for shape in out_shapes
    ]
    return pl.pallas_call(
        body,
        out_shape=shapes,
        in_specs=[far_spec if place in far else near_spec for place in range(len(operands))],
        out_specs=[far_spec if place in far_out else near_spec for place in range(len(shapes))],
        scratch_shapes=list(scratch),
        input_output_aliases=aliases or {},
        compiler_params=pltpu.CompilerParams(vmem_limit_bytes=room * 1024 * 1024),
        name=name,
    )(*operands)


def on_device(adjoint, momentum, design, solid_mask, port_label):
    levels, rows, lanes = adjoint.shape[1:]
    slots = lanes // tile
    groups = len(groups_of(levels))
    x_pairs, y_pairs, z_pairs = (len(pairings(axis)) for axis in ("gx", "gy", "depth"))
    loaded = local_call(
        functools.partial(load_kernel, z_pairs),
        "load",
        [
            pltpu.with_memory_space_constraint(array, pltpu.HBM)
            for array in (adjoint, momentum, design, solid_mask, port_label)
        ],
        [
            pltpu.VMEM(momentum.shape, jnp.float32),
            pltpu.VMEM(design.shape, jnp.float32),
            pltpu.VMEM(solid_mask.shape, jnp.int32),
            pltpu.VMEM(port_label.shape, jnp.int32),
        ]
        + [pltpu.VMEM((len(laterals), rows, lanes), jnp.float32)] * z_pairs,
        scratch=[pltpu.SemaphoreType.DMA((z_pairs * len(laterals) + 4,))],
        far=range(5),
    )
    momentum, design, solid_mask, port_label = loaded[:4]
    z_got = [swap(face, "depth", pairing) for pairing, face in enumerate(loaded[4:])]
    packed = local_call(
        functools.partial(pack_kernel, (x_pairs, y_pairs)),
        "pack_faces",
        [adjoint, momentum, design, solid_mask, port_label],
        [(rows, lanes)] * x_pairs
        + [(kinds * slots, lanes)] * y_pairs
        + [(rows, lanes), (2, 3, rows, lanes)],
    )
    filled = local_call(
        functools.partial(depth_kernel, (x_pairs, y_pairs, z_pairs), levels),
        "add_z_faces",
        [*z_got, *packed],
        [(rows + slots, lanes)] * x_pairs + [(kinds * slots, lanes)] * y_pairs + [(rows, lanes)],
    )
    x_sent, y_sent, own = (
        filled[:x_pairs],
        filled[x_pairs : x_pairs + y_pairs],
        filled[x_pairs + y_pairs],
    )
    y_got = [swap(y_sent[pairing], "gy", pairing) for pairing in range(y_pairs)]
    x_got = [None] * x_pairs
    for pairing in reversed(range(x_pairs)):
        x_got[pairing] = swap(x_sent[pairing], "gx", pairing)
    merged = local_call(
        functools.partial(middle_kernel, (x_pairs, y_pairs), levels),
        "add_x_faces",
        [*x_got[::-1], *x_sent, own],
        [(slots + 2 * tile, lanes)] * y_pairs + [(2, rows, lanes)],
    )
    ends_sent, middle = (merged[:y_pairs], merged[y_pairs])
    ends_got = [swap(ends_sent[pairing], "gy", pairing) for pairing in range(y_pairs)]
    new_adjoint, edge_rows, norm = local_call(
        functools.partial(collide_kernel, (x_pairs, y_pairs, z_pairs)),
        "collide",
        [adjoint, design, solid_mask, port_label, *x_got[::-1], *z_got],
        [adjoint.shape, (max(y_pairs, 1), len(velocities), levels, lanes), (rows, lanes)],
        scratch=[pltpu.VMEM(adjoint.shape, jnp.float32), pltpu.SemaphoreType.DMA((groups,))],
        far_out=(0,),
    )
    (column,) = local_call(
        functools.partial(extend_kernel, y_pairs),
        "add_y_faces",
        [*y_got, *y_sent, *ends_got, *ends_sent, middle, norm],
        [(2, rows + 2 * tile, lanes)],
    )
    if z_pairs == 1:
        other = swap(column, "depth", 0)
    else:
        other = lax.psum(column, "depth") - column
    if y_pairs:
        (new_adjoint,) = local_call(
            functools.partial(row_kernel, y_pairs),
            "add_y_rows",
            [new_adjoint, edge_rows, design, solid_mask, port_label, *y_got, *ends_got],
            [adjoint.shape],
            scratch=[
                pltpu.VMEM((y_pairs, len(velocities), levels, tile, lanes), jnp.float32),
                pltpu.SemaphoreType.DMA((y_pairs,)),
            ],
            far=(0,),
            far_out=(0,),
            aliases={0: 0},
        )
    (sensitivity,) = local_call(
        filter_kernel, "cone_filter", [column, other, norm], [(rows, lanes)]
    )
    return (new_adjoint, sensitivity)


def solution(mesh):
    in_specs = (
        P(None, "depth", "gy", "gx"),
        P(None, "depth", "gy", "gx"),
        P("gy", "gx"),
        P("depth", "gy", "gx"),
        P("depth", "gy", "gx"),
    )
    out_specs = (P(None, "depth", "gy", "gx"), P("gy", "gx"))
    return jax.shard_map(
        on_device, mesh=mesh, in_specs=in_specs, out_specs=out_specs, check_vma=False
    )
```

```python
import functools
import math

import jax
import jax.numpy as jnp
from jax import lax
from jax.experimental import pallas as pl
from jax.experimental.pallas import tpu as pltpu
from jax.sharding import PartitionSpec as P

velocities = (
    (0, 0, 0),
    (1, 0, 0),
    (-1, 0, 0),
    (0, 1, 0),
    (0, -1, 0),
    (0, 0, 1),
    (0, 0, -1),
    (1, 1, 0),
    (-1, -1, 0),
    (1, -1, 0),
    (-1, 1, 0),
    (1, 0, 1),
    (-1, 0, -1),
    (1, 0, -1),
    (-1, 0, 1),
    (0, 1, 1),
    (0, -1, -1),
    (0, 1, -1),
    (0, -1, 1),
)
lattice_weights = (1.0 / 3.0,) + (1.0 / 18.0,) * 6 + (1.0 / 36.0,) * 12
opposite = (0, 2, 1, 4, 3, 6, 5, 8, 7, 10, 9, 12, 11, 14, 13, 16, 15, 18, 17)
relax_rate = 1.25
damp_top = 0.5
cone_radius = 5.0
filter_reach = 4
wide = filter_reach + 1
tile = 8
level_group = 3
laterals = ((0, 0), (1, 0), (-1, 0), (0, 1), (0, -1))
lateral_weights = (1.0 / 18.0,) + (1.0 / 36.0,) * 4
kinds = len(laterals) + 3


def crossing(axis, sign):
    others = [other for other in range(3) if other != axis]
    return [
        next(
            number
            for number, vector in enumerate(velocities)
            if vector[axis] == sign and (vector[others[0]], vector[others[1]]) == lateral
        )
        for lateral in laterals
    ]


def cone(offset_y, offset_x):
    return max(0.0, cone_radius - math.sqrt(offset_y * offset_y + offset_x * offset_x))


def pairings(axis):
    return range(min(lax.axis_size(axis) - 1, 2))


def swap(array, axis, pairing):
    size, cores = (lax.axis_size(axis), lax.axis_size("depth"))
    pairs = []
    for low in range(pairing, size - 1, 2):
        pairs += [(low, low + 1), (low + 1, low)]
    alone = [place for place in range(size) if place not in dict(pairs)]
    if axis == "depth" or cores % 2 != 0 or not alone:
        return lax.ppermute(array, axis, pairs)
    full = [(a * cores + core, b * cores + core) for a, b in pairs for core in range(cores)]
    for place in alone:
        full += [(place * cores + core, place * cores + (core ^ 1)) for core in range(cores)]
    return lax.ppermute(array, (axis, "depth"), full)


def partner_after(axis, pairing):
    return lax.rem(lax.axis_index(axis) + pairing, 2) == 0


def partners(axis, pairing):
    place, after = (lax.axis_index(axis), partner_after(axis, pairing))
    none_before, none_after = (place == 0, place == lax.axis_size(axis) - 1)
    return (
        jnp.logical_not(jnp.logical_or(after, none_before)),
        jnp.logical_and(after, jnp.logical_not(none_after)),
    )


def present(axis, pairing, array):
    before, after = partners(axis, pairing)
    return pick(jnp.logical_or(before, after), array, jnp.zeros_like(array))


def pick(flag, yes, no):
    return lax.select(flag, yes, no)


def turn(array, shift, axis):
    shift = shift % array.shape[axis]
    return array if shift == 0 else pltpu.roll(array, shift, axis)


def lanes_of(shape):
    return lax.broadcasted_iota(jnp.int32, shape, len(shape) - 1)


def rows_of(shape):
    return lax.broadcasted_iota(jnp.int32, shape, len(shape) - 2)


def halves(axis, arrays):
    before, after = 0.0, 0.0
    for pairing, array in enumerate(arrays):
        is_before, is_after = partners(axis, pairing)
        none = jnp.zeros_like(array)
        before = before + pick(is_before, array, none)
        after = after + pick(is_after, array, none)
    return (before, after)


def depth_plane(adjoint, halo, number, level):
    levels = adjoint.shape[1]
    if 0 <= level < levels:
        return adjoint[number, level]
    sign = 1 if level == levels else -1
    side = halo[1] if sign > 0 else halo[0]
    return side[crossing(2, sign).index(number)]


def gain_of(momentum, scale, solid, port, level):
    kept = (solid[level] == 0) & (port[level] != 1)
    factor = jnp.where(kept, scale, 0.0)
    return [factor * momentum[part, level] for part in range(3)]


def along_x(plane, step):
    lane = lanes_of(plane.shape)
    edge = plane.shape[-1] - 1 if step > 0 else 0
    return jnp.where(lane == edge, 0.0, turn(plane, -step, 1))


def along_y(plane, step):
    row = rows_of(plane.shape)
    edge = plane.shape[-2] - 1 if step > 0 else 0
    return jnp.where(row == edge, 0.0, turn(plane, -step, 0))


def own_moment(take):
    heavy, light = (1.0 / 18.0, 1.0 / 36.0)
    p = {
        number: take(number, vector[2]) for number, vector in enumerate(velocities) if number != 0
    }
    for number in (7, 8, 9, 10):
        p[number] = along_y(p[number], velocities[number][1])
    right_x = along_x(heavy * p[1] + light * ((p[7] + p[9]) + (p[11] + p[13])), 1)
    left_x = along_x(heavy * p[2] + light * ((p[8] + p[10]) + (p[12] + p[14])), -1)
    right_y = along_x(light * (p[7] - p[9]), 1)
    left_y = along_x(light * (p[10] - p[8]), -1)
    right_z = along_x(light * (p[11] - p[13]), 1)
    left_z = along_x(light * (p[14] - p[12]), -1)
    lower_y = along_y(heavy * p[3] + light * (p[15] + p[17]), 1)
    upper_y = along_y(heavy * p[4] + light * (p[16] + p[18]), -1)
    lower_z = along_y(light * (p[15] - p[17]), 1)
    upper_z = along_y(light * (p[18] - p[16]), -1)
    moment_x = right_x - left_x
    moment_y = (lower_y - upper_y) + (right_y + left_y)
    moment_z = heavy * (p[5] - p[6]) + ((right_z + left_z) + (lower_z + upper_z))
    return (moment_x, moment_y, moment_z)


def groups_of(levels):
    return [(low, min(low + level_group, levels)) for low in range(0, levels, level_group)]


def load_kernel(z_pairs, adjoint, momentum, design, solid, port, *refs):
    near, outs, sems = (refs[:4], refs[4 : 4 + z_pairs], refs[4 + z_pairs])
    levels = adjoint.shape[1]
    pairs = []
    for pairing in range(z_pairs):
        after = partner_after("depth", pairing)
        level = jnp.where(after, levels - 1, 0)
        for kind, numbers in enumerate(zip(crossing(2, -1), crossing(2, 1))):
            number = jnp.where(after, numbers[0], numbers[1])
            pairs.append((adjoint.at[number, level], outs[pairing].at[kind]))
    pairs += zip((momentum, design, solid, port), near)
    copies = [
        pltpu.make_async_copy(source, target, sems.at[place])
        for place, (source, target) in enumerate(pairs)
    ]
    for copy in copies:
        copy.start()
    for copy in copies:
        copy.wait()


def pack_kernel(counts, adjoint, momentum, design, solid, port, *refs):
    x_pairs, y_pairs = counts
    x_out, refs = (refs[:x_pairs], refs[x_pairs:])
    y_out, refs = (refs[:y_pairs], refs[y_pairs:])
    own_out, edge_gain = refs
    levels, rows, lanes = adjoint.shape[1:]
    slots = lanes // tile
    assert levels + 3 <= slots
    scale = 6.0 * damp_top / ((1.0 + design[...]) * (1.0 + design[...]))
    lane = lanes_of((rows, lanes))
    for pairing in range(y_pairs):
        y_out[pairing][...] = jnp.zeros(y_out[pairing].shape, jnp.float32)
    total = jnp.zeros((rows, lanes), jnp.float32)
    first_pack = jnp.zeros((rows, lanes), jnp.float32)
    last_pack = jnp.zeros((rows, lanes), jnp.float32)
    for level in range(levels):
        gain = gain_of(momentum, scale, solid, port, level)
        moment = own_moment(
            lambda number, step: adjoint[number, level + step]
            if 0 <= level + step < levels
            else jnp.zeros((rows, lanes), jnp.float32)
        )
        total = total + (gain[0] * moment[0] + gain[1] * moment[1] + gain[2] * moment[2])
        for side, edge in enumerate((0, levels - 1)):
            if level == edge:
                for part in range(3):
                    edge_gain[side, part] = gain[part]
        for pairing in range(y_pairs):
            after = partner_after("gy", pairing)
            for part in range(3):
                place = (len(laterals) + part) * slots + level
                y_out[pairing][place : place + 1, :] = pick(
                    after, gain[part][rows - 1 : rows], gain[part][0:1]
                )
        for kind in range(kinds):
            if kind < len(laterals):
                first = adjoint[crossing(0, 1)[kind], level]
                last = adjoint[crossing(0, -1)[kind], level]
            else:
                first = last = gain[kind - len(laterals)]
            place = level * tile + kind
            first_pack = jnp.where(lane == place, turn(first, place, 1), first_pack)
            last_pack = jnp.where(lane == place, turn(last, place + 1, 1), last_pack)
    for pairing in range(y_pairs):
        after = partner_after("gy", pairing)
        for kind in range(len(laterals)):
            last, first = (crossing(1, -1)[kind], crossing(1, 1)[kind])
            y_out[pairing][kind * slots : kind * slots + levels, :] = pick(
                after, adjoint[last, :, rows - 1, :], adjoint[first, :, 0, :]
            )
    own_out[...] = total
    for pairing in range(x_pairs):
        x_out[pairing][...] = pick(partner_after("gx", pairing), last_pack, first_pack)


def depth_kernel(counts, levels, *refs):
    x_pairs, y_pairs, z_pairs = counts
    z_got, refs = (refs[:z_pairs], refs[z_pairs:])
    x_pack, refs = (refs[:x_pairs], refs[x_pairs:])
    y_pack, refs = (refs[:y_pairs], refs[y_pairs:])
    own, edge_gain, refs = (*refs[:2], refs[2:])
    x_out, refs = (refs[:x_pairs], refs[x_pairs:])
    y_out, own_out = (refs[:y_pairs], refs[y_pairs])
    rows, lanes = own.shape
    slots = lanes // tile
    halo = halves("depth", [got[...] for got in z_got])
    lane = lanes_of((rows, lanes))
    total = own[...]
    if z_pairs:
        for side, sign in enumerate((-1, 1)):
            gain = [edge_gain[side, part] for part in range(3)]
            for kind, (step_x_, step_y_) in enumerate(laterals):
                plane = halo[side][kind]
                pull = sign * gain[2]
                if step_x_ != 0:
                    plane = along_x(plane, step_x_)
                    pull = pull + step_x_ * gain[0]
                if step_y_ != 0:
                    plane = along_y(plane, step_y_)
                    pull = pull + step_y_ * gain[1]
                total = total + lateral_weights[kind] * plane * pull
    own_out[...] = total
    beyond = ((3, levels, 1), (4, -1, 0))
    for pairing in range(y_pairs):
        after = partner_after("gy", pairing)
        y_out[pairing][...] = y_pack[pairing][...]
        if z_pairs:
            for kind, level, side in beyond:
                planes = crossing(2, 1 if side else -1)
                last, first = (
                    halo[side][planes.index(crossing(1, sign)[kind])] for sign in (-1, 1)
                )
                place = kind * slots + level % slots
                y_out[pairing][place : place + 1, :] = pick(
                    after, last[rows - 1 : rows], first[0:1]
                )
    spare = (levels + 1) * tile
    chosen = (lane >= spare) & (lane < spare + filter_reach)
    packs = []
    for edge_shift, sign, sums in ((0, 1, 0), (1, -1, filter_reach)):
        pack = jnp.where(chosen, turn(total, spare + sums, 1), 0.0)
        if z_pairs:
            for kind, level, side in beyond:
                planes = crossing(2, 1 if side else -1)
                plane = halo[side][planes.index(crossing(0, sign)[kind])]
                place = (level % slots) * tile + kind
                pack = jnp.where(lane == place, turn(plane, place + edge_shift, 1), pack)
        packs.append(pack)
    ends = [jnp.zeros((slots, lanes), jnp.float32) for side in range(2)]
    lane = lanes_of((slots, lanes))
    for pairing in range(y_pairs):
        for kind in range(kinds):
            line = y_out[pairing][kind * slots : (kind + 1) * slots, :]
            place = (pairing * kinds + kind) * wide
            chosen = (lane >= place) & (lane < place + wide)
            ends[0] = jnp.where(chosen, turn(line, place, 1), ends[0])
            ends[1] = jnp.where(chosen, turn(line, place + wide, 1), ends[1])
    for pairing in range(x_pairs):
        after = partner_after("gx", pairing)
        x_out[pairing][0:rows, :] = x_pack[pairing][...] + pick(after, packs[1], packs[0])
        x_out[pairing][rows : rows + slots, :] = pick(after, ends[1], ends[0])


def cross_x(levels, faces, gains, sign):
    rows, lanes = faces.shape
    lane, row = (lanes_of(faces.shape), rows_of(faces.shape))
    gain = [turn(gains, -(len(laterals) + part), 1) for part in range(3)]
    total = jnp.zeros_like(faces)
    for kind, (step_y, step_z) in enumerate(laterals):
        source = turn(faces, -kind - tile * step_z, 1)
        pull = sign * gain[0]
        if step_y != 0:
            edge = rows - 1 if step_y > 0 else 0
            source = jnp.where(row == edge, 0.0, turn(source, -step_y, 0))
            pull = pull + step_y * gain[1]
        if step_z != 0:
            pull = pull + step_z * gain[2]
        total = total + lateral_weights[kind] * source * pull
    used = (lane % tile == 0) & (lane < tile * levels)
    return jnp.sum(jnp.where(used, total, 0.0), axis=1, keepdims=True)


def middle_kernel(counts, levels, *refs):
    x_pairs, y_pairs = counts
    x_got, refs = (refs[:x_pairs][::-1], refs[x_pairs:])
    x_sent, refs = (refs[:x_pairs], refs[x_pairs:])
    own, refs = (refs[0], refs[1:])
    y_out, middle = (refs[:y_pairs], refs[y_pairs])
    rows, lanes = own.shape
    slots = lanes // tile
    lane = lanes_of((rows, lanes))
    main = own[...]
    side = jnp.zeros((rows, lanes), jnp.float32)
    spare = (levels + 1) * tile
    for pairing in range(x_pairs):
        after = partner_after("gx", pairing)
        sign = jnp.where(after, 1.0, -1.0)
        got = present("gx", pairing, x_got[pairing][0:rows, :])
        sent = x_sent[pairing][0:rows, :]
        there = cross_x(levels, sent, got, -sign)
        here = cross_x(levels, got, sent, sign)
        right = jnp.where(lane < filter_reach, turn(got, -spare, 1), 0.0)
        right = right + jnp.where(lane == 0, there, 0.0)
        left = jnp.where(lane >= lanes - filter_reach, turn(got, -spare - filter_reach, 1), 0.0)
        left = left + jnp.where(lane == lanes - 1, there, 0.0)
        side = side + pick(after, right, left)
        edge = jnp.where(after, lanes - 1, 0)
        main = main + jnp.where(lane == edge, here, 0.0)
    middle[0] = main
    middle[1] = side
    left_ends, right_ends = halves("gx", [got[rows : rows + slots, :] for got in x_got])
    lane = lanes_of((slots, lanes))
    size = kinds * wide
    for pairing in range(y_pairs):
        after = partner_after("gy", pairing)
        out = y_out[pairing]
        ends = jnp.zeros((slots, lanes), jnp.float32)
        if x_pairs:
            ends = jnp.where(lane < size, turn(left_ends, -pairing * size, 1), ends)
            ends = jnp.where(
                (lane >= size) & (lane < 2 * size), turn(right_ends, size - pairing * size, 1), ends
            )
        out[0:slots, :] = ends
        for number, part in enumerate((main, side)):
            place = slots + number * tile
            out[place : place + tile, :] = pick(after, part[rows - tile :], part[0:tile])


def spread_ends(ends, kind, lanes):
    lane = lanes_of(ends.shape)
    size = kinds * wide
    right = jnp.where(lane < wide, turn(ends, -size - kind * wide, 1), 0.0)
    return jnp.where(lane >= lanes - wide, turn(ends, -wide - kind * wide, 1), right)


def step_x(main, side, step):
    if step == 0:
        return (main, side)
    lane = lanes_of(main.shape)
    edge = lane == (main.shape[-1] - 1 if step > 0 else 0)
    main, side = (turn(main, -step, 1), turn(side, -step, 1))
    return (jnp.where(edge, side, main), jnp.where(edge, main, side))


def cross_y(faces, gains, sign):
    total_main, total_side = (0.0, 0.0)
    for kind, (lateral_x, lateral_z) in enumerate(laterals):
        main, side = step_x(*faces[kind], lateral_x)
        main, side = (turn(main, -lateral_z, 0), turn(side, -lateral_z, 0))
        pull_main, pull_side = (sign * gains[1][0], sign * gains[1][1])
        if lateral_x != 0:
            pull_main = pull_main + lateral_x * gains[0][0]
            pull_side = pull_side + lateral_x * gains[0][1]
        if lateral_z != 0:
            pull_main = pull_main + lateral_z * gains[2][0]
            pull_side = pull_side + lateral_z * gains[2][1]
        total_main = total_main + lateral_weights[kind] * main * pull_main
        total_side = total_side + lateral_weights[kind] * side * pull_side
    return (
        jnp.sum(total_main, axis=0, keepdims=True),
        jnp.sum(total_side, axis=0, keepdims=True),
    )


def face_lines(lines, ends, slots, lanes):
    return [
        (lines[kind * slots : (kind + 1) * slots], spread_ends(ends[0:slots], kind, lanes))
        for kind in range(kinds)
    ]


def extend_kernel(y_pairs, *refs):
    y_got, refs = (refs[:y_pairs], refs[y_pairs:])
    y_sent, refs = (refs[:y_pairs], refs[y_pairs:])
    ends_got, refs = (refs[:y_pairs], refs[y_pairs:])
    ends_sent, refs = (refs[:y_pairs], refs[y_pairs:])
    middle, norm, out = refs
    rows, lanes = middle.shape[1:]
    slots = lanes // tile
    row, row_tile = (rows_of((rows, lanes)), rows_of((tile, lanes)))
    own = [middle[0], middle[1]]
    before = [jnp.zeros((tile, lanes), jnp.float32) for part in range(2)]
    after = [jnp.zeros((tile, lanes), jnp.float32) for part in range(2)]
    for pairing in range(y_pairs):
        flag = partner_after("gy", pairing)
        sign = jnp.where(flag, 1.0, -1.0)
        got_lines = present("gy", pairing, y_got[pairing][...])
        got_ends = present("gy", pairing, ends_got[pairing][...])
        got = face_lines(got_lines, got_ends, slots, lanes)
        sent = face_lines(y_sent[pairing][...], ends_sent[pairing][...], slots, lanes)
        there = cross_y(sent[:5], got[5:], -sign)
        here = cross_y(got[:5], sent[5:], sign)
        edge_here = jnp.where(flag, rows - 1, 0)
        edge_there = jnp.where(flag, 0, tile - 1)
        for part in range(2):
            place = slots + part * tile
            sums = got_ends[place : place + tile]
            sums = sums + jnp.where(row_tile == edge_there, there[part], 0.0)
            none = jnp.zeros_like(sums)
            before[part] = before[part] + pick(flag, none, sums)
            after[part] = after[part] + pick(flag, sums, none)
            own[part] = own[part] + jnp.where(row == edge_here, here[part], 0.0)
    for part in range(2):
        out[part, 0:tile, :] = before[part]
        out[part, tile : tile + rows, :] = own[part]
        out[part, tile + rows :, :] = after[part]


def cone_sum(main, side, rows):
    lanes = main.shape[-1]
    lane = lanes_of(main.shape)
    pairs = [main]
    for offset in range(1, filter_reach + 1):
        up = jnp.where(lane < lanes - offset, turn(main, -offset, 1), turn(side, -offset, 1))
        down = jnp.where(lane >= offset, turn(main, offset, 1), turn(side, offset, 1))
        pairs.append(up + down)
    total = jnp.zeros((rows, lanes), jnp.float32)
    for offset in range(filter_reach + 1):
        weighted = jnp.zeros_like(main)
        for distance, pair in enumerate(pairs):
            weight = cone(offset, distance)
            if weight > 0.0:
                weighted = weighted + weight * pair
        for step in sorted({offset, -offset}):
            total = total + turn(weighted, -step, 0)[tile : tile + rows]
    return total


def filter_kernel(mine, other, norm, out):
    rows = out.shape[0]
    out[...] = cone_sum(mine[0] + other[0], mine[1] + other[1], rows) * norm[...]


def filter_norm(rows, lanes):
    shape = (rows + 2 * tile, lanes)
    row, lane = (rows_of(shape), lanes_of(shape))
    place = lax.axis_index("gy") * rows + row - tile
    inside = jnp.where((place >= 0) & (place < lax.axis_size("gy") * rows), 1.0, 0.0)
    left = (lax.axis_index("gx") > 0).astype(jnp.float32)
    right = (lax.axis_index("gx") < lax.axis_size("gx") - 1).astype(jnp.float32)
    beside = inside * jnp.where(lane < lanes // 2, right, left)
    return 1.0 / cone_sum(inside, beside, rows)


def collide_kernel(counts, adjoint, design, solid, port, *refs):
    x_pairs, y_pairs, z_pairs = counts
    x_got, refs = (refs[:x_pairs][::-1], refs[x_pairs:])
    z_got, refs = (refs[:z_pairs], refs[z_pairs:])
    far, edge_rows, norm, out, sems = refs
    levels, rows, lanes = adjoint.shape[1:]
    slots = lanes // tile
    halo_z = halves("depth", [got[...] for got in z_got])
    halo_x = halves("gx", [got[0:rows, :] for got in x_got])
    damping = damp_top * (1.0 - design[...]) / (1.0 + design[...])
    rate = 3.0 * (relax_rate - damping)
    lane = lanes_of((rows, lanes))
    copies = []
    for level in range(levels):
        pulled = []
        for number, (step_x_, step_y_, step_z_) in enumerate(velocities):
            source = level + step_z_
            if z_pairs or 0 <= source < levels:
                plane = depth_plane(adjoint, halo_z, number, source)
            else:
                plane = jnp.zeros((rows, lanes), jnp.float32)
            if step_x_ != 0:
                edge = lanes - 1 if step_x_ > 0 else 0
                column = 0.0
                if x_pairs:
                    kind = crossing(0, step_x_).index(number)
                    place = (source % slots) * tile + kind
                    column = turn(halo_x[1 if step_x_ > 0 else 0], edge - place, 1)
                plane = jnp.where(lane == edge, column, turn(plane, -step_x_, 1))
            if step_y_ != 0:
                plane = along_y(plane, step_y_)
            pulled.append(plane)
        zeroth, moment = sums_of(pulled)
        base = relax_rate * zeroth
        scaled = [rate * part for part in moment]
        fluid, inlet = (solid[level] == 0, port[level] == 1)
        outflow = jnp.where(port[level] == 2, 1.0, 0.0)
        for number, vector in enumerate(velocities):
            updated = base + (1.0 - relax_rate) * pulled[number]
            if number > 0:
                updated = updated + along(vector, scaled)
            updated = jnp.where(fluid, updated, pulled[opposite[number]])
            updated = jnp.where(inlet, 0.0, updated)
            if vector[0] != 0:
                updated = updated + vector[0] * outflow
            out[number, level] = updated
        for place, (low, high) in enumerate(groups_of(levels)):
            if level == high - 1:
                copy = pltpu.make_async_copy(
                    out.at[:, low:high], far.at[:, low:high], sems.at[place]
                )
                copy.start()
                copies.append(copy)
    for pairing in range(y_pairs):
        after = partner_after("gy", pairing)
        for number in range(len(velocities)):
            edge_rows[pairing, number] = pick(after, out[number, :, rows - 1, :], out[number, :, 0, :])
    norm[...] = filter_norm(rows, lanes)
    for copy in copies:
        copy.wait()


def along(vector, parts):
    total = 0.0
    for component, part in zip(vector, parts):
        if component > 0:
            total = total + part
        if component < 0:
            total = total - part
    return total


def sums_of(pulled):
    heavy, light = (lattice_weights[1], lattice_weights[7])
    both, gap = ({}, {})
    for number in range(1, len(velocities), 2):
        both[number] = pulled[number] + pulled[number + 1]
        gap[number] = pulled[number] - pulled[number + 1]
    zeroth = lattice_weights[0] * pulled[0] + heavy * ((both[1] + both[3]) + both[5])
    zeroth = zeroth + light * (((both[7] + both[9]) + (both[11] + both[13])) + (both[15] + both[17]))
    moment = (
        heavy * gap[1] + light * ((gap[7] + gap[9]) + (gap[11] + gap[13])),
        heavy * gap[3] + light * ((gap[7] - gap[9]) + (gap[15] + gap[17])),
        heavy * gap[5] + light * ((gap[11] - gap[13]) + (gap[15] - gap[17])),
    )
    return (zeroth, moment)


def row_kernel(y_pairs, new, edge_rows, design, solid, port, *refs):
    y_got, refs = (refs[:y_pairs], refs[y_pairs:])
    ends_got, (far, out, sems) = (refs[:y_pairs], refs[y_pairs:])
    levels, rows, lanes = solid.shape
    slots = lanes // tile
    copies = []
    for pairing in range(y_pairs):
        after = partner_after("gy", pairing)
        sign = jnp.where(after, 1.0, -1.0)
        got = present("gy", pairing, y_got[pairing][...])
        ends = present("gy", pairing, ends_got[pairing][0:slots, :])
        extra, moment = ({}, [0.0, 0.0, 0.0])
        zeroth = 0.0
        for kind, (lateral_x, lateral_z) in enumerate(laterals):
            line = got[kind * slots : (kind + 1) * slots]
            if lateral_x != 0:
                line = step_x(line, spread_ends(ends, kind, lanes), lateral_x)[0]
            line = turn(line, -lateral_z, 0)[0:levels]
            none = jnp.zeros_like(line)
            extra[crossing(1, 1)[kind]] = pick(after, line, none)
            extra[crossing(1, -1)[kind]] = pick(after, none, line)
            weighted = lateral_weights[kind] * line
            zeroth = zeroth + weighted
            moment[0] = moment[0] + lateral_x * weighted
            moment[2] = moment[2] + lateral_z * weighted
        moment[1] = sign * zeroth
        edge_design = pick(after, design[rows - 1 : rows, :], design[0:1, :])
        damping = damp_top * (1.0 - edge_design) / (1.0 + edge_design)
        rate = 3.0 * (relax_rate - damping)
        fluid = pick(after, solid[:, rows - 1, :], solid[:, 0, :]) == 0
        inlet = pick(after, port[:, rows - 1, :], port[:, 0, :]) == 1
        scaled = [rate * part for part in moment]
        base = relax_rate * zeroth
        for number, vector in enumerate(velocities):
            added = base
            if number > 0:
                added = added + along(vector, scaled)
            if number in extra:
                added = added + (1.0 - relax_rate) * extra[number]
            added = jnp.where(fluid, added, extra.get(opposite[number], 0.0))
            added = jnp.where(inlet, 0.0, added)
            out[pairing, number, :, 0, :] = edge_rows[pairing, number] + added
        place = jnp.where(after, rows - 1, 0)
        copies.append(
            pltpu.make_async_copy(
                out.at[pairing, :, :, 0:1, :], far.at[:, :, pl.ds(place, 1), :], sems.at[pairing]
            )
        )
        copies[-1].start()
    for copy in copies:
        copy.wait()


def local_call(body, name, operands, out_shapes, scratch=(), far=(), far_out=(), aliases=None, room=16, cost=None):
    near_spec = pl.BlockSpec(memory_space=pltpu.VMEM)
    far_spec = pl.BlockSpec(memory_space=pltpu.HBM)
    shapes = [
        jax.ShapeDtypeStruct(shape, jnp.float32) if isinstance(shape, tuple) else shape
        for shape in out_shapes
    ]
    return pl.pallas_call(
        body,
        out_shape=shapes,
        in_specs=[far_spec if place in far else near_spec for place in range(len(operands))],
        out_specs=[far_spec if place in far_out else near_spec for place in range(len(shapes))],
        scratch_shapes=list(scratch),
        input_output_aliases=aliases or {},
        compiler_params=pltpu.CompilerParams(vmem_limit_bytes=room * 1024 * 1024),
        name=name,
        cost_estimate=cost,
    )(*operands)


def on_device(adjoint, momentum, design, solid_mask, port_label):
    levels, rows, lanes = adjoint.shape[1:]
    slots = lanes // tile
    groups = len(groups_of(levels))
    x_pairs, y_pairs, z_pairs = (len(pairings(axis)) for axis in ("gx", "gy", "depth"))
    loaded = local_call(
        functools.partial(load_kernel, z_pairs),
        "load",
        [
            pltpu.with_memory_space_constraint(array, pltpu.HBM)
            for array in (adjoint, momentum, design, solid_mask, port_label)
        ],
        [
            pltpu.VMEM(momentum.shape, jnp.float32),
            pltpu.VMEM(design.shape, jnp.float32),
            pltpu.VMEM(solid_mask.shape, jnp.int32),
            pltpu.VMEM(port_label.shape, jnp.int32),
        ]
        + [pltpu.VMEM((len(laterals), rows, lanes), jnp.float32)] * z_pairs,
        scratch=[pltpu.SemaphoreType.DMA((z_pairs * len(laterals) + 4,))],
        far=range(5),
    )
    momentum, design, solid_mask, port_label = loaded[:4]
    z_got = [swap(face, "depth", pairing) for pairing, face in enumerate(loaded[4:])]
    packed = local_call(
        functools.partial(pack_kernel, (x_pairs, y_pairs)),
        "pack_faces",
        [adjoint, momentum, design, solid_mask, port_label],
        [(rows, lanes)] * x_pairs
        + [(kinds * slots, lanes)] * y_pairs
        + [(rows, lanes), (2, 3, rows, lanes)],
    )
    filled = local_call(
        functools.partial(depth_kernel, (x_pairs, y_pairs, z_pairs), levels),
        "add_z_faces",
        [*z_got, *packed],
        [(rows + slots, lanes)] * x_pairs + [(kinds * slots, lanes)] * y_pairs + [(rows, lanes)],
    )
    x_sent, y_sent, own = (
        filled[:x_pairs],
        filled[x_pairs : x_pairs + y_pairs],
        filled[x_pairs + y_pairs],
    )
    y_got = [swap(y_sent[pairing], "gy", pairing) for pairing in range(y_pairs)]
    x_got = [None] * x_pairs
    for pairing in reversed(range(x_pairs)):
        x_got[pairing] = swap(x_sent[pairing], "gx", pairing)
    merged = local_call(
        functools.partial(middle_kernel, (x_pairs, y_pairs), levels),
        "add_x_faces",
        [*x_got[::-1], *x_sent, own],
        [(slots + 2 * tile, lanes)] * y_pairs + [(2, rows, lanes)],
    )
    ends_sent, middle = (merged[:y_pairs], merged[y_pairs])
    ends_got = [swap(ends_sent[pairing], "gy", pairing) for pairing in range(y_pairs)]
    new_adjoint, edge_rows, norm = local_call(
        functools.partial(collide_kernel, (x_pairs, y_pairs, z_pairs)),
        "collide",
        [adjoint, design, solid_mask, port_label, *x_got[::-1], *z_got],
        [adjoint.shape, (max(y_pairs, 1), len(velocities), levels, lanes), (rows, lanes)],
        scratch=[pltpu.VMEM(adjoint.shape, jnp.float32), pltpu.SemaphoreType.DMA((groups,))],
        far_out=(0,),
        cost=pl.CostEstimate(
            flops=8000 * math.prod(adjoint.shape), bytes_accessed=4000000, transcendentals=0
        ),
    )
    (column,) = local_call(
        functools.partial(extend_kernel, y_pairs),
        "add_y_faces",
        [*y_got, *y_sent, *ends_got, *ends_sent, middle, norm],
        [(2, rows + 2 * tile, lanes)],
    )
    if z_pairs == 1:
        other = swap(column, "depth", 0)
    else:
        other = lax.psum(column, "depth") - column
    if y_pairs:
        (new_adjoint,) = local_call(
            functools.partial(row_kernel, y_pairs),
            "add_y_rows",
            [new_adjoint, edge_rows, design, solid_mask, port_label, *y_got, *ends_got],
            [adjoint.shape],
            scratch=[
                pltpu.VMEM((y_pairs, len(velocities), levels, tile, lanes), jnp.float32),
                pltpu.SemaphoreType.DMA((y_pairs,)),
            ],
            far=(0,),
            far_out=(0,),
            aliases={0: 0},
        )
    (sensitivity,) = local_call(
        filter_kernel, "cone_filter", [column, other, norm], [(rows, lanes)]
    )
    return (new_adjoint, sensitivity)


def solution(mesh):
    in_specs = (
        P(None, "depth", "gy", "gx"),
        P(None, "depth", "gy", "gx"),
        P("gy", "gx"),
        P("depth", "gy", "gx"),
        P("depth", "gy", "gx"),
    )
    out_specs = (P(None, "depth", "gy", "gx"), P("gy", "gx"))
    return jax.shard_map(
        on_device, mesh=mesh, in_specs=in_specs, out_specs=out_specs, check_vma=False
    )
```

```python
import functools
import math

import jax
import jax.numpy as jnp
from jax import lax
from jax.experimental import pallas as pl
from jax.experimental.pallas import tpu as pltpu
from jax.sharding import PartitionSpec as P

velocities = (
    (0, 0, 0),
    (1, 0, 0),
    (-1, 0, 0),
    (0, 1, 0),
    (0, -1, 0),
    (0, 0, 1),
    (0, 0, -1),
    (1, 1, 0),
    (-1, -1, 0),
    (1, -1, 0),
    (-1, 1, 0),
    (1, 0, 1),
    (-1, 0, -1),
    (1, 0, -1),
    (-1, 0, 1),
    (0, 1, 1),
    (0, -1, -1),
    (0, 1, -1),
    (0, -1, 1),
)
lattice_weights = (1.0 / 3.0,) + (1.0 / 18.0,) * 6 + (1.0 / 36.0,) * 12
opposite = (0, 2, 1, 4, 3, 6, 5, 8, 7, 10, 9, 12, 11, 14, 13, 16, 15, 18, 17)
relax_rate = 1.25
damp_top = 0.5
cone_radius = 5.0
filter_reach = 4
wide = filter_reach + 1
tile = 8
level_group = 3
laterals = ((0, 0), (1, 0), (-1, 0), (0, 1), (0, -1))
lateral_weights = (1.0 / 18.0,) + (1.0 / 36.0,) * 4
kinds = len(laterals) + 3


def crossing(axis, sign):
    others = [other for other in range(3) if other != axis]
    return [
        next(
            number
            for number, vector in enumerate(velocities)
            if vector[axis] == sign and (vector[others[0]], vector[others[1]]) == lateral
        )
        for lateral in laterals
    ]


def cone(offset_y, offset_x):
    return max(0.0, cone_radius - math.sqrt(offset_y * offset_y + offset_x * offset_x))


def pairings(axis):
    return range(min(lax.axis_size(axis) - 1, 2))


def swap(array, axis, pairing):
    size, cores = (lax.axis_size(axis), lax.axis_size("depth"))
    pairs = []
    for low in range(pairing, size - 1, 2):
        pairs += [(low, low + 1), (low + 1, low)]
    alone = [place for place in range(size) if place not in dict(pairs)]
    if axis == "depth" or cores % 2 != 0 or not alone:
        return lax.ppermute(array, axis, pairs)
    full = [(a * cores + core, b * cores + core) for a, b in pairs for core in range(cores)]
    for place in alone:
        full += [(place * cores + core, place * cores + (core ^ 1)) for core in range(cores)]
    return lax.ppermute(array, (axis, "depth"), full)


def partner_after(axis, pairing):
    return lax.rem(lax.axis_index(axis) + pairing, 2) == 0


def partners(axis, pairing):
    place, after = (lax.axis_index(axis), partner_after(axis, pairing))
    none_before, none_after = (place == 0, place == lax.axis_size(axis) - 1)
    return (
        jnp.logical_not(jnp.logical_or(after, none_before)),
        jnp.logical_and(after, jnp.logical_not(none_after)),
    )


def present(axis, pairing, array):
    before, after = partners(axis, pairing)
    return pick(jnp.logical_or(before, after), array, jnp.zeros_like(array))


def pick(flag, yes, no):
    return lax.select(flag, yes, no)


def turn(array, shift, axis):
    shift = shift % array.shape[axis]
    return array if shift == 0 else pltpu.roll(array, shift, axis)


def lanes_of(shape):
    return lax.broadcasted_iota(jnp.int32, shape, len(shape) - 1)


def rows_of(shape):
    return lax.broadcasted_iota(jnp.int32, shape, len(shape) - 2)


def halves(axis, arrays):
    before, after = 0.0, 0.0
    for pairing, array in enumerate(arrays):
        is_before, is_after = partners(axis, pairing)
        none = jnp.zeros_like(array)
        before = before + pick(is_before, array, none)
        after = after + pick(is_after, array, none)
    return (before, after)


def depth_plane(adjoint, halo, number, level):
    levels = adjoint.shape[1]
    if 0 <= level < levels:
        return adjoint[number, level]
    sign = 1 if level == levels else -1
    side = halo[1] if sign > 0 else halo[0]
    return side[crossing(2, sign).index(number)]


def gain_of(momentum, scale, solid, port, level):
    kept = (solid[level] == 0) & (port[level] != 1)
    factor = jnp.where(kept, scale, 0.0)
    return [factor * momentum[part, level] for part in range(3)]


def along_x(plane, step):
    lane = lanes_of(plane.shape)
    edge = plane.shape[-1] - 1 if step > 0 else 0
    return jnp.where(lane == edge, 0.0, turn(plane, -step, 1))


def along_y(plane, step):
    row = rows_of(plane.shape)
    edge = plane.shape[-2] - 1 if step > 0 else 0
    return jnp.where(row == edge, 0.0, turn(plane, -step, 0))


def own_moment(take):
    heavy, light = (1.0 / 18.0, 1.0 / 36.0)
    p = {
        number: take(number, vector[2]) for number, vector in enumerate(velocities) if number != 0
    }
    for number in (7, 8, 9, 10):
        p[number] = along_y(p[number], velocities[number][1])
    right_x = along_x(heavy * p[1] + light * ((p[7] + p[9]) + (p[11] + p[13])), 1)
    left_x = along_x(heavy * p[2] + light * ((p[8] + p[10]) + (p[12] + p[14])), -1)
    right_y = along_x(light * (p[7] - p[9]), 1)
    left_y = along_x(light * (p[10] - p[8]), -1)
    right_z = along_x(light * (p[11] - p[13]), 1)
    left_z = along_x(light * (p[14] - p[12]), -1)
    lower_y = along_y(heavy * p[3] + light * (p[15] + p[17]), 1)
    upper_y = along_y(heavy * p[4] + light * (p[16] + p[18]), -1)
    lower_z = along_y(light * (p[15] - p[17]), 1)
    upper_z = along_y(light * (p[18] - p[16]), -1)
    moment_x = right_x - left_x
    moment_y = (lower_y - upper_y) + (right_y + left_y)
    moment_z = heavy * (p[5] - p[6]) + ((right_z + left_z) + (lower_z + upper_z))
    return (moment_x, moment_y, moment_z)


def groups_of(levels):
    return [(low, min(low + level_group, levels)) for low in range(0, levels, level_group)]


def run_all(copies):
    for copy in copies:
        copy.start()
    for copy in copies:
        copy.wait()


def face_kernel(z_pairs, adjoint, *refs):
    outs, sems = (refs[:z_pairs], refs[z_pairs])
    copies = []
    for pairing in range(z_pairs):
        after = partner_after("depth", pairing)
        level = jnp.where(after, adjoint.shape[1] - 1, 0)
        for kind, numbers in enumerate(zip(crossing(2, -1), crossing(2, 1))):
            number = jnp.where(after, numbers[0], numbers[1])
            source, target = (adjoint.at[number, level], outs[pairing].at[kind])
            copies.append(pltpu.make_async_copy(source, target, sems.at[len(copies)]))
    run_all(copies)


def pack_kernel(counts, adjoint, momentum, design, solid, port, *refs):
    x_pairs, y_pairs = counts
    x_out, refs = (refs[:x_pairs], refs[x_pairs:])
    y_out, refs = (refs[:y_pairs], refs[y_pairs:])
    own_out, edge_gain = refs
    levels, rows, lanes = adjoint.shape[1:]
    slots = lanes // tile
    assert levels + 3 <= slots
    scale = 6.0 * damp_top / ((1.0 + design[...]) * (1.0 + design[...]))
    lane = lanes_of((rows, lanes))
    for pairing in range(y_pairs):
        y_out[pairing][...] = jnp.zeros(y_out[pairing].shape, jnp.float32)
    total = jnp.zeros((rows, lanes), jnp.float32)
    first_pack = jnp.zeros((rows, lanes), jnp.float32)
    last_pack = jnp.zeros((rows, lanes), jnp.float32)
    for level in range(levels):
        gain = gain_of(momentum, scale, solid, port, level)
        moment = own_moment(
            lambda number, step: adjoint[number, level + step]
            if 0 <= level + step < levels
            else jnp.zeros((rows, lanes), jnp.float32)
        )
        total = total + (gain[0] * moment[0] + gain[1] * moment[1] + gain[2] * moment[2])
        for side, edge in enumerate((0, levels - 1)):
            if level == edge:
                for part in range(3):
                    edge_gain[side, part] = gain[part]
        for pairing in range(y_pairs):
            after = partner_after("gy", pairing)
            for part in range(3):
                place = (len(laterals) + part) * slots + level
                y_out[pairing][place : place + 1, :] = pick(
                    after, gain[part][rows - 1 : rows], gain[part][0:1]
                )
        for kind in range(kinds):
            if kind < len(laterals):
                first = adjoint[crossing(0, 1)[kind], level]
                last = adjoint[crossing(0, -1)[kind], level]
            else:
                first = last = gain[kind - len(laterals)]
            place = level * tile + kind
            first_pack = jnp.where(lane == place, turn(first, place, 1), first_pack)
            last_pack = jnp.where(lane == place, turn(last, place + 1, 1), last_pack)
    for pairing in range(y_pairs):
        after = partner_after("gy", pairing)
        for kind in range(len(laterals)):
            last, first = (crossing(1, -1)[kind], crossing(1, 1)[kind])
            y_out[pairing][kind * slots : kind * slots + levels, :] = pick(
                after, adjoint[last, :, rows - 1, :], adjoint[first, :, 0, :]
            )
    own_out[...] = total
    for pairing in range(x_pairs):
        x_out[pairing][...] = pick(partner_after("gx", pairing), last_pack, first_pack)


def depth_kernel(counts, levels, *refs):
    x_pairs, y_pairs, z_pairs = counts
    z_got, refs = (refs[:z_pairs], refs[z_pairs:])
    x_pack, refs = (refs[:x_pairs], refs[x_pairs:])
    y_pack, refs = (refs[:y_pairs], refs[y_pairs:])
    own, edge_gain, refs = (*refs[:2], refs[2:])
    x_out, refs = (refs[:x_pairs], refs[x_pairs:])
    y_out, own_out = (refs[:y_pairs], refs[y_pairs])
    rows, lanes = own.shape
    slots = lanes // tile
    halo = halves("depth", [got[...] for got in z_got])
    lane = lanes_of((rows, lanes))
    total = own[...]
    if z_pairs:
        for side, sign in enumerate((-1, 1)):
            gain = [edge_gain[side, part] for part in range(3)]
            for kind, (step_x_, step_y_) in enumerate(laterals):
                plane = halo[side][kind]
                pull = sign * gain[2]
                if step_x_ != 0:
                    plane = along_x(plane, step_x_)
                    pull = pull + step_x_ * gain[0]
                if step_y_ != 0:
                    plane = along_y(plane, step_y_)
                    pull = pull + step_y_ * gain[1]
                total = total + lateral_weights[kind] * plane * pull
    own_out[...] = total
    beyond = ((3, levels, 1), (4, -1, 0))
    for pairing in range(y_pairs):
        after = partner_after("gy", pairing)
        y_out[pairing][...] = y_pack[pairing][...]
        if z_pairs:
            for kind, level, side in beyond:
                planes = crossing(2, 1 if side else -1)
                last, first = (
                    halo[side][planes.index(crossing(1, sign)[kind])] for sign in (-1, 1)
                )
                place = kind * slots + level % slots
                y_out[pairing][place : place + 1, :] = pick(
                    after, last[rows - 1 : rows], first[0:1]
                )
    spare = (levels + 1) * tile
    chosen = (lane >= spare) & (lane < spare + filter_reach)
    packs = []
    for edge_shift, sign, sums in ((0, 1, 0), (1, -1, filter_reach)):
        pack = jnp.where(chosen, turn(total, spare + sums, 1), 0.0)
        if z_pairs:
            for kind, level, side in beyond:
                planes = crossing(2, 1 if side else -1)
                plane = halo[side][planes.index(crossing(0, sign)[kind])]
                place = (level % slots) * tile + kind
                pack = jnp.where(lane == place, turn(plane, place + edge_shift, 1), pack)
        packs.append(pack)
    ends = [jnp.zeros((slots, lanes), jnp.float32) for side in range(2)]
    lane = lanes_of((slots, lanes))
    for pairing in range(y_pairs):
        for kind in range(kinds):
            line = y_out[pairing][kind * slots : (kind + 1) * slots, :]
            place = (pairing * kinds + kind) * wide
            chosen = (lane >= place) & (lane < place + wide)
            ends[0] = jnp.where(chosen, turn(line, place, 1), ends[0])
            ends[1] = jnp.where(chosen, turn(line, place + wide, 1), ends[1])
    for pairing in range(x_pairs):
        after = partner_after("gx", pairing)
        x_out[pairing][0:rows, :] = x_pack[pairing][...] + pick(after, packs[1], packs[0])
        x_out[pairing][rows : rows + slots, :] = pick(after, ends[1], ends[0])


def cross_x(levels, faces, gains, sign):
    rows, lanes = faces.shape
    lane, row = (lanes_of(faces.shape), rows_of(faces.shape))
    gain = [turn(gains, -(len(laterals) + part), 1) for part in range(3)]
    total = jnp.zeros_like(faces)
    for kind, (step_y, step_z) in enumerate(laterals):
        source = turn(faces, -kind - tile * step_z, 1)
        pull = sign * gain[0]
        if step_y != 0:
            edge = rows - 1 if step_y > 0 else 0
            source = jnp.where(row == edge, 0.0, turn(source, -step_y, 0))
            pull = pull + step_y * gain[1]
        if step_z != 0:
            pull = pull + step_z * gain[2]
        total = total + lateral_weights[kind] * source * pull
    used = (lane % tile == 0) & (lane < tile * levels)
    return jnp.sum(jnp.where(used, total, 0.0), axis=1, keepdims=True)


def middle_kernel(counts, levels, *refs):
    x_pairs, y_pairs = counts
    x_got, refs = (refs[:x_pairs][::-1], refs[x_pairs:])
    x_sent, refs = (refs[:x_pairs], refs[x_pairs:])
    own, refs = (refs[0], refs[1:])
    y_out, middle = (refs[:y_pairs], refs[y_pairs])
    rows, lanes = own.shape
    slots = lanes // tile
    lane = lanes_of((rows, lanes))
    main = own[...]
    side = jnp.zeros((rows, lanes), jnp.float32)
    spare = (levels + 1) * tile
    for pairing in range(x_pairs):
        after = partner_after("gx", pairing)
        sign = jnp.where(after, 1.0, -1.0)
        got = present("gx", pairing, x_got[pairing][0:rows, :])
        sent = x_sent[pairing][0:rows, :]
        there = cross_x(levels, sent, got, -sign)
        here = cross_x(levels, got, sent, sign)
        right = jnp.where(lane < filter_reach, turn(got, -spare, 1), 0.0)
        right = right + jnp.where(lane == 0, there, 0.0)
        left = jnp.where(lane >= lanes - filter_reach, turn(got, -spare - filter_reach, 1), 0.0)
        left = left + jnp.where(lane == lanes - 1, there, 0.0)
        side = side + pick(after, right, left)
        edge = jnp.where(after, lanes - 1, 0)
        main = main + jnp.where(lane == edge, here, 0.0)
    middle[0] = main
    middle[1] = side
    left_ends, right_ends = halves("gx", [got[rows : rows + slots, :] for got in x_got])
    lane = lanes_of((slots, lanes))
    size = kinds * wide
    for pairing in range(y_pairs):
        after = partner_after("gy", pairing)
        out = y_out[pairing]
        ends = jnp.zeros((slots, lanes), jnp.float32)
        if x_pairs:
            ends = jnp.where(lane < size, turn(left_ends, -pairing * size, 1), ends)
            ends = jnp.where(
                (lane >= size) & (lane < 2 * size), turn(right_ends, size - pairing * size, 1), ends
            )
        out[0:slots, :] = ends
        for number, part in enumerate((main, side)):
            place = slots + number * tile
            out[place : place + tile, :] = pick(after, part[rows - tile :], part[0:tile])


def spread_ends(ends, kind, lanes):
    lane = lanes_of(ends.shape)
    size = kinds * wide
    right = jnp.where(lane < wide, turn(ends, -size - kind * wide, 1), 0.0)
    return jnp.where(lane >= lanes - wide, turn(ends, -wide - kind * wide, 1), right)


def step_x(main, side, step):
    if step == 0:
        return (main, side)
    lane = lanes_of(main.shape)
    edge = lane == (main.shape[-1] - 1 if step > 0 else 0)
    main, side = (turn(main, -step, 1), turn(side, -step, 1))
    return (jnp.where(edge, side, main), jnp.where(edge, main, side))


def cross_y(faces, gains, sign):
    total_main, total_side = (0.0, 0.0)
    for kind, (lateral_x, lateral_z) in enumerate(laterals):
        main, side = step_x(*faces[kind], lateral_x)
        main, side = (turn(main, -lateral_z, 0), turn(side, -lateral_z, 0))
        pull_main, pull_side = (sign * gains[1][0], sign * gains[1][1])
        if lateral_x != 0:
            pull_main = pull_main + lateral_x * gains[0][0]
            pull_side = pull_side + lateral_x * gains[0][1]
        if lateral_z != 0:
            pull_main = pull_main + lateral_z * gains[2][0]
            pull_side = pull_side + lateral_z * gains[2][1]
        total_main = total_main + lateral_weights[kind] * main * pull_main
        total_side = total_side + lateral_weights[kind] * side * pull_side
    return (
        jnp.sum(total_main, axis=0, keepdims=True),
        jnp.sum(total_side, axis=0, keepdims=True),
    )


def face_lines(lines, ends, slots, lanes):
    return [
        (lines[kind * slots : (kind + 1) * slots], spread_ends(ends[0:slots], kind, lanes))
        for kind in range(kinds)
    ]


def extend_kernel(y_pairs, *refs):
    y_got, refs = (refs[:y_pairs], refs[y_pairs:])
    y_sent, refs = (refs[:y_pairs], refs[y_pairs:])
    ends_got, refs = (refs[:y_pairs], refs[y_pairs:])
    ends_sent, refs = (refs[:y_pairs], refs[y_pairs:])
    middle, norm, out = refs
    rows, lanes = middle.shape[1:]
    slots = lanes // tile
    row, row_tile = (rows_of((rows, lanes)), rows_of((tile, lanes)))
    own = [middle[0], middle[1]]
    before = [jnp.zeros((tile, lanes), jnp.float32) for part in range(2)]
    after = [jnp.zeros((tile, lanes), jnp.float32) for part in range(2)]
    for pairing in range(y_pairs):
        flag = partner_after("gy", pairing)
        sign = jnp.where(flag, 1.0, -1.0)
        got_lines = present("gy", pairing, y_got[pairing][...])
        got_ends = present("gy", pairing, ends_got[pairing][...])
        got = face_lines(got_lines, got_ends, slots, lanes)
        sent = face_lines(y_sent[pairing][...], ends_sent[pairing][...], slots, lanes)
        there = cross_y(sent[:5], got[5:], -sign)
        here = cross_y(got[:5], sent[5:], sign)
        edge_here = jnp.where(flag, rows - 1, 0)
        edge_there = jnp.where(flag, 0, tile - 1)
        for part in range(2):
            place = slots + part * tile
            sums = got_ends[place : place + tile]
            sums = sums + jnp.where(row_tile == edge_there, there[part], 0.0)
            none = jnp.zeros_like(sums)
            before[part] = before[part] + pick(flag, none, sums)
            after[part] = after[part] + pick(flag, sums, none)
            own[part] = own[part] + jnp.where(row == edge_here, here[part], 0.0)
    main, side = (
        jnp.concatenate([before[part], own[part], after[part]], axis=0) for part in range(2)
    )
    out[...] = cone_sum(main, side, rows) * norm[...]


def cone_sum(main, side, rows):
    lanes = main.shape[-1]
    lane = lanes_of(main.shape)
    pairs = [main]
    for offset in range(1, filter_reach + 1):
        up = jnp.where(lane < lanes - offset, turn(main, -offset, 1), turn(side, -offset, 1))
        down = jnp.where(lane >= offset, turn(main, offset, 1), turn(side, offset, 1))
        pairs.append(up + down)
    total = jnp.zeros((rows, lanes), jnp.float32)
    for offset in range(filter_reach + 1):
        weighted = jnp.zeros_like(main)
        for distance, pair in enumerate(pairs):
            weight = cone(offset, distance)
            if weight > 0.0:
                weighted = weighted + weight * pair
        for step in sorted({offset, -offset}):
            total = total + turn(weighted, -step, 0)[tile : tile + rows]
    return total


def filter_kernel(mine, other, out):
    out[...] = mine[...] + other[...]


def filter_norm(rows, lanes):
    shape = (rows + 2 * tile, lanes)
    row, lane = (rows_of(shape), lanes_of(shape))
    place = lax.axis_index("gy") * rows + row - tile
    inside = jnp.where((place >= 0) & (place < lax.axis_size("gy") * rows), 1.0, 0.0)
    left = (lax.axis_index("gx") > 0).astype(jnp.float32)
    right = (lax.axis_index("gx") < lax.axis_size("gx") - 1).astype(jnp.float32)
    beside = inside * jnp.where(lane < lanes // 2, right, left)
    return 1.0 / cone_sum(inside, beside, rows)


def collide_kernel(counts, adjoint, design, solid, port, *refs):
    x_pairs, y_pairs, z_pairs = counts
    x_got, refs = (refs[:x_pairs][::-1], refs[x_pairs:])
    z_got, refs = (refs[:z_pairs], refs[z_pairs:])
    far, edge_rows, norm, out, sems = refs
    levels, rows, lanes = adjoint.shape[1:]
    slots = lanes // tile
    halo_z = halves("depth", [got[...] for got in z_got])
    halo_x = halves("gx", [got[0:rows, :] for got in x_got])
    damping = damp_top * (1.0 - design[...]) / (1.0 + design[...])
    rate = 3.0 * (relax_rate - damping)
    lane = lanes_of((rows, lanes))
    copies = []
    for level in range(levels):
        pulled = []
        for number, (step_x_, step_y_, step_z_) in enumerate(velocities):
            source = level + step_z_
            if z_pairs or 0 <= source < levels:
                plane = depth_plane(adjoint, halo_z, number, source)
            else:
                plane = jnp.zeros((rows, lanes), jnp.float32)
            if step_x_ != 0:
                edge = lanes - 1 if step_x_ > 0 else 0
                column = 0.0
                if x_pairs:
                    kind = crossing(0, step_x_).index(number)
                    place = (source % slots) * tile + kind
                    column = turn(halo_x[1 if step_x_ > 0 else 0], edge - place, 1)
                plane = jnp.where(lane == edge, column, turn(plane, -step_x_, 1))
            if step_y_ != 0:
                plane = along_y(plane, step_y_)
            pulled.append(plane)
        zeroth, moment = sums_of(pulled)
        base = relax_rate * zeroth
        scaled = [rate * part for part in moment]
        fluid, inlet = (solid[level] == 0, port[level] == 1)
        outflow = jnp.where(port[level] == 2, 1.0, 0.0)
        for number, vector in enumerate(velocities):
            updated = base + (1.0 - relax_rate) * pulled[number]
            if number > 0:
                updated = updated + along(vector, scaled)
            updated = jnp.where(fluid, updated, pulled[opposite[number]])
            updated = jnp.where(inlet, 0.0, updated)
            if vector[0] != 0:
                updated = updated + vector[0] * outflow
            out[number, level] = updated
        for place, (low, high) in enumerate(groups_of(levels)):
            if level == high - 1:
                copy = pltpu.make_async_copy(
                    out.at[:, low:high], far.at[:, low:high], sems.at[place]
                )
                copy.start()
                copies.append(copy)
    for pairing in range(y_pairs):
        after = partner_after("gy", pairing)
        for number in range(len(velocities)):
            edge_rows[pairing, number] = pick(after, out[number, :, rows - 1, :], out[number, :, 0, :])
    norm[...] = filter_norm(rows, lanes)
    for copy in copies:
        copy.wait()


def along(vector, parts):
    total = 0.0
    for component, part in zip(vector, parts):
        if component > 0:
            total = total + part
        if component < 0:
            total = total - part
    return total


def sums_of(pulled):
    heavy, light = (lattice_weights[1], lattice_weights[7])
    both, gap = ({}, {})
    for number in range(1, len(velocities), 2):
        both[number] = pulled[number] + pulled[number + 1]
        gap[number] = pulled[number] - pulled[number + 1]
    zeroth = lattice_weights[0] * pulled[0] + heavy * ((both[1] + both[3]) + both[5])
    zeroth = zeroth + light * (((both[7] + both[9]) + (both[11] + both[13])) + (both[15] + both[17]))
    moment = (
        heavy * gap[1] + light * ((gap[7] + gap[9]) + (gap[11] + gap[13])),
        heavy * gap[3] + light * ((gap[7] - gap[9]) + (gap[15] + gap[17])),
        heavy * gap[5] + light * ((gap[11] - gap[13]) + (gap[15] - gap[17])),
    )
    return (zeroth, moment)


def row_kernel(y_pairs, new, edge_rows, design, solid, port, *refs):
    y_got, refs = (refs[:y_pairs], refs[y_pairs:])
    ends_got, (far, out, sems) = (refs[:y_pairs], refs[y_pairs:])
    levels, rows, lanes = solid.shape
    slots = lanes // tile
    copies = []
    for pairing in range(y_pairs):
        after = partner_after("gy", pairing)
        sign = jnp.where(after, 1.0, -1.0)
        got = present("gy", pairing, y_got[pairing][...])
        ends = present("gy", pairing, ends_got[pairing][0:slots, :])
        extra, moment = ({}, [0.0, 0.0, 0.0])
        zeroth = 0.0
        for kind, (lateral_x, lateral_z) in enumerate(laterals):
            line = got[kind * slots : (kind + 1) * slots]
            if lateral_x != 0:
                line = step_x(line, spread_ends(ends, kind, lanes), lateral_x)[0]
            line = turn(line, -lateral_z, 0)[0:levels]
            none = jnp.zeros_like(line)
            extra[crossing(1, 1)[kind]] = pick(after, line, none)
            extra[crossing(1, -1)[kind]] = pick(after, none, line)
            weighted = lateral_weights[kind] * line
            zeroth = zeroth + weighted
            moment[0] = moment[0] + lateral_x * weighted
            moment[2] = moment[2] + lateral_z * weighted
        moment[1] = sign * zeroth
        edge_design = pick(after, design[rows - 1 : rows, :], design[0:1, :])
        damping = damp_top * (1.0 - edge_design) / (1.0 + edge_design)
        rate = 3.0 * (relax_rate - damping)
        fluid = pick(after, solid[:, rows - 1, :], solid[:, 0, :]) == 0
        inlet = pick(after, port[:, rows - 1, :], port[:, 0, :]) == 1
        scaled = [rate * part for part in moment]
        base = relax_rate * zeroth
        for number, vector in enumerate(velocities):
            added = base
            if number > 0:
                added = added + along(vector, scaled)
            if number in extra:
                added = added + (1.0 - relax_rate) * extra[number]
            added = jnp.where(fluid, added, extra.get(opposite[number], 0.0))
            added = jnp.where(inlet, 0.0, added)
            out[pairing, number, :, 0, :] = edge_rows[pairing, number] + added
        place = jnp.where(after, rows - 1, 0)
        copies.append(
            pltpu.make_async_copy(
                out.at[pairing, :, :, 0:1, :], far.at[:, :, pl.ds(place, 1), :], sems.at[pairing]
            )
        )
        copies[-1].start()
    for copy in copies:
        copy.wait()


def local_call(body, name, operands, out_shapes, scratch=(), far=(), far_out=(), aliases=None, room=16, cost=None):
    near_spec = pl.BlockSpec(memory_space=pltpu.VMEM)
    far_spec = pl.BlockSpec(memory_space=pltpu.HBM)
    shapes = [
        jax.ShapeDtypeStruct(shape, jnp.float32) if isinstance(shape, tuple) else shape
        for shape in out_shapes
    ]
    return pl.pallas_call(
        body,
        out_shape=shapes,
        in_specs=[far_spec if place in far else near_spec for place in range(len(operands))],
        out_specs=[far_spec if place in far_out else near_spec for place in range(len(shapes))],
        scratch_shapes=list(scratch),
        input_output_aliases=aliases or {},
        compiler_params=pltpu.CompilerParams(vmem_limit_bytes=room * 1024 * 1024),
        name=name,
        cost_estimate=cost,
    )(*operands)


def on_device(adjoint, momentum, design, solid_mask, port_label):
    levels, rows, lanes = adjoint.shape[1:]
    slots = lanes // tile
    groups = len(groups_of(levels))
    x_pairs, y_pairs, z_pairs = (len(pairings(axis)) for axis in ("gx", "gy", "depth"))
    z_got = []
    if z_pairs:
        faces = local_call(
            functools.partial(face_kernel, z_pairs),
            "depth_faces",
            [pltpu.with_memory_space_constraint(adjoint, pltpu.HBM)],
            [pltpu.VMEM((len(laterals), rows, lanes), jnp.float32)] * z_pairs,
            scratch=[pltpu.SemaphoreType.DMA((z_pairs * len(laterals),))],
            far=(0,),
            cost=pl.CostEstimate(flops=2000 * math.prod(adjoint.shape), bytes_accessed=100000, transcendentals=0),
        )
        z_got = [swap(face, "depth", pairing) for pairing, face in enumerate(faces)]
    packed = local_call(
        functools.partial(pack_kernel, (x_pairs, y_pairs)),
        "pack_faces",
        [adjoint, momentum, design, solid_mask, port_label],
        [(rows, lanes)] * x_pairs
        + [(kinds * slots, lanes)] * y_pairs
        + [(rows, lanes), (2, 3, rows, lanes)],
    )
    filled = local_call(
        functools.partial(depth_kernel, (x_pairs, y_pairs, z_pairs), levels),
        "add_z_faces",
        [*z_got, *packed],
        [(rows + slots, lanes)] * x_pairs + [(kinds * slots, lanes)] * y_pairs + [(rows, lanes)],
    )
    x_sent, y_sent, own = (
        filled[:x_pairs],
        filled[x_pairs : x_pairs + y_pairs],
        filled[x_pairs + y_pairs],
    )
    y_got = [swap(y_sent[pairing], "gy", pairing) for pairing in range(y_pairs)]
    x_got = [None] * x_pairs
    for pairing in reversed(range(x_pairs)):
        x_got[pairing] = swap(x_sent[pairing], "gx", pairing)
    merged = local_call(
        functools.partial(middle_kernel, (x_pairs, y_pairs), levels),
        "add_x_faces",
        [*x_got[::-1], *x_sent, own],
        [(slots + 2 * tile, lanes)] * y_pairs + [(2, rows, lanes)],
    )
    ends_sent, middle = (merged[:y_pairs], merged[y_pairs])
    ends_got = [swap(ends_sent[pairing], "gy", pairing) for pairing in range(y_pairs)]
    new_adjoint, edge_rows, norm = local_call(
        functools.partial(collide_kernel, (x_pairs, y_pairs, z_pairs)),
        "collide",
        [adjoint, design, solid_mask, port_label, *x_got[::-1], *z_got],
        [adjoint.shape, (max(y_pairs, 1), len(velocities), levels, lanes), (rows, lanes)],
        scratch=[pltpu.VMEM(adjoint.shape, jnp.float32), pltpu.SemaphoreType.DMA((groups,))],
        far_out=(0,),
        cost=pl.CostEstimate(
            flops=8000 * math.prod(adjoint.shape), bytes_accessed=4000000, transcendentals=0
        ),
    )
    (column,) = local_call(
        functools.partial(extend_kernel, y_pairs),
        "add_y_faces",
        [*y_got, *y_sent, *ends_got, *ends_sent, middle, norm],
        [(rows, lanes)],
    )
    if z_pairs == 1:
        other = swap(column, "depth", 0)
    else:
        other = lax.psum(column, "depth") - column
    if y_pairs:
        (new_adjoint,) = local_call(
            functools.partial(row_kernel, y_pairs),
            "add_y_rows",
            [new_adjoint, edge_rows, design, solid_mask, port_label, *y_got, *ends_got],
            [adjoint.shape],
            scratch=[
                pltpu.VMEM((y_pairs, len(velocities), levels, tile, lanes), jnp.float32),
                pltpu.SemaphoreType.DMA((y_pairs,)),
            ],
            far=(0,),
            far_out=(0,),
            aliases={0: 0},
        )
    (sensitivity,) = local_call(
        filter_kernel, "add_depth", [column, other], [(rows, lanes)]
    )
    return (new_adjoint, sensitivity)


def solution(mesh):
    in_specs = (
        P(None, "depth", "gy", "gx"),
        P(None, "depth", "gy", "gx"),
        P("gy", "gx"),
        P("depth", "gy", "gx"),
        P("depth", "gy", "gx"),
    )
    out_specs = (P(None, "depth", "gy", "gx"), P("gy", "gx"))
    return jax.shard_map(
        on_device, mesh=mesh, in_specs=in_specs, out_specs=out_specs, check_vma=False
    )
```

```python
import functools
import math

import jax
import jax.numpy as jnp
from jax import lax
from jax.experimental import pallas as pl
from jax.experimental.pallas import tpu as pltpu
from jax.sharding import PartitionSpec as P

velocities = (
    (0, 0, 0),
    (1, 0, 0),
    (-1, 0, 0),
    (0, 1, 0),
    (0, -1, 0),
    (0, 0, 1),
    (0, 0, -1),
    (1, 1, 0),
    (-1, -1, 0),
    (1, -1, 0),
    (-1, 1, 0),
    (1, 0, 1),
    (-1, 0, -1),
    (1, 0, -1),
    (-1, 0, 1),
    (0, 1, 1),
    (0, -1, -1),
    (0, 1, -1),
    (0, -1, 1),
)
lattice_weights = (1.0 / 3.0,) + (1.0 / 18.0,) * 6 + (1.0 / 36.0,) * 12
opposite = (0, 2, 1, 4, 3, 6, 5, 8, 7, 10, 9, 12, 11, 14, 13, 16, 15, 18, 17)
relax_rate = 1.25
damp_top = 0.5
cone_radius = 5.0
filter_reach = 4
wide = filter_reach + 1
tile = 8
level_group = 3
laterals = ((0, 0), (1, 0), (-1, 0), (0, 1), (0, -1))
lateral_weights = (1.0 / 18.0,) + (1.0 / 36.0,) * 4
kinds = len(laterals) + 3
both_ends = 2 * wide


def spot(kind):
    return 2 * kind + 1 if kind < kinds // 2 else 2 * kind - kinds


def crossing(axis, sign):
    others = [other for other in range(3) if other != axis]
    return [
        next(
            number
            for number, vector in enumerate(velocities)
            if vector[axis] == sign and (vector[others[0]], vector[others[1]]) == lateral
        )
        for lateral in laterals
    ]


def cone(offset_y, offset_x):
    return max(0.0, cone_radius - math.sqrt(offset_y * offset_y + offset_x * offset_x))


def pairings(axis):
    return range(min(lax.axis_size(axis) - 1, 2))


def swap(array, axis, pairing):
    size, cores = (lax.axis_size(axis), lax.axis_size("depth"))
    pairs = []
    for low in range(pairing, size - 1, 2):
        pairs += [(low, low + 1), (low + 1, low)]
    alone = [place for place in range(size) if place not in dict(pairs)]
    if axis == "depth" or cores % 2 != 0 or not alone:
        return lax.ppermute(array, axis, pairs)
    full = [(a * cores + core, b * cores + core) for a, b in pairs for core in range(cores)]
    for place in alone:
        full += [(place * cores + core, place * cores + (core ^ 1)) for core in range(cores)]
    return lax.ppermute(array, (axis, "depth"), full)


def partner_after(axis, pairing):
    return lax.rem(lax.axis_index(axis) + pairing, 2) == 0


def partners(axis, pairing):
    place, after = (lax.axis_index(axis), partner_after(axis, pairing))
    none_before, none_after = (place == 0, place == lax.axis_size(axis) - 1)
    return (
        jnp.logical_not(jnp.logical_or(after, none_before)),
        jnp.logical_and(after, jnp.logical_not(none_after)),
    )


def present(axis, pairing, array):
    before, after = partners(axis, pairing)
    return pick(jnp.logical_or(before, after), array, jnp.zeros_like(array))


def pick(flag, yes, no):
    return lax.select(flag, yes, no)


def turn(array, shift, axis):
    shift = shift % array.shape[axis]
    return array if shift == 0 else pltpu.roll(array, shift, axis)


def lanes_of(shape):
    return lax.broadcasted_iota(jnp.int32, shape, len(shape) - 1)


def rows_of(shape):
    return lax.broadcasted_iota(jnp.int32, shape, len(shape) - 2)


def halves(axis, arrays):
    before, after = 0.0, 0.0
    for pairing, array in enumerate(arrays):
        is_before, is_after = partners(axis, pairing)
        none = jnp.zeros_like(array)
        before = before + pick(is_before, array, none)
        after = after + pick(is_after, array, none)
    return (before, after)


def depth_plane(adjoint, halo, number, level):
    levels = adjoint.shape[1]
    if 0 <= level < levels:
        return adjoint[number, level]
    sign = 1 if level == levels else -1
    side = halo[1] if sign > 0 else halo[0]
    return side[crossing(2, sign).index(number)]


def gain_of(momentum, scale, solid, port, level):
    kept = (solid[level] == 0) & (port[level] != 1)
    factor = jnp.where(kept, scale, 0.0)
    return [factor * momentum[part, level] for part in range(3)]


def along_x(plane, step):
    lane = lanes_of(plane.shape)
    edge = plane.shape[-1] - 1 if step > 0 else 0
    return jnp.where(lane == edge, 0.0, turn(plane, -step, 1))


def along_y(plane, step):
    row = rows_of(plane.shape)
    edge = plane.shape[-2] - 1 if step > 0 else 0
    return jnp.where(row == edge, 0.0, turn(plane, -step, 0))


def own_moment(take):
    heavy, light = (1.0 / 18.0, 1.0 / 36.0)
    p = {
        number: take(number, vector[2]) for number, vector in enumerate(velocities) if number != 0
    }
    for number in (7, 8, 9, 10):
        p[number] = along_y(p[number], velocities[number][1])
    right_x = along_x(heavy * p[1] + light * ((p[7] + p[9]) + (p[11] + p[13])), 1)
    left_x = along_x(heavy * p[2] + light * ((p[8] + p[10]) + (p[12] + p[14])), -1)
    right_y = along_x(light * (p[7] - p[9]), 1)
    left_y = along_x(light * (p[10] - p[8]), -1)
    right_z = along_x(light * (p[11] - p[13]), 1)
    left_z = along_x(light * (p[14] - p[12]), -1)
    lower_y = along_y(heavy * p[3] + light * (p[15] + p[17]), 1)
    upper_y = along_y(heavy * p[4] + light * (p[16] + p[18]), -1)
    lower_z = along_y(light * (p[15] - p[17]), 1)
    upper_z = along_y(light * (p[18] - p[16]), -1)
    moment_x = right_x - left_x
    moment_y = (lower_y - upper_y) + (right_y + left_y)
    moment_z = heavy * (p[5] - p[6]) + ((right_z + left_z) + (lower_z + upper_z))
    return (moment_x, moment_y, moment_z)


def groups_of(levels):
    return [(low, min(low + level_group, levels)) for low in range(0, levels, level_group)]


def run_all(copies):
    for copy in copies:
        copy.start()
    for copy in copies:
        copy.wait()


def face_kernel(z_pairs, adjoint, *refs):
    outs, sems = (refs[:z_pairs], refs[z_pairs])
    copies = []
    for pairing in range(z_pairs):
        after = partner_after("depth", pairing)
        level = jnp.where(after, adjoint.shape[1] - 1, 0)
        for kind, numbers in enumerate(zip(crossing(2, -1), crossing(2, 1))):
            number = jnp.where(after, numbers[0], numbers[1])
            source, target = (adjoint.at[number, level], outs[pairing].at[kind])
            copies.append(pltpu.make_async_copy(source, target, sems.at[len(copies)]))
    run_all(copies)


def pack_kernel(counts, adjoint, momentum, design, solid, port, *refs):
    x_pairs, y_pairs = counts
    x_out, refs = (refs[:x_pairs], refs[x_pairs:])
    y_out, refs = (refs[:y_pairs], refs[y_pairs:])
    own_out, edge_gain = refs
    levels, rows, lanes = adjoint.shape[1:]
    slots = lanes // tile
    assert levels + 3 <= slots
    scale = 6.0 * damp_top / ((1.0 + design[...]) * (1.0 + design[...]))
    lane = lanes_of((rows, lanes))
    for pairing in range(y_pairs):
        y_out[pairing][...] = jnp.zeros(y_out[pairing].shape, jnp.float32)
    total = jnp.zeros((rows, lanes), jnp.float32)
    joint = [jnp.zeros((rows, lanes), jnp.float32) for half in range(2)]
    for level in range(levels):
        gain = gain_of(momentum, scale, solid, port, level)
        moment = own_moment(
            lambda number, step: adjoint[number, level + step]
            if 0 <= level + step < levels
            else jnp.zeros((rows, lanes), jnp.float32)
        )
        total = total + (gain[0] * moment[0] + gain[1] * moment[1] + gain[2] * moment[2])
        for side, edge in enumerate((0, levels - 1)):
            if level == edge:
                for part in range(3):
                    edge_gain[side, part] = gain[part]
        for pairing in range(y_pairs):
            after = partner_after("gy", pairing)
            for part in range(3):
                place = (len(laterals) + part) * slots + level
                y_out[pairing][place : place + 1, :] = pick(
                    after, gain[part][rows - 1 : rows], gain[part][0:1]
                )
        for kind in range(kinds):
            if kind < len(laterals):
                first = adjoint[crossing(0, 1)[kind], level]
                last = adjoint[crossing(0, -1)[kind], level]
                plane = jnp.where(lane == lanes - 1, last, first)
            else:
                plane = gain[kind - len(laterals)]
            half, place = (kind // (kinds // 2), level * tile + 2 * (kind % (kinds // 2)))
            chosen = lane // 2 == place // 2
            joint[half] = jnp.where(chosen, turn(plane, place + 1, 1), joint[half])
    for pairing in range(y_pairs):
        after = partner_after("gy", pairing)
        for kind in range(len(laterals)):
            last, first = (crossing(1, -1)[kind], crossing(1, 1)[kind])
            y_out[pairing][kind * slots : kind * slots + levels, :] = pick(
                after, adjoint[last, :, rows - 1, :], adjoint[first, :, 0, :]
            )
    own_out[...] = total
    odd = lane % 2 == 1
    first_pack = jnp.where(odd, joint[0], turn(joint[1], -1, 1))
    last_pack = jnp.where(odd, turn(joint[0], 1, 1), joint[1])
    for pairing in range(x_pairs):
        x_out[pairing][...] = pick(partner_after("gx", pairing), last_pack, first_pack)


def depth_kernel(counts, levels, *refs):
    x_pairs, y_pairs, z_pairs = counts
    z_got, refs = (refs[:z_pairs], refs[z_pairs:])
    x_pack, refs = (refs[:x_pairs], refs[x_pairs:])
    y_pack, refs = (refs[:y_pairs], refs[y_pairs:])
    own, edge_gain, refs = (*refs[:2], refs[2:])
    x_out, refs = (refs[:x_pairs], refs[x_pairs:])
    y_out, own_out = (refs[:y_pairs], refs[y_pairs])
    rows, lanes = own.shape
    slots = lanes // tile
    halo = halves("depth", [got[...] for got in z_got])
    lane = lanes_of((rows, lanes))
    total = own[...]
    if z_pairs:
        for side, sign in enumerate((-1, 1)):
            gain = [edge_gain[side, part] for part in range(3)]
            for kind, (step_x_, step_y_) in enumerate(laterals):
                plane = halo[side][kind]
                pull = sign * gain[2]
                if step_x_ != 0:
                    plane = along_x(plane, step_x_)
                    pull = pull + step_x_ * gain[0]
                if step_y_ != 0:
                    plane = along_y(plane, step_y_)
                    pull = pull + step_y_ * gain[1]
                total = total + lateral_weights[kind] * plane * pull
    own_out[...] = total
    beyond = ((3, levels, 1), (4, -1, 0))
    for pairing in range(y_pairs):
        after = partner_after("gy", pairing)
        y_out[pairing][...] = y_pack[pairing][...]
        if z_pairs:
            for kind, level, side in beyond:
                planes = crossing(2, 1 if side else -1)
                last, first = (
                    halo[side][planes.index(crossing(1, sign)[kind])] for sign in (-1, 1)
                )
                place = kind * slots + level % slots
                y_out[pairing][place : place + 1, :] = pick(
                    after, last[rows - 1 : rows], first[0:1]
                )
    spare = (levels + 1) * tile
    chosen = (lane >= spare) & (lane < spare + 2 * filter_reach)
    sums = jnp.where(chosen, turn(total, spare + filter_reach, 1), 0.0)
    packs = []
    for edge_shift, sign in ((0, 1), (1, -1)):
        pack = sums
        if z_pairs:
            for kind, level, side in beyond:
                planes = crossing(2, 1 if side else -1)
                plane = halo[side][planes.index(crossing(0, sign)[kind])]
                place = (level % slots) * tile + spot(kind)
                pack = jnp.where(lane == place, turn(plane, place + edge_shift, 1), pack)
        packs.append(pack)
    for pairing in range(x_pairs):
        after = partner_after("gx", pairing)
        x_out[pairing][0:rows, :] = x_pack[pairing][...] + pick(after, packs[1], packs[0])
    lane = lanes_of((slots, lanes))
    for y_pairing in range(y_pairs):
        ends = jnp.zeros((slots, lanes), jnp.float32)
        for kind in range(kinds):
            line = y_out[y_pairing][kind * slots : (kind + 1) * slots, :]
            place = kind * both_ends
            chosen = (lane >= place) & (lane < place + both_ends)
            ends = jnp.where(chosen, turn(line, place + wide, 1), ends)
        for pairing in range(x_pairs):
            base = rows + y_pairing * slots
            x_out[pairing][base : base + slots, :] = ends


def cross_x(levels, faces, gains, sign):
    rows, lanes = faces.shape
    lane, row = (lanes_of(faces.shape), rows_of(faces.shape))
    gain = [turn(gains, -spot(len(laterals) + part), 1) for part in range(3)]
    total = jnp.zeros_like(faces)
    for kind, (step_y, step_z) in enumerate(laterals):
        source = turn(faces, -spot(kind) - tile * step_z, 1)
        pull = sign * gain[0]
        if step_y != 0:
            edge = rows - 1 if step_y > 0 else 0
            source = jnp.where(row == edge, 0.0, turn(source, -step_y, 0))
            pull = pull + step_y * gain[1]
        if step_z != 0:
            pull = pull + step_z * gain[2]
        total = total + lateral_weights[kind] * source * pull
    used = (lane % tile == 0) & (lane < tile * levels)
    return jnp.sum(jnp.where(used, total, 0.0), axis=1, keepdims=True)


def middle_kernel(counts, levels, *refs):
    x_pairs, y_pairs = counts
    x_got, refs = (refs[:x_pairs][::-1], refs[x_pairs:])
    x_sent, refs = (refs[:x_pairs], refs[x_pairs:])
    own, refs = (refs[0], refs[1:])
    y_out, middle = (refs[:y_pairs], refs[y_pairs])
    rows, lanes = own.shape
    slots = lanes // tile
    lane = lanes_of((rows, lanes))
    main = own[...]
    side = jnp.zeros((rows, lanes), jnp.float32)
    spare = (levels + 1) * tile
    for pairing in range(x_pairs):
        after = partner_after("gx", pairing)
        sign = jnp.where(after, 1.0, -1.0)
        got = present("gx", pairing, x_got[pairing][0:rows, :])
        sent = x_sent[pairing][0:rows, :]
        there = cross_x(levels, sent, got, -sign)
        here = cross_x(levels, got, sent, sign)
        beyond = jnp.where(after, 0, lanes - filter_reach)
        chosen = (lane >= beyond) & (lane < beyond + filter_reach)
        side = side + jnp.where(chosen, turn(got, -spare - filter_reach, 1), 0.0)
        side = side + jnp.where(lane == jnp.where(after, 0, lanes - 1), there, 0.0)
        edge = jnp.where(after, lanes - 1, 0)
        main = main + jnp.where(lane == edge, here, 0.0)
    middle[0] = main
    middle[1] = side
    lane = lanes_of((slots, lanes))
    for pairing in range(y_pairs):
        after = partner_after("gy", pairing)
        out = y_out[pairing]
        ends = jnp.zeros((slots, lanes), jnp.float32)
        if x_pairs:
            base = rows + pairing * slots
            left, right = halves("gx", [got[base : base + slots, :] for got in x_got])
            ends = jnp.where(lane % both_ends < wide, left, right)
        beside = turn(pick(after, side[rows - tile :], side[0:tile]), spare_lanes(lanes), 1)
        used = lane < kinds * both_ends
        out[0:slots, :] = jnp.where(used, ends, 0.0)
        out[0:tile, :] = jnp.where(used[0:tile], ends[0:tile], beside)
        out[slots : slots + tile, :] = pick(after, main[rows - tile :], main[0:tile])


def spare_lanes(lanes):
    assert kinds * both_ends + 2 * filter_reach <= lanes
    return kinds * both_ends + filter_reach


def spread_ends(ends, kind, lanes):
    return turn(ends, -kind * both_ends - wide, 1)


def step_x(main, side, step):
    if step == 0:
        return (main, side)
    lane = lanes_of(main.shape)
    edge = lane == (main.shape[-1] - 1 if step > 0 else 0)
    main, side = (turn(main, -step, 1), turn(side, -step, 1))
    return (jnp.where(edge, side, main), jnp.where(edge, main, side))


def cross_y(faces, gains, sign):
    total_main, total_side = (0.0, 0.0)
    for kind, (lateral_x, lateral_z) in enumerate(laterals):
        main, side = step_x(*faces[kind], lateral_x)
        main, side = (turn(main, -lateral_z, 0), turn(side, -lateral_z, 0))
        pull_main, pull_side = (sign * gains[1][0], sign * gains[1][1])
        if lateral_x != 0:
            pull_main = pull_main + lateral_x * gains[0][0]
            pull_side = pull_side + lateral_x * gains[0][1]
        if lateral_z != 0:
            pull_main = pull_main + lateral_z * gains[2][0]
            pull_side = pull_side + lateral_z * gains[2][1]
        total_main = total_main + lateral_weights[kind] * main * pull_main
        total_side = total_side + lateral_weights[kind] * side * pull_side
    return (
        jnp.sum(total_main, axis=0, keepdims=True),
        jnp.sum(total_side, axis=0, keepdims=True),
    )


def face_lines(lines, ends, slots, lanes):
    return [
        (lines[kind * slots : (kind + 1) * slots], spread_ends(ends[0:slots], kind, lanes))
        for kind in range(kinds)
    ]


def extend_kernel(y_pairs, *refs):
    y_got, refs = (refs[:y_pairs], refs[y_pairs:])
    y_sent, refs = (refs[:y_pairs], refs[y_pairs:])
    ends_got, refs = (refs[:y_pairs], refs[y_pairs:])
    ends_sent, refs = (refs[:y_pairs], refs[y_pairs:])
    middle, norm, out = refs
    rows, lanes = middle.shape[1:]
    slots = lanes // tile
    row, row_tile = (rows_of((rows, lanes)), rows_of((tile, lanes)))
    own = [middle[0], middle[1]]
    before = [jnp.zeros((tile, lanes), jnp.float32) for part in range(2)]
    after = [jnp.zeros((tile, lanes), jnp.float32) for part in range(2)]
    for pairing in range(y_pairs):
        flag = partner_after("gy", pairing)
        sign = jnp.where(flag, 1.0, -1.0)
        got_lines = present("gy", pairing, y_got[pairing][...])
        got_ends = present("gy", pairing, ends_got[pairing][...])
        got = face_lines(got_lines, got_ends, slots, lanes)
        sent = face_lines(y_sent[pairing][...], ends_sent[pairing][...], slots, lanes)
        there = cross_y(sent[:5], got[5:], -sign)
        here = cross_y(got[:5], sent[5:], sign)
        edge_here = jnp.where(flag, rows - 1, 0)
        edge_there = jnp.where(flag, 0, tile - 1)
        for part in range(2):
            sums = got_ends[slots : slots + tile]
            if part == 1:
                sums = turn(got_ends[0:tile], -spare_lanes(lanes), 1)
            sums = sums + jnp.where(row_tile == edge_there, there[part], 0.0)
            none = jnp.zeros_like(sums)
            before[part] = before[part] + pick(flag, none, sums)
            after[part] = after[part] + pick(flag, sums, none)
            own[part] = own[part] + jnp.where(row == edge_here, here[part], 0.0)
    main, side = (
        jnp.concatenate([before[part], own[part], after[part]], axis=0) for part in range(2)
    )
    out[...] = cone_sum(main, side, rows) * norm[...]


def cone_sum(main, side, rows):
    lanes = main.shape[-1]
    lane = lanes_of(main.shape)
    pairs = [main]
    for offset in range(1, filter_reach + 1):
        up = jnp.where(lane < lanes - offset, turn(main, -offset, 1), turn(side, -offset, 1))
        down = jnp.where(lane >= offset, turn(main, offset, 1), turn(side, offset, 1))
        pairs.append(up + down)
    total = jnp.zeros((rows, lanes), jnp.float32)
    for offset in range(filter_reach + 1):
        weighted = jnp.zeros_like(main)
        for distance, pair in enumerate(pairs):
            weight = cone(offset, distance)
            if weight > 0.0:
                weighted = weighted + weight * pair
        for step in sorted({offset, -offset}):
            total = total + turn(weighted, -step, 0)[tile : tile + rows]
    return total


def filter_kernel(mine, other, out):
    out[...] = mine[...] + other[...]


def filter_norm(rows, lanes):
    shape = (rows + 2 * tile, lanes)
    row, lane = (rows_of(shape), lanes_of(shape))
    place = lax.axis_index("gy") * rows + row - tile
    inside = jnp.where((place >= 0) & (place < lax.axis_size("gy") * rows), 1.0, 0.0)
    left = (lax.axis_index("gx") > 0).astype(jnp.float32)
    right = (lax.axis_index("gx") < lax.axis_size("gx") - 1).astype(jnp.float32)
    beside = inside * jnp.where(lane < lanes // 2, right, left)
    return 1.0 / cone_sum(inside, beside, rows)


def collide_kernel(counts, adjoint, design, solid, port, *refs):
    x_pairs, y_pairs, z_pairs = counts
    x_got, refs = (refs[:x_pairs][::-1], refs[x_pairs:])
    z_got, refs = (refs[:z_pairs], refs[z_pairs:])
    far, edge_rows, norm, out, sems = refs
    levels, rows, lanes = adjoint.shape[1:]
    slots = lanes // tile
    halo_z = halves("depth", [got[...] for got in z_got])
    halo_x = halves("gx", [got[0:rows, :] for got in x_got])
    damping = damp_top * (1.0 - design[...]) / (1.0 + design[...])
    rate = 3.0 * (relax_rate - damping)
    lane = lanes_of((rows, lanes))
    copies = []
    for level in range(levels):
        pulled = []
        for number, (step_x_, step_y_, step_z_) in enumerate(velocities):
            source = level + step_z_
            if z_pairs or 0 <= source < levels:
                plane = depth_plane(adjoint, halo_z, number, source)
            else:
                plane = jnp.zeros((rows, lanes), jnp.float32)
            if step_x_ != 0:
                edge = lanes - 1 if step_x_ > 0 else 0
                column = 0.0
                if x_pairs:
                    kind = crossing(0, step_x_).index(number)
                    place = (source % slots) * tile + spot(kind)
                    column = turn(halo_x[1 if step_x_ > 0 else 0], edge - place, 1)
                plane = jnp.where(lane == edge, column, turn(plane, -step_x_, 1))
            if step_y_ != 0:
                plane = along_y(plane, step_y_)
            pulled.append(plane)
        zeroth, moment = sums_of(pulled)
        base = relax_rate * zeroth
        scaled = [rate * part for part in moment]
        fluid, inlet = (solid[level] == 0, port[level] == 1)
        outflow = jnp.where(port[level] == 2, 1.0, 0.0)
        for number, vector in enumerate(velocities):
            updated = base + (1.0 - relax_rate) * pulled[number]
            if number > 0:
                updated = updated + along(vector, scaled)
            updated = jnp.where(fluid, updated, pulled[opposite[number]])
            updated = jnp.where(inlet, 0.0, updated)
            if vector[0] != 0:
                updated = updated + vector[0] * outflow
            out[number, level] = updated
        for place, (low, high) in enumerate(groups_of(levels)):
            if level == high - 1:
                copy = pltpu.make_async_copy(
                    out.at[:, low:high], far.at[:, low:high], sems.at[place]
                )
                copy.start()
                copies.append(copy)
    for pairing in range(y_pairs):
        after = partner_after("gy", pairing)
        for number in range(len(velocities)):
            edge_rows[pairing, number] = pick(after, out[number, :, rows - 1, :], out[number, :, 0, :])
    norm[...] = filter_norm(rows, lanes)
    for copy in copies:
        copy.wait()


def along(vector, parts):
    total = 0.0
    for component, part in zip(vector, parts):
        if component > 0:
            total = total + part
        if component < 0:
            total = total - part
    return total


def sums_of(pulled):
    heavy, light = (lattice_weights[1], lattice_weights[7])
    both, gap = ({}, {})
    for number in range(1, len(velocities), 2):
        both[number] = pulled[number] + pulled[number + 1]
        gap[number] = pulled[number] - pulled[number + 1]
    zeroth = lattice_weights[0] * pulled[0] + heavy * ((both[1] + both[3]) + both[5])
    zeroth = zeroth + light * (((both[7] + both[9]) + (both[11] + both[13])) + (both[15] + both[17]))
    moment = (
        heavy * gap[1] + light * ((gap[7] + gap[9]) + (gap[11] + gap[13])),
        heavy * gap[3] + light * ((gap[7] - gap[9]) + (gap[15] + gap[17])),
        heavy * gap[5] + light * ((gap[11] - gap[13]) + (gap[15] - gap[17])),
    )
    return (zeroth, moment)


def row_kernel(y_pairs, new, edge_rows, design, solid, port, *refs):
    y_got, refs = (refs[:y_pairs], refs[y_pairs:])
    ends_got, (far, out, sems) = (refs[:y_pairs], refs[y_pairs:])
    levels, rows, lanes = solid.shape
    slots = lanes // tile
    copies = []
    for pairing in range(y_pairs):
        after = partner_after("gy", pairing)
        sign = jnp.where(after, 1.0, -1.0)
        got = present("gy", pairing, y_got[pairing][...])
        ends = present("gy", pairing, ends_got[pairing][0:slots, :])
        extra, moment = ({}, [0.0, 0.0, 0.0])
        zeroth = 0.0
        for kind, (lateral_x, lateral_z) in enumerate(laterals):
            line = got[kind * slots : (kind + 1) * slots]
            if lateral_x != 0:
                line = step_x(line, spread_ends(ends, kind, lanes), lateral_x)[0]
            line = turn(line, -lateral_z, 0)[0:levels]
            none = jnp.zeros_like(line)
            extra[crossing(1, 1)[kind]] = pick(after, line, none)
            extra[crossing(1, -1)[kind]] = pick(after, none, line)
            weighted = lateral_weights[kind] * line
            zeroth = zeroth + weighted
            moment[0] = moment[0] + lateral_x * weighted
            moment[2] = moment[2] + lateral_z * weighted
        moment[1] = sign * zeroth
        edge_design = pick(after, design[rows - 1 : rows, :], design[0:1, :])
        damping = damp_top * (1.0 - edge_design) / (1.0 + edge_design)
        rate = 3.0 * (relax_rate - damping)
        fluid = pick(after, solid[:, rows - 1, :], solid[:, 0, :]) == 0
        inlet = pick(after, port[:, rows - 1, :], port[:, 0, :]) == 1
        scaled = [rate * part for part in moment]
        base = relax_rate * zeroth
        for number, vector in enumerate(velocities):
            added = base
            if number > 0:
                added = added + along(vector, scaled)
            if number in extra:
                added = added + (1.0 - relax_rate) * extra[number]
            added = jnp.where(fluid, added, extra.get(opposite[number], 0.0))
            added = jnp.where(inlet, 0.0, added)
            out[pairing, number, :, 0, :] = edge_rows[pairing, number] + added
        place = jnp.where(after, rows - 1, 0)
        copies.append(
            pltpu.make_async_copy(
                out.at[pairing, :, :, 0:1, :], far.at[:, :, pl.ds(place, 1), :], sems.at[pairing]
            )
        )
        copies[-1].start()
    for copy in copies:
        copy.wait()


def local_call(body, name, operands, out_shapes, scratch=(), far=(), far_out=(), aliases=None, room=16, cost=None):
    near_spec = pl.BlockSpec(memory_space=pltpu.VMEM)
    far_spec = pl.BlockSpec(memory_space=pltpu.HBM)
    shapes = [
        jax.ShapeDtypeStruct(shape, jnp.float32) if isinstance(shape, tuple) else shape
        for shape in out_shapes
    ]
    return pl.pallas_call(
        body,
        out_shape=shapes,
        in_specs=[far_spec if place in far else near_spec for place in range(len(operands))],
        out_specs=[far_spec if place in far_out else near_spec for place in range(len(shapes))],
        scratch_shapes=list(scratch),
        input_output_aliases=aliases or {},
        compiler_params=pltpu.CompilerParams(vmem_limit_bytes=room * 1024 * 1024),
        name=name,
        cost_estimate=cost,
    )(*operands)


def on_device(adjoint, momentum, design, solid_mask, port_label):
    levels, rows, lanes = adjoint.shape[1:]
    slots = lanes // tile
    groups = len(groups_of(levels))
    x_pairs, y_pairs, z_pairs = (len(pairings(axis)) for axis in ("gx", "gy", "depth"))
    z_got = []
    if z_pairs:
        faces = local_call(
            functools.partial(face_kernel, z_pairs),
            "depth_faces",
            [pltpu.with_memory_space_constraint(adjoint, pltpu.HBM)],
            [pltpu.VMEM((len(laterals), rows, lanes), jnp.float32)] * z_pairs,
            scratch=[pltpu.SemaphoreType.DMA((z_pairs * len(laterals),))],
            far=(0,),
            cost=pl.CostEstimate(flops=2000 * math.prod(adjoint.shape), bytes_accessed=100000, transcendentals=0),
        )
        z_got = [swap(face, "depth", pairing) for pairing, face in enumerate(faces)]
    packed = local_call(
        functools.partial(pack_kernel, (x_pairs, y_pairs)),
        "pack_faces",
        [adjoint, momentum, design, solid_mask, port_label],
        [(rows, lanes)] * x_pairs
        + [(kinds * slots, lanes)] * y_pairs
        + [(rows, lanes), (2, 3, rows, lanes)],
    )
    filled = local_call(
        functools.partial(depth_kernel, (x_pairs, y_pairs, z_pairs), levels),
        "add_z_faces",
        [*z_got, *packed],
        [(rows + y_pairs * slots, lanes)] * x_pairs
        + [(kinds * slots, lanes)] * y_pairs
        + [(rows, lanes)],
    )
    x_sent, y_sent, own = (
        filled[:x_pairs],
        filled[x_pairs : x_pairs + y_pairs],
        filled[x_pairs + y_pairs],
    )
    y_got = [swap(y_sent[pairing], "gy", pairing) for pairing in range(y_pairs)]
    x_got = [None] * x_pairs
    for pairing in reversed(range(x_pairs)):
        x_got[pairing] = swap(x_sent[pairing], "gx", pairing)
    merged = local_call(
        functools.partial(middle_kernel, (x_pairs, y_pairs), levels),
        "add_x_faces",
        [*x_got[::-1], *x_sent, own],
        [(slots + tile, lanes)] * y_pairs + [(2, rows, lanes)],
    )
    ends_sent, middle = (merged[:y_pairs], merged[y_pairs])
    ends_got = [swap(ends_sent[pairing], "gy", pairing) for pairing in range(y_pairs)]
    new_adjoint, edge_rows, norm = local_call(
        functools.partial(collide_kernel, (x_pairs, y_pairs, z_pairs)),
        "collide",
        [adjoint, design, solid_mask, port_label, *x_got[::-1], *z_got],
        [adjoint.shape, (max(y_pairs, 1), len(velocities), levels, lanes), (rows, lanes)],
        scratch=[pltpu.VMEM(adjoint.shape, jnp.float32), pltpu.SemaphoreType.DMA((groups,))],
        far_out=(0,),
        cost=pl.CostEstimate(
            flops=8000 * math.prod(adjoint.shape), bytes_accessed=4000000, transcendentals=0
        ),
    )
    (column,) = local_call(
        functools.partial(extend_kernel, y_pairs),
        "add_y_faces",
        [*y_got, *y_sent, *ends_got, *ends_sent, middle, norm],
        [(rows, lanes)],
    )
    if z_pairs == 1:
        other = swap(column, "depth", 0)
    else:
        other = lax.psum(column, "depth") - column
    if y_pairs:
        (new_adjoint,) = local_call(
            functools.partial(row_kernel, y_pairs),
            "add_y_rows",
            [new_adjoint, edge_rows, design, solid_mask, port_label, *y_got, *ends_got],
            [adjoint.shape],
            scratch=[
                pltpu.VMEM((y_pairs, len(velocities), levels, tile, lanes), jnp.float32),
                pltpu.SemaphoreType.DMA((y_pairs,)),
            ],
            far=(0,),
            far_out=(0,),
            aliases={0: 0},
        )
    (sensitivity,) = local_call(
        filter_kernel, "add_depth", [column, other], [(rows, lanes)]
    )
    return (new_adjoint, sensitivity)


def solution(mesh):
    in_specs = (
        P(None, "depth", "gy", "gx"),
        P(None, "depth", "gy", "gx"),
        P("gy", "gx"),
        P("depth", "gy", "gx"),
        P("depth", "gy", "gx"),
    )
    out_specs = (P(None, "depth", "gy", "gx"), P("gy", "gx"))
    return jax.shard_map(
        on_device, mesh=mesh, in_specs=in_specs, out_specs=out_specs, check_vma=False
    )
```

```python
import functools
import math

import jax
import jax.numpy as jnp
from jax import lax
from jax.experimental import pallas as pl
from jax.experimental.pallas import tpu as pltpu
from jax.sharding import PartitionSpec as P

velocities = (
    (0, 0, 0),
    (1, 0, 0),
    (-1, 0, 0),
    (0, 1, 0),
    (0, -1, 0),
    (0, 0, 1),
    (0, 0, -1),
    (1, 1, 0),
    (-1, -1, 0),
    (1, -1, 0),
    (-1, 1, 0),
    (1, 0, 1),
    (-1, 0, -1),
    (1, 0, -1),
    (-1, 0, 1),
    (0, 1, 1),
    (0, -1, -1),
    (0, 1, -1),
    (0, -1, 1),
)
lattice_weights = (1.0 / 3.0,) + (1.0 / 18.0,) * 6 + (1.0 / 36.0,) * 12
opposite = (0, 2, 1, 4, 3, 6, 5, 8, 7, 10, 9, 12, 11, 14, 13, 16, 15, 18, 17)
relax_rate = 1.25
damp_top = 0.5
cone_radius = 5.0
filter_reach = 4
wide = filter_reach + 1
tile = 8
level_group = 3
laterals = ((0, 0), (1, 0), (-1, 0), (0, 1), (0, -1))
lateral_weights = (1.0 / 18.0,) + (1.0 / 36.0,) * 4
kinds = len(laterals) + 3
both_ends = 2 * wide


def spot(kind):
    return 2 * kind + 1 if kind < kinds // 2 else 2 * kind - kinds


def crossing(axis, sign):
    others = [other for other in range(3) if other != axis]
    return [
        next(
            number
            for number, vector in enumerate(velocities)
            if vector[axis] == sign and (vector[others[0]], vector[others[1]]) == lateral
        )
        for lateral in laterals
    ]


def cone(offset_y, offset_x):
    return max(0.0, cone_radius - math.sqrt(offset_y * offset_y + offset_x * offset_x))


def pairings(axis):
    return range(min(lax.axis_size(axis) - 1, 2))


def swap(array, axis, pairing):
    size, cores = (lax.axis_size(axis), lax.axis_size("depth"))
    pairs = []
    for low in range(pairing, size - 1, 2):
        pairs += [(low, low + 1), (low + 1, low)]
    alone = [place for place in range(size) if place not in dict(pairs)]
    if axis == "depth" or cores % 2 != 0 or not alone:
        return lax.ppermute(array, axis, pairs)
    full = [(a * cores + core, b * cores + core) for a, b in pairs for core in range(cores)]
    for place in alone:
        full += [(place * cores + core, place * cores + (core ^ 1)) for core in range(cores)]
    return lax.ppermute(array, (axis, "depth"), full)


def partner_after(axis, pairing):
    return lax.rem(lax.axis_index(axis) + pairing, 2) == 0


def partners(axis, pairing):
    place, after = (lax.axis_index(axis), partner_after(axis, pairing))
    none_before, none_after = (place == 0, place == lax.axis_size(axis) - 1)
    return (
        jnp.logical_not(jnp.logical_or(after, none_before)),
        jnp.logical_and(after, jnp.logical_not(none_after)),
    )


def present(axis, pairing, array):
    before, after = partners(axis, pairing)
    return pick(jnp.logical_or(before, after), array, jnp.zeros_like(array))


def pick(flag, yes, no):
    return lax.select(flag, yes, no)


def turn(array, shift, axis):
    shift = shift % array.shape[axis]
    return array if shift == 0 else pltpu.roll(array, shift, axis)


def lanes_of(shape):
    return lax.broadcasted_iota(jnp.int32, shape, len(shape) - 1)


def rows_of(shape):
    return lax.broadcasted_iota(jnp.int32, shape, len(shape) - 2)


def halves(axis, arrays):
    before, after = 0.0, 0.0
    for pairing, array in enumerate(arrays):
        is_before, is_after = partners(axis, pairing)
        none = jnp.zeros_like(array)
        before = before + pick(is_before, array, none)
        after = after + pick(is_after, array, none)
    return (before, after)


def depth_plane(adjoint, halo, number, level):
    levels = adjoint.shape[1]
    if 0 <= level < levels:
        return adjoint[number, level]
    sign = 1 if level == levels else -1
    side = halo[1] if sign > 0 else halo[0]
    return side[crossing(2, sign).index(number)]


def gain_of(momentum, scale, solid, port, level):
    kept = (solid[level] == 0) & (port[level] != 1)
    factor = jnp.where(kept, scale, 0.0)
    return [factor * momentum[part, level] for part in range(3)]


def along_x(plane, step):
    lane = lanes_of(plane.shape)
    edge = plane.shape[-1] - 1 if step > 0 else 0
    return jnp.where(lane == edge, 0.0, turn(plane, -step, 1))


def along_y(plane, step):
    row = rows_of(plane.shape)
    edge = plane.shape[-2] - 1 if step > 0 else 0
    return jnp.where(row == edge, 0.0, turn(plane, -step, 0))


def own_moment(take):
    heavy, light = (1.0 / 18.0, 1.0 / 36.0)
    p = {
        number: take(number, vector[2]) for number, vector in enumerate(velocities) if number != 0
    }
    for number in (7, 8, 9, 10):
        p[number] = along_y(p[number], velocities[number][1])
    right_x = along_x(heavy * p[1] + light * ((p[7] + p[9]) + (p[11] + p[13])), 1)
    left_x = along_x(heavy * p[2] + light * ((p[8] + p[10]) + (p[12] + p[14])), -1)
    right_y = along_x(light * (p[7] - p[9]), 1)
    left_y = along_x(light * (p[10] - p[8]), -1)
    right_z = along_x(light * (p[11] - p[13]), 1)
    left_z = along_x(light * (p[14] - p[12]), -1)
    lower_y = along_y(heavy * p[3] + light * (p[15] + p[17]), 1)
    upper_y = along_y(heavy * p[4] + light * (p[16] + p[18]), -1)
    lower_z = along_y(light * (p[15] - p[17]), 1)
    upper_z = along_y(light * (p[18] - p[16]), -1)
    moment_x = right_x - left_x
    moment_y = (lower_y - upper_y) + (right_y + left_y)
    moment_z = heavy * (p[5] - p[6]) + ((right_z + left_z) + (lower_z + upper_z))
    return (moment_x, moment_y, moment_z)


def groups_of(levels):
    return [(low, min(low + level_group, levels)) for low in range(0, levels, level_group)]


def run_all(copies):
    for copy in copies:
        copy.start()
    for copy in copies:
        copy.wait()


def face_kernel(z_pairs, adjoint, *refs):
    outs, sems = (refs[:z_pairs], refs[z_pairs])
    copies = []
    for pairing in range(z_pairs):
        after = partner_after("depth", pairing)
        level = jnp.where(after, adjoint.shape[1] - 1, 0)
        for kind, numbers in enumerate(zip(crossing(2, -1), crossing(2, 1))):
            number = jnp.where(after, numbers[0], numbers[1])
            source, target = (adjoint.at[number, level], outs[pairing].at[kind])
            copies.append(pltpu.make_async_copy(source, target, sems.at[len(copies)]))
    run_all(copies)


def pack_kernel(counts, adjoint, momentum, design, solid, port, *refs):
    x_pairs, y_pairs = counts
    x_out, refs = (refs[:x_pairs], refs[x_pairs:])
    y_out, refs = (refs[:y_pairs], refs[y_pairs:])
    own_out, edge_gain = refs
    levels, rows, lanes = adjoint.shape[1:]
    slots = lanes // tile
    assert levels + 3 <= slots
    scale = 6.0 * damp_top / ((1.0 + design[...]) * (1.0 + design[...]))
    lane = lanes_of((rows, lanes))
    for pairing in range(y_pairs):
        y_out[pairing][...] = jnp.zeros(y_out[pairing].shape, jnp.float32)
    total = jnp.zeros((rows, lanes), jnp.float32)
    joint = [jnp.zeros((rows, lanes), jnp.float32) for half in range(2)]
    for level in range(levels):
        gain = gain_of(momentum, scale, solid, port, level)
        moment = own_moment(
            lambda number, step: adjoint[number, level + step]
            if 0 <= level + step < levels
            else jnp.zeros((rows, lanes), jnp.float32)
        )
        total = total + (gain[0] * moment[0] + gain[1] * moment[1] + gain[2] * moment[2])
        for side, edge in enumerate((0, levels - 1)):
            if level == edge:
                for part in range(3):
                    edge_gain[side, part] = gain[part]
        for pairing in range(y_pairs):
            after = partner_after("gy", pairing)
            for part in range(3):
                place = (len(laterals) + part) * slots + level
                y_out[pairing][place : place + 1, :] = pick(
                    after, gain[part][rows - 1 : rows], gain[part][0:1]
                )
        for kind in range(kinds):
            if kind < len(laterals):
                first = adjoint[crossing(0, 1)[kind], level]
                last = adjoint[crossing(0, -1)[kind], level]
                plane = jnp.where(lane == lanes - 1, last, first)
            else:
                plane = gain[kind - len(laterals)]
            half, place = (kind // (kinds // 2), level * tile + 2 * (kind % (kinds // 2)))
            chosen = lane // 2 == place // 2
            joint[half] = jnp.where(chosen, turn(plane, place + 1, 1), joint[half])
    for pairing in range(y_pairs):
        after = partner_after("gy", pairing)
        for kind in range(len(laterals)):
            last, first = (crossing(1, -1)[kind], crossing(1, 1)[kind])
            y_out[pairing][kind * slots : kind * slots + levels, :] = pick(
                after, adjoint[last, :, rows - 1, :], adjoint[first, :, 0, :]
            )
    own_out[...] = total
    odd = lane % 2 == 1
    first_pack = jnp.where(odd, joint[0], turn(joint[1], -1, 1))
    last_pack = jnp.where(odd, turn(joint[0], 1, 1), joint[1])
    for pairing in range(x_pairs):
        x_out[pairing][...] = pick(partner_after("gx", pairing), last_pack, first_pack)


def depth_kernel(counts, levels, *refs):
    x_pairs, y_pairs, z_pairs = counts
    z_got, refs = (refs[:z_pairs], refs[z_pairs:])
    x_pack, refs = (refs[:x_pairs], refs[x_pairs:])
    y_pack, refs = (refs[:y_pairs], refs[y_pairs:])
    own, edge_gain, refs = (*refs[:2], refs[2:])
    x_out, refs = (refs[:x_pairs], refs[x_pairs:])
    y_out, own_out = (refs[:y_pairs], refs[y_pairs])
    rows, lanes = own.shape
    slots = lanes // tile
    halo = halves("depth", [got[...] for got in z_got])
    lane = lanes_of((rows, lanes))
    total = own[...]
    if z_pairs:
        for side, sign in enumerate((-1, 1)):
            gain = [edge_gain[side, part] for part in range(3)]
            for kind, (step_x_, step_y_) in enumerate(laterals):
                plane = halo[side][kind]
                pull = sign * gain[2]
                if step_x_ != 0:
                    plane = along_x(plane, step_x_)
                    pull = pull + step_x_ * gain[0]
                if step_y_ != 0:
                    plane = along_y(plane, step_y_)
                    pull = pull + step_y_ * gain[1]
                total = total + lateral_weights[kind] * plane * pull
    own_out[...] = total
    beyond = ((3, levels, 1), (4, -1, 0))
    for pairing in range(y_pairs):
        after = partner_after("gy", pairing)
        y_out[pairing][...] = y_pack[pairing][...]
        if z_pairs:
            for kind, level, side in beyond:
                planes = crossing(2, 1 if side else -1)
                last, first = (
                    halo[side][planes.index(crossing(1, sign)[kind])] for sign in (-1, 1)
                )
                place = kind * slots + level % slots
                y_out[pairing][place : place + 1, :] = pick(
                    after, last[rows - 1 : rows], first[0:1]
                )
    spare = (levels + 1) * tile
    chosen = (lane >= spare) & (lane < spare + 2 * filter_reach)
    sums = jnp.where(chosen, turn(total, spare + filter_reach, 1), 0.0)
    packs = []
    for edge_shift, sign in ((0, 1), (1, -1)):
        pack = sums
        if z_pairs:
            for kind, level, side in beyond:
                planes = crossing(2, 1 if side else -1)
                plane = halo[side][planes.index(crossing(0, sign)[kind])]
                place = (level % slots) * tile + spot(kind)
                pack = jnp.where(lane == place, turn(plane, place + edge_shift, 1), pack)
        packs.append(pack)
    for pairing in range(x_pairs):
        after = partner_after("gx", pairing)
        x_out[pairing][0:rows, :] = x_pack[pairing][...] + pick(after, packs[1], packs[0])
    lane = lanes_of((slots, lanes))
    for y_pairing in range(y_pairs):
        ends = jnp.zeros((slots, lanes), jnp.float32)
        for kind in range(kinds):
            line = y_out[y_pairing][kind * slots : (kind + 1) * slots, :]
            place = kind * both_ends
            chosen = (lane >= place) & (lane < place + both_ends)
            ends = jnp.where(chosen, turn(line, place + wide, 1), ends)
        for pairing in range(x_pairs):
            base = rows + y_pairing * slots
            x_out[pairing][base : base + slots, :] = ends


def cross_x(levels, faces, gains, sign):
    rows = faces.shape[0]
    lane, row = (lanes_of(faces.shape), rows_of(faces.shape))
    gain = [turn(gains, -spot(len(laterals) + part), 1) for part in range(3)]
    terms = []
    for kind, (step_y, step_z) in enumerate(laterals):
        source = turn(faces, -spot(kind) - tile * step_z, 1)
        pull = sign * gain[0]
        if step_y != 0:
            edge = rows - 1 if step_y > 0 else 0
            source = jnp.where(row == edge, 0.0, turn(source, -step_y, 0))
            pull = pull + step_y * gain[1]
        if step_z != 0:
            pull = pull + step_z * gain[2]
        terms.append(lateral_weights[kind] * source * pull)
    used = (lane % tile == 0) & (lane < tile * levels)
    return jnp.sum(jnp.where(used, tree_sum(terms), 0.0), axis=1, keepdims=True)


def middle_kernel(counts, levels, *refs):
    x_pairs, y_pairs = counts
    x_got, refs = (refs[:x_pairs][::-1], refs[x_pairs:])
    x_sent, refs = (refs[:x_pairs], refs[x_pairs:])
    own, refs = (refs[0], refs[1:])
    y_out, middle = (refs[:y_pairs], refs[y_pairs])
    rows, lanes = own.shape
    slots = lanes // tile
    lane = lanes_of((rows, lanes))
    main = own[...]
    side, beside = (jnp.zeros((rows, lanes), jnp.float32) for part in range(2))
    free = spare_lanes(lanes)
    spare = (levels + 1) * tile
    got_left, got_right = halves("gx", [got[0:rows, :] for got in x_got])
    sent_left, sent_right = halves("gx", [sent[0:rows, :] for sent in x_sent])
    if x_pairs:
        there_left = cross_x(levels, sent_left, got_left, 1)
        there_right = cross_x(levels, sent_right, got_right, -1)
        here_left = cross_x(levels, got_left, sent_left, -1)
        here_right = cross_x(levels, got_right, sent_right, 1)
        main = main + jnp.where(lane == 0, here_left, 0.0)
        main = main + jnp.where(lane == lanes - 1, here_right, 0.0)
        sums = jnp.where(lane // filter_reach == spare // filter_reach, got_left, got_right)
        side = jnp.where(lane == 0, there_right, jnp.where(lane == lanes - 1, there_left, 0.0))
        chosen = (lane < filter_reach) | (lane >= lanes - filter_reach)
        side = side + jnp.where(chosen, turn(sums, -spare - filter_reach, 1), 0.0)
        beside = jnp.where(lane == free, there_right, 0.0)
        beside = beside + jnp.where(lane == free - 1, there_left, 0.0)
        chosen = (lane >= free - filter_reach) & (lane < free + filter_reach)
        beside = beside + jnp.where(chosen, turn(sums, free - spare - filter_reach, 1), 0.0)
    middle[0] = main
    middle[1] = side
    lane = lanes_of((slots, lanes))
    for pairing in range(y_pairs):
        after = partner_after("gy", pairing)
        out = y_out[pairing]
        ends = jnp.zeros((slots, lanes), jnp.float32)
        if x_pairs:
            base = rows + pairing * slots
            left, right = halves("gx", [got[base : base + slots, :] for got in x_got])
            ends = jnp.where(lane % both_ends < wide, left, right)
        ends = jnp.where(lane < kinds * both_ends, ends, 0.0)
        out[0:tile, :] = ends[0:tile] + pick(after, beside[rows - tile :], beside[0:tile])
        out[tile:slots, :] = ends[tile:]
        out[slots : slots + tile, :] = pick(after, main[rows - tile :], main[0:tile])


def spare_lanes(lanes):
    assert kinds * both_ends + 2 * tile <= lanes and lanes & (lanes - 1) == 0
    return kinds * both_ends + tile


def step_x(line, ends, kind, step):
    lanes = line.shape[-1]
    main = turn(line, -step, 1)
    side = turn(ends, -kind * both_ends - wide - step, 1)
    if step == 0:
        return (main, side)
    edge = lanes_of(line.shape) == (lanes - 1 if step > 0 else 0)
    return (jnp.where(edge, side, main), jnp.where(edge, main, side))


def cross_y(faces, gains, sign):
    (lines, ends), (gain_lines, gain_ends) = (faces, gains)
    gain = [
        step_x(gain_lines[len(laterals) + part], gain_ends, len(laterals) + part, 0)
        for part in range(3)
    ]
    total_main, total_side = (0.0, 0.0)
    for kind, (lateral_x, lateral_z) in enumerate(laterals):
        main, side = step_x(lines[kind], ends, kind, lateral_x)
        main, side = (turn(main, -lateral_z, 0), turn(side, -lateral_z, 0))
        pull_main, pull_side = (sign * gain[1][0], sign * gain[1][1])
        if lateral_x != 0:
            pull_main = pull_main + lateral_x * gain[0][0]
            pull_side = pull_side + lateral_x * gain[0][1]
        if lateral_z != 0:
            pull_main = pull_main + lateral_z * gain[2][0]
            pull_side = pull_side + lateral_z * gain[2][1]
        total_main = total_main + lateral_weights[kind] * main * pull_main
        total_side = total_side + lateral_weights[kind] * side * pull_side
    return (
        jnp.sum(total_main, axis=0, keepdims=True),
        jnp.sum(total_side, axis=0, keepdims=True),
    )


def face_lines(lines, ends, slots):
    return (
        [lines[kind * slots : (kind + 1) * slots] for kind in range(kinds)],
        ends[0:slots],
    )


def extend_kernel(y_pairs, *refs):
    y_got, refs = (refs[:y_pairs], refs[y_pairs:])
    y_sent, refs = (refs[:y_pairs], refs[y_pairs:])
    ends_got, refs = (refs[:y_pairs], refs[y_pairs:])
    ends_sent, refs = (refs[:y_pairs], refs[y_pairs:])
    middle, norm, out = refs
    rows, lanes = middle.shape[1:]
    slots = lanes // tile
    row, row_tile = (rows_of((rows, lanes)), rows_of((tile, lanes)))
    own = [middle[0], middle[1]]
    before = [jnp.zeros((tile, lanes), jnp.float32) for part in range(2)]
    after = [jnp.zeros((tile, lanes), jnp.float32) for part in range(2)]
    for pairing in range(y_pairs):
        flag = partner_after("gy", pairing)
        sign = jnp.where(flag, 1.0, -1.0)
        got_lines = present("gy", pairing, y_got[pairing][...])
        got_ends = present("gy", pairing, ends_got[pairing][...])
        got = face_lines(got_lines, got_ends, slots)
        sent = face_lines(y_sent[pairing][...], ends_sent[pairing][...], slots)
        there = cross_y(sent, got, -sign)
        here = cross_y(got, sent, sign)
        edge_here = jnp.where(flag, rows - 1, 0)
        edge_there = jnp.where(flag, 0, tile - 1)
        for part in range(2):
            sums = got_ends[slots : slots + tile]
            if part == 1:
                sums = turn(got_ends[0:tile], -spare_lanes(lanes), 1)
            sums = sums + jnp.where(row_tile == edge_there, there[part], 0.0)
            none = jnp.zeros_like(sums)
            before[part] = before[part] + pick(flag, none, sums)
            after[part] = after[part] + pick(flag, sums, none)
            own[part] = own[part] + jnp.where(row == edge_here, here[part], 0.0)
    main, side = (
        jnp.concatenate([before[part], own[part], after[part]], axis=0) for part in range(2)
    )
    out[...] = cone_sum(main, side, rows) * norm[...]


def cone_sum(main, side, rows):
    lanes = main.shape[-1]
    lane = lanes_of(main.shape)
    pairs = [main]
    for offset in range(1, filter_reach + 1):
        up = jnp.where(lane < lanes - offset, turn(main, -offset, 1), turn(side, -offset, 1))
        down = jnp.where(lane >= offset, turn(main, offset, 1), turn(side, offset, 1))
        pairs.append(up + down)
    terms = []
    for offset in range(filter_reach + 1):
        weights = [cone(offset, distance) for distance in range(filter_reach + 1)]
        weighted = tree_sum([weight * pair for weight, pair in zip(weights, pairs) if weight > 0.0])
        for step in sorted({offset, -offset}):
            terms.append(turn(weighted, -step, 0)[tile : tile + rows])
    return tree_sum(terms)


def tree_sum(terms):
    while len(terms) > 1:
        terms = [sum(terms[place + 1 : place + 2], terms[place]) for place in range(0, len(terms), 2)]
    return terms[0]


def filter_kernel(mine, other, out):
    out[...] = mine[...] + other[...]


def filter_norm(rows, lanes):
    shape = (rows + 2 * tile, lanes)
    row, lane = (rows_of(shape), lanes_of(shape))
    place = lax.axis_index("gy") * rows + row - tile
    inside = jnp.where((place >= 0) & (place < lax.axis_size("gy") * rows), 1.0, 0.0)
    left = (lax.axis_index("gx") > 0).astype(jnp.float32)
    right = (lax.axis_index("gx") < lax.axis_size("gx") - 1).astype(jnp.float32)
    beside = inside * jnp.where(lane < lanes // 2, right, left)
    return 1.0 / cone_sum(inside, beside, rows)


def collide_kernel(counts, adjoint, design, solid, port, *refs):
    x_pairs, y_pairs, z_pairs = counts
    x_got, refs = (refs[:x_pairs][::-1], refs[x_pairs:])
    z_got, refs = (refs[:z_pairs], refs[z_pairs:])
    far, edge_rows, norm, out, sems = refs
    levels, rows, lanes = adjoint.shape[1:]
    slots = lanes // tile
    halo_z = halves("depth", [got[...] for got in z_got])
    halo_x = halves("gx", [got[0:rows, :] for got in x_got])
    damping = damp_top * (1.0 - design[...]) / (1.0 + design[...])
    rate = 3.0 * (relax_rate - damping)
    lane = lanes_of((rows, lanes))
    copies = []
    for level in range(levels):
        pulled = []
        for number, (step_x_, step_y_, step_z_) in enumerate(velocities):
            source = level + step_z_
            if z_pairs or 0 <= source < levels:
                plane = depth_plane(adjoint, halo_z, number, source)
            else:
                plane = jnp.zeros((rows, lanes), jnp.float32)
            if step_x_ != 0:
                edge = lanes - 1 if step_x_ > 0 else 0
                column = 0.0
                if x_pairs:
                    kind = crossing(0, step_x_).index(number)
                    place = (source % slots) * tile + spot(kind)
                    column = turn(halo_x[1 if step_x_ > 0 else 0], edge - place, 1)
                plane = jnp.where(lane == edge, column, turn(plane, -step_x_, 1))
            if step_y_ != 0:
                plane = along_y(plane, step_y_)
            pulled.append(plane)
        zeroth, moment = sums_of(pulled)
        base = relax_rate * zeroth
        scaled = [rate * part for part in moment]
        fluid, inlet = (solid[level] == 0, port[level] == 1)
        outflow = jnp.where(port[level] == 2, 1.0, 0.0)
        for number, vector in enumerate(velocities):
            updated = base + (1.0 - relax_rate) * pulled[number]
            if number > 0:
                updated = updated + along(vector, scaled)
            updated = jnp.where(fluid, updated, pulled[opposite[number]])
            updated = jnp.where(inlet, 0.0, updated)
            if vector[0] != 0:
                updated = updated + vector[0] * outflow
            out[number, level] = updated
        for place, (low, high) in enumerate(groups_of(levels)):
            if level == high - 1:
                copy = pltpu.make_async_copy(
                    out.at[:, low:high], far.at[:, low:high], sems.at[place]
                )
                copy.start()
                copies.append(copy)
    for pairing in range(y_pairs):
        after = partner_after("gy", pairing)
        for number in range(len(velocities)):
            edge_rows[pairing, number] = pick(after, out[number, :, rows - 1, :], out[number, :, 0, :])
    norm[...] = filter_norm(rows, lanes)
    for copy in copies:
        copy.wait()


def along(vector, parts):
    total = 0.0
    for component, part in zip(vector, parts):
        if component > 0:
            total = total + part
        if component < 0:
            total = total - part
    return total


def sums_of(pulled):
    heavy, light = (lattice_weights[1], lattice_weights[7])
    both, gap = ({}, {})
    for number in range(1, len(velocities), 2):
        both[number] = pulled[number] + pulled[number + 1]
        gap[number] = pulled[number] - pulled[number + 1]
    zeroth = lattice_weights[0] * pulled[0] + heavy * ((both[1] + both[3]) + both[5])
    zeroth = zeroth + light * (((both[7] + both[9]) + (both[11] + both[13])) + (both[15] + both[17]))
    moment = (
        heavy * gap[1] + light * ((gap[7] + gap[9]) + (gap[11] + gap[13])),
        heavy * gap[3] + light * ((gap[7] - gap[9]) + (gap[15] + gap[17])),
        heavy * gap[5] + light * ((gap[11] - gap[13]) + (gap[15] - gap[17])),
    )
    return (zeroth, moment)


def row_kernel(y_pairs, new, edge_rows, design, solid, port, *refs):
    y_got, refs = (refs[:y_pairs], refs[y_pairs:])
    ends_got, (far, out, sems) = (refs[:y_pairs], refs[y_pairs:])
    levels, rows, lanes = solid.shape
    slots = lanes // tile
    copies = []
    for pairing in range(y_pairs):
        after = partner_after("gy", pairing)
        sign = jnp.where(after, 1.0, -1.0)
        got = present("gy", pairing, y_got[pairing][...])
        ends = present("gy", pairing, ends_got[pairing][0:slots, :])
        extra, moment = ({}, [0.0, 0.0, 0.0])
        zeroth = 0.0
        for kind, (lateral_x, lateral_z) in enumerate(laterals):
            line = got[kind * slots : (kind + 1) * slots]
            if lateral_x != 0:
                line = step_x(line, ends, kind, lateral_x)[0]
            line = turn(line, -lateral_z, 0)[0:levels]
            none = jnp.zeros_like(line)
            extra[crossing(1, 1)[kind]] = pick(after, line, none)
            extra[crossing(1, -1)[kind]] = pick(after, none, line)
            weighted = lateral_weights[kind] * line
            zeroth = zeroth + weighted
            moment[0] = moment[0] + lateral_x * weighted
            moment[2] = moment[2] + lateral_z * weighted
        moment[1] = sign * zeroth
        edge_design = pick(after, design[rows - 1 : rows, :], design[0:1, :])
        damping = damp_top * (1.0 - edge_design) / (1.0 + edge_design)
        rate = 3.0 * (relax_rate - damping)
        fluid = pick(after, solid[:, rows - 1, :], solid[:, 0, :]) == 0
        inlet = pick(after, port[:, rows - 1, :], port[:, 0, :]) == 1
        scaled = [rate * part for part in moment]
        base = relax_rate * zeroth
        for number, vector in enumerate(velocities):
            added = base
            if number > 0:
                added = added + along(vector, scaled)
            if number in extra:
                added = added + (1.0 - relax_rate) * extra[number]
            added = jnp.where(fluid, added, extra.get(opposite[number], 0.0))
            added = jnp.where(inlet, 0.0, added)
            out[pairing, number, :, 0, :] = edge_rows[pairing, number] + added
        place = jnp.where(after, rows - 1, 0)
        copies.append(
            pltpu.make_async_copy(
                out.at[pairing, :, :, 0:1, :], far.at[:, :, pl.ds(place, 1), :], sems.at[pairing]
            )
        )
        copies[-1].start()
    for copy in copies:
        copy.wait()


def local_call(body, name, operands, out_shapes, scratch=(), far=(), far_out=(), aliases=None, room=16, cost=None):
    near_spec = pl.BlockSpec(memory_space=pltpu.VMEM)
    far_spec = pl.BlockSpec(memory_space=pltpu.HBM)
    shapes = [
        jax.ShapeDtypeStruct(shape, jnp.float32) if isinstance(shape, tuple) else shape
        for shape in out_shapes
    ]
    return pl.pallas_call(
        body,
        out_shape=shapes,
        in_specs=[far_spec if place in far else near_spec for place in range(len(operands))],
        out_specs=[far_spec if place in far_out else near_spec for place in range(len(shapes))],
        scratch_shapes=list(scratch),
        input_output_aliases=aliases or {},
        compiler_params=pltpu.CompilerParams(vmem_limit_bytes=room * 1024 * 1024),
        name=name,
        cost_estimate=cost,
    )(*operands)


def on_device(adjoint, momentum, design, solid_mask, port_label):
    levels, rows, lanes = adjoint.shape[1:]
    slots = lanes // tile
    groups = len(groups_of(levels))
    x_pairs, y_pairs, z_pairs = (len(pairings(axis)) for axis in ("gx", "gy", "depth"))
    z_got = []
    if z_pairs:
        faces = local_call(
            functools.partial(face_kernel, z_pairs),
            "depth_faces",
            [pltpu.with_memory_space_constraint(adjoint, pltpu.HBM)],
            [pltpu.VMEM((len(laterals), rows, lanes), jnp.float32)] * z_pairs,
            scratch=[pltpu.SemaphoreType.DMA((z_pairs * len(laterals),))],
            far=(0,),
            cost=pl.CostEstimate(flops=2000 * math.prod(adjoint.shape), bytes_accessed=100000, transcendentals=0),
        )
        z_got = [swap(face, "depth", pairing) for pairing, face in enumerate(faces)]
    packed = local_call(
        functools.partial(pack_kernel, (x_pairs, y_pairs)),
        "pack_faces",
        [adjoint, momentum, design, solid_mask, port_label],
        [(rows, lanes)] * x_pairs
        + [(kinds * slots, lanes)] * y_pairs
        + [(rows, lanes), (2, 3, rows, lanes)],
    )
    filled = local_call(
        functools.partial(depth_kernel, (x_pairs, y_pairs, z_pairs), levels),
        "add_z_faces",
        [*z_got, *packed],
        [(rows + y_pairs * slots, lanes)] * x_pairs
        + [(kinds * slots, lanes)] * y_pairs
        + [(rows, lanes)],
    )
    x_sent, y_sent, own = (
        filled[:x_pairs],
        filled[x_pairs : x_pairs + y_pairs],
        filled[x_pairs + y_pairs],
    )
    y_got = [swap(y_sent[pairing], "gy", pairing) for pairing in range(y_pairs)]
    x_got = [None] * x_pairs
    for pairing in reversed(range(x_pairs)):
        x_got[pairing] = swap(x_sent[pairing], "gx", pairing)
    merged = local_call(
        functools.partial(middle_kernel, (x_pairs, y_pairs), levels),
        "add_x_faces",
        [*x_got[::-1], *x_sent, own],
        [(slots + tile, lanes)] * y_pairs + [(2, rows, lanes)],
    )
    ends_sent, middle = (merged[:y_pairs], merged[y_pairs])
    ends_got = [swap(ends_sent[pairing], "gy", pairing) for pairing in range(y_pairs)]
    new_adjoint, edge_rows, norm = local_call(
        functools.partial(collide_kernel, (x_pairs, y_pairs, z_pairs)),
        "collide",
        [adjoint, design, solid_mask, port_label, *x_got[::-1], *z_got],
        [adjoint.shape, (max(y_pairs, 1), len(velocities), levels, lanes), (rows, lanes)],
        scratch=[pltpu.VMEM(adjoint.shape, jnp.float32), pltpu.SemaphoreType.DMA((groups,))],
        far_out=(0,),
        cost=pl.CostEstimate(
            flops=8000 * math.prod(adjoint.shape), bytes_accessed=4000000, transcendentals=0
        ),
    )
    (column,) = local_call(
        functools.partial(extend_kernel, y_pairs),
        "add_y_faces",
        [*y_got, *y_sent, *ends_got, *ends_sent, middle, norm],
        [(rows, lanes)],
    )
    if z_pairs == 1:
        other = swap(column, "depth", 0)
    else:
        other = lax.psum(column, "depth") - column
    if y_pairs:
        (new_adjoint,) = local_call(
            functools.partial(row_kernel, y_pairs),
            "add_y_rows",
            [new_adjoint, edge_rows, design, solid_mask, port_label, *y_got, *ends_got],
            [adjoint.shape],
            scratch=[
                pltpu.VMEM((y_pairs, len(velocities), levels, tile, lanes), jnp.float32),
                pltpu.SemaphoreType.DMA((y_pairs,)),
            ],
            far=(0,),
            far_out=(0,),
            aliases={0: 0},
        )
    (sensitivity,) = local_call(
        filter_kernel, "add_depth", [column, other], [(rows, lanes)]
    )
    return (new_adjoint, sensitivity)


def solution(mesh):
    in_specs = (
        P(None, "depth", "gy", "gx"),
        P(None, "depth", "gy", "gx"),
        P("gy", "gx"),
        P("depth", "gy", "gx"),
        P("depth", "gy", "gx"),
    )
    out_specs = (P(None, "depth", "gy", "gx"), P("gy", "gx"))
    return jax.shard_map(
        on_device, mesh=mesh, in_specs=in_specs, out_specs=out_specs, check_vma=False
    )
```

```python
import functools
import math

import jax
import jax.numpy as jnp
from jax import lax
from jax.experimental import pallas as pl
from jax.experimental.pallas import tpu as pltpu
from jax.sharding import PartitionSpec as P

velocities = (
    (0, 0, 0),
    (1, 0, 0),
    (-1, 0, 0),
    (0, 1, 0),
    (0, -1, 0),
    (0, 0, 1),
    (0, 0, -1),
    (1, 1, 0),
    (-1, -1, 0),
    (1, -1, 0),
    (-1, 1, 0),
    (1, 0, 1),
    (-1, 0, -1),
    (1, 0, -1),
    (-1, 0, 1),
    (0, 1, 1),
    (0, -1, -1),
    (0, 1, -1),
    (0, -1, 1),
)
lattice_weights = (1.0 / 3.0,) + (1.0 / 18.0,) * 6 + (1.0 / 36.0,) * 12
opposite = (0, 2, 1, 4, 3, 6, 5, 8, 7, 10, 9, 12, 11, 14, 13, 16, 15, 18, 17)
relax_rate = 1.25
damp_top = 0.5
cone_radius = 5.0
filter_reach = 4
wide = filter_reach + 1
tile = 8
level_group = 3
laterals = ((0, 0), (1, 0), (-1, 0), (0, 1), (0, -1))
lateral_weights = (1.0 / 18.0,) + (1.0 / 36.0,) * 4
kinds = len(laterals) + 3
both_ends = 2 * wide


def spot(kind):
    return 2 * kind + 1 if kind < kinds // 2 else 2 * kind - kinds


def x_lane(level, kind):
    return (level + 1) * tile + tile // 2 + spot(kind)


def crossing(axis, sign):
    others = [other for other in range(3) if other != axis]
    return [
        next(
            number
            for number, vector in enumerate(velocities)
            if vector[axis] == sign and (vector[others[0]], vector[others[1]]) == lateral
        )
        for lateral in laterals
    ]


def cone(offset_y, offset_x):
    return max(0.0, cone_radius - math.sqrt(offset_y * offset_y + offset_x * offset_x))


def pairings(axis):
    return range(min(lax.axis_size(axis) - 1, 2))


def swap(array, axis, pairing):
    size, cores = (lax.axis_size(axis), lax.axis_size("depth"))
    pairs = []
    for low in range(pairing, size - 1, 2):
        pairs += [(low, low + 1), (low + 1, low)]
    alone = [place for place in range(size) if place not in dict(pairs)]
    if axis == "depth" or cores % 2 != 0 or not alone:
        return lax.ppermute(array, axis, pairs)
    full = [(a * cores + core, b * cores + core) for a, b in pairs for core in range(cores)]
    for place in alone:
        full += [(place * cores + core, place * cores + (core ^ 1)) for core in range(cores)]
    return lax.ppermute(array, (axis, "depth"), full)


def partner_after(axis, pairing):
    return lax.rem(lax.axis_index(axis) + pairing, 2) == 0


def partners(axis, pairing):
    place, after = (lax.axis_index(axis), partner_after(axis, pairing))
    none_before, none_after = (place == 0, place == lax.axis_size(axis) - 1)
    return (
        jnp.logical_not(jnp.logical_or(after, none_before)),
        jnp.logical_and(after, jnp.logical_not(none_after)),
    )


def present(axis, pairing, array):
    before, after = partners(axis, pairing)
    return pick(jnp.logical_or(before, after), array, jnp.zeros_like(array))


def pick(flag, yes, no):
    return lax.select(flag, yes, no)


def turn(array, shift, axis):
    shift = shift % array.shape[axis]
    return array if shift == 0 else pltpu.roll(array, shift, axis)


def lanes_of(shape):
    return lax.broadcasted_iota(jnp.int32, shape, len(shape) - 1)


def rows_of(shape):
    return lax.broadcasted_iota(jnp.int32, shape, len(shape) - 2)


def halves(axis, arrays):
    before, after = 0.0, 0.0
    for pairing, array in enumerate(arrays):
        is_before, is_after = partners(axis, pairing)
        none = jnp.zeros_like(array)
        before = before + pick(is_before, array, none)
        after = after + pick(is_after, array, none)
    return (before, after)


def depth_plane(adjoint, halo, number, level):
    levels = adjoint.shape[1]
    if 0 <= level < levels:
        return adjoint[number, level]
    sign = 1 if level == levels else -1
    side = halo[1] if sign > 0 else halo[0]
    return side[crossing(2, sign).index(number)]


def gain_of(momentum, scale, solid, port, level):
    kept = (solid[level] == 0) & (port[level] != 1)
    factor = jnp.where(kept, scale, 0.0)
    return [factor * momentum[part, level] for part in range(3)]


def along_x(plane, step):
    lane = lanes_of(plane.shape)
    edge = plane.shape[-1] - 1 if step > 0 else 0
    return jnp.where(lane == edge, 0.0, turn(plane, -step, 1))


def along_y(plane, step):
    row = rows_of(plane.shape)
    edge = plane.shape[-2] - 1 if step > 0 else 0
    return jnp.where(row == edge, 0.0, turn(plane, -step, 0))


def own_moment(take):
    heavy, light = (1.0 / 18.0, 1.0 / 36.0)
    p = {
        number: take(number, vector[2]) for number, vector in enumerate(velocities) if number != 0
    }
    for number in (7, 8, 9, 10):
        p[number] = along_y(p[number], velocities[number][1])
    right_x = along_x(heavy * p[1] + light * ((p[7] + p[9]) + (p[11] + p[13])), 1)
    left_x = along_x(heavy * p[2] + light * ((p[8] + p[10]) + (p[12] + p[14])), -1)
    right_y = along_x(light * (p[7] - p[9]), 1)
    left_y = along_x(light * (p[10] - p[8]), -1)
    right_z = along_x(light * (p[11] - p[13]), 1)
    left_z = along_x(light * (p[14] - p[12]), -1)
    lower_y = along_y(heavy * p[3] + light * (p[15] + p[17]), 1)
    upper_y = along_y(heavy * p[4] + light * (p[16] + p[18]), -1)
    lower_z = along_y(light * (p[15] - p[17]), 1)
    upper_z = along_y(light * (p[18] - p[16]), -1)
    moment_x = right_x - left_x
    moment_y = (lower_y - upper_y) + (right_y + left_y)
    moment_z = heavy * (p[5] - p[6]) + ((right_z + left_z) + (lower_z + upper_z))
    return (moment_x, moment_y, moment_z)


def groups_of(levels):
    return [(low, min(low + level_group, levels)) for low in range(0, levels, level_group)]


def run_all(copies):
    for copy in copies:
        copy.start()
    for copy in copies:
        copy.wait()


def face_kernel(z_pairs, adjoint, *refs):
    outs, sems = (refs[:z_pairs], refs[z_pairs])
    copies = []
    for pairing in range(z_pairs):
        after = partner_after("depth", pairing)
        level = jnp.where(after, adjoint.shape[1] - 1, 0)
        for kind, numbers in enumerate(zip(crossing(2, -1), crossing(2, 1))):
            number = jnp.where(after, numbers[0], numbers[1])
            source, target = (adjoint.at[number, level], outs[pairing].at[kind])
            copies.append(pltpu.make_async_copy(source, target, sems.at[len(copies)]))
    run_all(copies)


def pack_kernel(counts, adjoint, momentum, design, solid, port, *refs):
    x_pairs, y_pairs = counts
    x_out, refs = (refs[:x_pairs], refs[x_pairs:])
    y_out, refs = (refs[:y_pairs], refs[y_pairs:])
    own_out, edge_gain = refs
    levels, rows, lanes = adjoint.shape[1:]
    slots = lanes // tile
    assert levels + 3 <= slots and 2 * filter_reach <= tile
    scale = 6.0 * damp_top / ((1.0 + design[...]) * (1.0 + design[...]))
    lane = lanes_of((rows, lanes))
    for pairing in range(y_pairs):
        y_out[pairing][...] = jnp.zeros(y_out[pairing].shape, jnp.float32)
    total = jnp.zeros((rows, lanes), jnp.float32)
    joint = [jnp.zeros((rows, lanes), jnp.float32) for half in range(2)]
    for level in range(levels):
        gain = gain_of(momentum, scale, solid, port, level)
        moment = own_moment(
            lambda number, step: adjoint[number, level + step]
            if 0 <= level + step < levels
            else jnp.zeros((rows, lanes), jnp.float32)
        )
        total = total + (gain[0] * moment[0] + gain[1] * moment[1] + gain[2] * moment[2])
        for side, edge in enumerate((0, levels - 1)):
            if level == edge:
                for part in range(3):
                    edge_gain[side, part] = gain[part]
        for pairing in range(y_pairs):
            after = partner_after("gy", pairing)
            for part in range(3):
                place = (len(laterals) + part) * slots + level
                y_out[pairing][place : place + 1, :] = pick(
                    after, gain[part][rows - 1 : rows], gain[part][0:1]
                )
        for kind in range(kinds):
            if kind < len(laterals):
                first = adjoint[crossing(0, 1)[kind], level]
                last = adjoint[crossing(0, -1)[kind], level]
                plane = jnp.where(lane == lanes - 1, last, first)
            else:
                plane = gain[kind - len(laterals)]
            half, place = (kind // (kinds // 2), x_lane(level, kind) // 2 * 2)
            chosen = lane // 2 == place // 2
            joint[half] = jnp.where(chosen, turn(plane, place + 1, 1), joint[half])
    for pairing in range(y_pairs):
        after = partner_after("gy", pairing)
        for kind in range(len(laterals)):
            last, first = (crossing(1, -1)[kind], crossing(1, 1)[kind])
            y_out[pairing][kind * slots : kind * slots + levels, :] = pick(
                after, adjoint[last, :, rows - 1, :], adjoint[first, :, 0, :]
            )
    own_out[...] = total
    odd = lane % 2 == 1
    first_pack = jnp.where(odd, joint[0], turn(joint[1], -1, 1))
    last_pack = jnp.where(odd, turn(joint[0], 1, 1), joint[1])
    for pairing in range(x_pairs):
        x_out[pairing][...] = pick(partner_after("gx", pairing), last_pack, first_pack)


def depth_kernel(counts, levels, *refs):
    x_pairs, y_pairs, z_pairs = counts
    z_got, refs = (refs[:z_pairs], refs[z_pairs:])
    x_pack, refs = (refs[:x_pairs], refs[x_pairs:])
    y_pack, refs = (refs[:y_pairs], refs[y_pairs:])
    own, edge_gain, refs = (*refs[:2], refs[2:])
    x_out, refs = (refs[:x_pairs], refs[x_pairs:])
    y_out, own_out = (refs[:y_pairs], refs[y_pairs])
    rows, lanes = own.shape
    slots = lanes // tile
    halo = halves("depth", [got[...] for got in z_got])
    lane = lanes_of((rows, lanes))
    total = own[...]
    if z_pairs:
        for side, sign in enumerate((-1, 1)):
            gain = [edge_gain[side, part] for part in range(3)]
            for kind, (step_x_, step_y_) in enumerate(laterals):
                plane = halo[side][kind]
                pull = sign * gain[2]
                if step_x_ != 0:
                    plane = along_x(plane, step_x_)
                    pull = pull + step_x_ * gain[0]
                if step_y_ != 0:
                    plane = along_y(plane, step_y_)
                    pull = pull + step_y_ * gain[1]
                total = total + lateral_weights[kind] * plane * pull
    own_out[...] = total
    beyond = ((3, levels, 1), (4, -1, 0))
    for pairing in range(y_pairs):
        after = partner_after("gy", pairing)
        y_out[pairing][...] = y_pack[pairing][...]
        if z_pairs:
            for kind, level, side in beyond:
                planes = crossing(2, 1 if side else -1)
                last, first = (
                    halo[side][planes.index(crossing(1, sign)[kind])] for sign in (-1, 1)
                )
                place = kind * slots + level % slots
                y_out[pairing][place : place + 1, :] = pick(
                    after, last[rows - 1 : rows], first[0:1]
                )
    chosen = (lane < filter_reach) | (lane >= lanes - filter_reach)
    sums = jnp.where(chosen, total, 0.0)
    packs = []
    for edge_shift, sign in ((0, 1), (1, -1)):
        pack = sums
        if z_pairs:
            for kind, level, side in beyond:
                planes = crossing(2, 1 if side else -1)
                plane = halo[side][planes.index(crossing(0, sign)[kind])]
                place = x_lane(level, kind)
                pack = jnp.where(lane == place, turn(plane, place + edge_shift, 1), pack)
        packs.append(pack)
    for pairing in range(x_pairs):
        after = partner_after("gx", pairing)
        x_out[pairing][0:rows, :] = x_pack[pairing][...] + pick(after, packs[1], packs[0])
    lane = lanes_of((slots, lanes))
    for y_pairing in range(y_pairs):
        ends = jnp.zeros((slots, lanes), jnp.float32)
        for kind in range(kinds):
            line = y_out[y_pairing][kind * slots : (kind + 1) * slots, :]
            place = kind * both_ends
            chosen = (lane >= place) & (lane < place + both_ends)
            ends = jnp.where(chosen, turn(line, place + wide, 1), ends)
        for pairing in range(x_pairs):
            base = rows + y_pairing * slots
            x_out[pairing][base : base + slots, :] = ends


def cross_x(levels, faces, gains, sign):
    rows = faces.shape[0]
    lane, row = (lanes_of(faces.shape), rows_of(faces.shape))
    first = x_lane(0, 0) - spot(0)
    gain = [turn(gains, -spot(len(laterals) + part), 1) for part in range(3)]
    terms = []
    for kind, (step_y, step_z) in enumerate(laterals):
        source = turn(faces, -spot(kind) - tile * step_z, 1)
        pull = sign * gain[0]
        if step_y != 0:
            edge = rows - 1 if step_y > 0 else 0
            source = jnp.where(row == edge, 0.0, turn(source, -step_y, 0))
            pull = pull + step_y * gain[1]
        if step_z != 0:
            pull = pull + step_z * gain[2]
        terms.append(lateral_weights[kind] * source * pull)
    used = (lane % tile == first % tile) & (lane >= first) & (lane < first + tile * levels)
    return jnp.sum(jnp.where(used, tree_sum(terms), 0.0), axis=1, keepdims=True)


def middle_kernel(counts, levels, *refs):
    x_pairs, y_pairs = counts
    x_got, refs = (refs[:x_pairs][::-1], refs[x_pairs:])
    x_sent, refs = (refs[:x_pairs], refs[x_pairs:])
    own, refs = (refs[0], refs[1:])
    y_out, middle = (refs[:y_pairs], refs[y_pairs])
    rows, lanes = own.shape
    slots = lanes // tile
    lane = lanes_of((rows, lanes))
    main = own[...]
    side, beside = (jnp.zeros((rows, lanes), jnp.float32) for part in range(2))
    free = spare_lanes(lanes)
    got_left, got_right = halves("gx", [got[0:rows, :] for got in x_got])
    sent_left, sent_right = halves("gx", [sent[0:rows, :] for sent in x_sent])
    if x_pairs:
        there_left = cross_x(levels, sent_left, got_left, 1)
        there_right = cross_x(levels, sent_right, got_right, -1)
        here_left = cross_x(levels, got_left, sent_left, -1)
        here_right = cross_x(levels, got_right, sent_right, 1)
        main = main + jnp.where(lane == 0, here_left, 0.0)
        main = main + jnp.where(lane == lanes - 1, here_right, 0.0)
        sums = jnp.where(lane < filter_reach, got_right, got_left)
        side = jnp.where(lane == 0, there_right, jnp.where(lane == lanes - 1, there_left, 0.0))
        chosen = (lane < filter_reach) | (lane >= lanes - filter_reach)
        side = side + jnp.where(chosen, sums, 0.0)
        beside = jnp.where(lane == free, there_right, 0.0)
        beside = beside + jnp.where(lane == free - 1, there_left, 0.0)
        chosen = (lane >= free - filter_reach) & (lane < free + filter_reach)
        beside = beside + jnp.where(chosen, turn(sums, free, 1), 0.0)
    middle[0] = main
    middle[1] = side
    lane = lanes_of((slots, lanes))
    for pairing in range(y_pairs):
        after = partner_after("gy", pairing)
        out = y_out[pairing]
        ends = jnp.zeros((slots, lanes), jnp.float32)
        if x_pairs:
            base = rows + pairing * slots
            left, right = halves("gx", [got[base : base + slots, :] for got in x_got])
            ends = jnp.where(lane % both_ends < wide, left, right)
        ends = jnp.where(lane < kinds * both_ends, ends, 0.0)
        out[0:tile, :] = ends[0:tile] + pick(after, beside[rows - tile :], beside[0:tile])
        out[tile:slots, :] = ends[tile:]
        out[slots : slots + tile, :] = pick(after, main[rows - tile :], main[0:tile])


def spare_lanes(lanes):
    assert kinds * both_ends + 2 * tile <= lanes and lanes & (lanes - 1) == 0
    return kinds * both_ends + tile


def step_x(line, ends, kind, step):
    lanes = line.shape[-1]
    main = turn(line, -step, 1)
    side = turn(ends, -kind * both_ends - wide - step, 1)
    if step == 0:
        return (main, side)
    edge = lanes_of(line.shape) == (lanes - 1 if step > 0 else 0)
    return (jnp.where(edge, side, main), jnp.where(edge, main, side))


def cross_y(faces, gains, sign):
    (lines, ends), (gain_lines, gain_ends) = (faces, gains)
    gain = [
        step_x(gain_lines[len(laterals) + part], gain_ends, len(laterals) + part, 0)
        for part in range(3)
    ]
    total_main, total_side = (0.0, 0.0)
    for kind, (lateral_x, lateral_z) in enumerate(laterals):
        main, side = step_x(lines[kind], ends, kind, lateral_x)
        main, side = (turn(main, -lateral_z, 0), turn(side, -lateral_z, 0))
        pull_main, pull_side = (sign * gain[1][0], sign * gain[1][1])
        if lateral_x != 0:
            pull_main = pull_main + lateral_x * gain[0][0]
            pull_side = pull_side + lateral_x * gain[0][1]
        if lateral_z != 0:
            pull_main = pull_main + lateral_z * gain[2][0]
            pull_side = pull_side + lateral_z * gain[2][1]
        total_main = total_main + lateral_weights[kind] * main * pull_main
        total_side = total_side + lateral_weights[kind] * side * pull_side
    return (
        jnp.sum(total_main, axis=0, keepdims=True),
        jnp.sum(total_side, axis=0, keepdims=True),
    )


def face_lines(lines, ends, slots):
    return (
        [lines[kind * slots : (kind + 1) * slots] for kind in range(kinds)],
        ends[0:slots],
    )


def extend_kernel(y_pairs, *refs):
    y_got, refs = (refs[:y_pairs], refs[y_pairs:])
    y_sent, refs = (refs[:y_pairs], refs[y_pairs:])
    ends_got, refs = (refs[:y_pairs], refs[y_pairs:])
    ends_sent, refs = (refs[:y_pairs], refs[y_pairs:])
    middle, norm, out = refs
    rows, lanes = middle.shape[1:]
    slots = lanes // tile
    row, row_tile = (rows_of((rows, lanes)), rows_of((tile, lanes)))
    own = [middle[0], middle[1]]
    before = [jnp.zeros((tile, lanes), jnp.float32) for part in range(2)]
    after = [jnp.zeros((tile, lanes), jnp.float32) for part in range(2)]
    for pairing in range(y_pairs):
        flag = partner_after("gy", pairing)
        sign = jnp.where(flag, 1.0, -1.0)
        got_lines = present("gy", pairing, y_got[pairing][...])
        got_ends = present("gy", pairing, ends_got[pairing][...])
        got = face_lines(got_lines, got_ends, slots)
        sent = face_lines(y_sent[pairing][...], ends_sent[pairing][...], slots)
        there = cross_y(sent, got, -sign)
        here = cross_y(got, sent, sign)
        edge_here = jnp.where(flag, rows - 1, 0)
        edge_there = jnp.where(flag, 0, tile - 1)
        for part in range(2):
            sums = got_ends[slots : slots + tile]
            if part == 1:
                sums = turn(got_ends[0:tile], -spare_lanes(lanes), 1)
            sums = sums + jnp.where(row_tile == edge_there, there[part], 0.0)
            none = jnp.zeros_like(sums)
            before[part] = before[part] + pick(flag, none, sums)
            after[part] = after[part] + pick(flag, sums, none)
            own[part] = own[part] + jnp.where(row == edge_here, here[part], 0.0)
    main, side = (
        jnp.concatenate([before[part], own[part], after[part]], axis=0) for part in range(2)
    )
    out[...] = cone_sum(main, side, rows) * norm[...]


def cone_sum(main, side, rows):
    lanes = main.shape[-1]
    lane = lanes_of(main.shape)
    pairs = [main]
    for offset in range(1, filter_reach + 1):
        up = jnp.where(lane < lanes - offset, turn(main, -offset, 1), turn(side, -offset, 1))
        down = jnp.where(lane >= offset, turn(main, offset, 1), turn(side, offset, 1))
        pairs.append(up + down)
    terms = []
    for offset in range(filter_reach + 1):
        weights = [cone(offset, distance) for distance in range(filter_reach + 1)]
        weighted = tree_sum([weight * pair for weight, pair in zip(weights, pairs) if weight > 0.0])
        for step in sorted({offset, -offset}):
            terms.append(turn(weighted, -step, 0)[tile : tile + rows])
    return tree_sum(terms)


def tree_sum(terms):
    while len(terms) > 1:
        terms = [sum(terms[place + 1 : place + 2], terms[place]) for place in range(0, len(terms), 2)]
    return terms[0]


def filter_kernel(mine, other, out):
    out[...] = mine[...] + other[...]


def filter_norm(rows, lanes):
    shape = (rows + 2 * tile, lanes)
    row, lane = (rows_of(shape), lanes_of(shape))
    place = lax.axis_index("gy") * rows + row - tile
    inside = jnp.where((place >= 0) & (place < lax.axis_size("gy") * rows), 1.0, 0.0)
    left = (lax.axis_index("gx") > 0).astype(jnp.float32)
    right = (lax.axis_index("gx") < lax.axis_size("gx") - 1).astype(jnp.float32)
    beside = inside * jnp.where(lane < lanes // 2, right, left)
    return 1.0 / cone_sum(inside, beside, rows)


def collide_kernel(counts, adjoint, design, solid, port, *refs):
    x_pairs, y_pairs, z_pairs = counts
    x_got, refs = (refs[:x_pairs][::-1], refs[x_pairs:])
    z_got, refs = (refs[:z_pairs], refs[z_pairs:])
    far, edge_rows, norm, out, sems = refs
    levels, rows, lanes = adjoint.shape[1:]
    slots = lanes // tile
    halo_z = halves("depth", [got[...] for got in z_got])
    halo_x = halves("gx", [got[0:rows, :] for got in x_got])
    damping = damp_top * (1.0 - design[...]) / (1.0 + design[...])
    rate = 3.0 * (relax_rate - damping)
    lane = lanes_of((rows, lanes))
    copies = []
    for level in range(levels):
        pulled = []
        for number, (step_x_, step_y_, step_z_) in enumerate(velocities):
            source = level + step_z_
            if z_pairs or 0 <= source < levels:
                plane = depth_plane(adjoint, halo_z, number, source)
            else:
                plane = jnp.zeros((rows, lanes), jnp.float32)
            if step_x_ != 0:
                edge = lanes - 1 if step_x_ > 0 else 0
                column = 0.0
                if x_pairs:
                    kind = crossing(0, step_x_).index(number)
                    side = halo_x[1 if step_x_ > 0 else 0]
                    column = turn(side, edge - x_lane(source, kind), 1)
                plane = jnp.where(lane == edge, column, turn(plane, -step_x_, 1))
            if step_y_ != 0:
                plane = along_y(plane, step_y_)
            pulled.append(plane)
        zeroth, moment = sums_of(pulled)
        base = relax_rate * zeroth
        scaled = [rate * part for part in moment]
        fluid, inlet = (solid[level] == 0, port[level] == 1)
        outflow = jnp.where(port[level] == 2, 1.0, 0.0)
        for number, vector in enumerate(velocities):
            updated = base + (1.0 - relax_rate) * pulled[number]
            if number > 0:
                updated = updated + along(vector, scaled)
            updated = jnp.where(fluid, updated, pulled[opposite[number]])
            updated = jnp.where(inlet, 0.0, updated)
            if vector[0] != 0:
                updated = updated + vector[0] * outflow
            out[number, level] = updated
        for place, (low, high) in enumerate(groups_of(levels)):
            if level == high - 1:
                copy = pltpu.make_async_copy(
                    out.at[:, low:high], far.at[:, low:high], sems.at[place]
                )
                copy.start()
                copies.append(copy)
    for pairing in range(y_pairs):
        after = partner_after("gy", pairing)
        for number in range(len(velocities)):
            edge_rows[pairing, number] = pick(after, out[number, :, rows - 1, :], out[number, :, 0, :])
    norm[...] = filter_norm(rows, lanes)
    for copy in copies:
        copy.wait()


def along(vector, parts):
    total = 0.0
    for component, part in zip(vector, parts):
        if component > 0:
            total = total + part
        if component < 0:
            total = total - part
    return total


def sums_of(pulled):
    heavy, light = (lattice_weights[1], lattice_weights[7])
    both, gap = ({}, {})
    for number in range(1, len(velocities), 2):
        both[number] = pulled[number] + pulled[number + 1]
        gap[number] = pulled[number] - pulled[number + 1]
    zeroth = lattice_weights[0] * pulled[0] + heavy * ((both[1] + both[3]) + both[5])
    zeroth = zeroth + light * (((both[7] + both[9]) + (both[11] + both[13])) + (both[15] + both[17]))
    moment = (
        heavy * gap[1] + light * ((gap[7] + gap[9]) + (gap[11] + gap[13])),
        heavy * gap[3] + light * ((gap[7] - gap[9]) + (gap[15] + gap[17])),
        heavy * gap[5] + light * ((gap[11] - gap[13]) + (gap[15] - gap[17])),
    )
    return (zeroth, moment)


def row_kernel(y_pairs, new, edge_rows, design, solid, port, *refs):
    y_got, refs = (refs[:y_pairs], refs[y_pairs:])
    ends_got, (far, out, sems) = (refs[:y_pairs], refs[y_pairs:])
    levels, rows, lanes = solid.shape
    slots = lanes // tile
    copies = []
    for pairing in range(y_pairs):
        after = partner_after("gy", pairing)
        sign = jnp.where(after, 1.0, -1.0)
        got = present("gy", pairing, y_got[pairing][...])
        ends = present("gy", pairing, ends_got[pairing][0:slots, :])
        extra, moment = ({}, [0.0, 0.0, 0.0])
        zeroth = 0.0
        for kind, (lateral_x, lateral_z) in enumerate(laterals):
            line = got[kind * slots : (kind + 1) * slots]
            if lateral_x != 0:
                line = step_x(line, ends, kind, lateral_x)[0]
            line = turn(line, -lateral_z, 0)[0:levels]
            none = jnp.zeros_like(line)
            extra[crossing(1, 1)[kind]] = pick(after, line, none)
            extra[crossing(1, -1)[kind]] = pick(after, none, line)
            weighted = lateral_weights[kind] * line
            zeroth = zeroth + weighted
            moment[0] = moment[0] + lateral_x * weighted
            moment[2] = moment[2] + lateral_z * weighted
        moment[1] = sign * zeroth
        edge_design = pick(after, design[rows - 1 : rows, :], design[0:1, :])
        damping = damp_top * (1.0 - edge_design) / (1.0 + edge_design)
        rate = 3.0 * (relax_rate - damping)
        fluid = pick(after, solid[:, rows - 1, :], solid[:, 0, :]) == 0
        inlet = pick(after, port[:, rows - 1, :], port[:, 0, :]) == 1
        scaled = [rate * part for part in moment]
        base = relax_rate * zeroth
        for number, vector in enumerate(velocities):
            added = base
            if number > 0:
                added = added + along(vector, scaled)
            if number in extra:
                added = added + (1.0 - relax_rate) * extra[number]
            added = jnp.where(fluid, added, extra.get(opposite[number], 0.0))
            added = jnp.where(inlet, 0.0, added)
            out[pairing, number, :, 0, :] = edge_rows[pairing, number] + added
        place = jnp.where(after, rows - 1, 0)
        copies.append(
            pltpu.make_async_copy(
                out.at[pairing, :, :, 0:1, :], far.at[:, :, pl.ds(place, 1), :], sems.at[pairing]
            )
        )
        copies[-1].start()
    for copy in copies:
        copy.wait()


def local_call(body, name, operands, out_shapes, scratch=(), far=(), far_out=(), aliases=None, room=16, cost=None):
    near_spec = pl.BlockSpec(memory_space=pltpu.VMEM)
    far_spec = pl.BlockSpec(memory_space=pltpu.HBM)
    shapes = [
        jax.ShapeDtypeStruct(shape, jnp.float32) if isinstance(shape, tuple) else shape
        for shape in out_shapes
    ]
    return pl.pallas_call(
        body,
        out_shape=shapes,
        in_specs=[far_spec if place in far else near_spec for place in range(len(operands))],
        out_specs=[far_spec if place in far_out else near_spec for place in range(len(shapes))],
        scratch_shapes=list(scratch),
        input_output_aliases=aliases or {},
        compiler_params=pltpu.CompilerParams(vmem_limit_bytes=room * 1024 * 1024),
        name=name,
        cost_estimate=cost,
    )(*operands)


def on_device(adjoint, momentum, design, solid_mask, port_label):
    levels, rows, lanes = adjoint.shape[1:]
    slots = lanes // tile
    groups = len(groups_of(levels))
    x_pairs, y_pairs, z_pairs = (len(pairings(axis)) for axis in ("gx", "gy", "depth"))
    z_got = []
    if z_pairs:
        faces = local_call(
            functools.partial(face_kernel, z_pairs),
            "depth_faces",
            [pltpu.with_memory_space_constraint(adjoint, pltpu.HBM)],
            [pltpu.VMEM((len(laterals), rows, lanes), jnp.float32)] * z_pairs,
            scratch=[pltpu.SemaphoreType.DMA((z_pairs * len(laterals),))],
            far=(0,),
            cost=pl.CostEstimate(flops=2000 * math.prod(adjoint.shape), bytes_accessed=100000, transcendentals=0),
        )
        z_got = [swap(face, "depth", pairing) for pairing, face in enumerate(faces)]
    packed = local_call(
        functools.partial(pack_kernel, (x_pairs, y_pairs)),
        "pack_faces",
        [adjoint, momentum, design, solid_mask, port_label],
        [(rows, lanes)] * x_pairs
        + [(kinds * slots, lanes)] * y_pairs
        + [(rows, lanes), (2, 3, rows, lanes)],
    )
    filled = local_call(
        functools.partial(depth_kernel, (x_pairs, y_pairs, z_pairs), levels),
        "add_z_faces",
        [*z_got, *packed],
        [(rows + y_pairs * slots, lanes)] * x_pairs
        + [(kinds * slots, lanes)] * y_pairs
        + [(rows, lanes)],
    )
    x_sent, y_sent, own = (
        filled[:x_pairs],
        filled[x_pairs : x_pairs + y_pairs],
        filled[x_pairs + y_pairs],
    )
    y_got = [swap(y_sent[pairing], "gy", pairing) for pairing in range(y_pairs)]
    x_got = [None] * x_pairs
    for pairing in reversed(range(x_pairs)):
        x_got[pairing] = swap(x_sent[pairing], "gx", pairing)
    merged = local_call(
        functools.partial(middle_kernel, (x_pairs, y_pairs), levels),
        "add_x_faces",
        [*x_got[::-1], *x_sent, own],
        [(slots + tile, lanes)] * y_pairs + [(2, rows, lanes)],
    )
    ends_sent, middle = (merged[:y_pairs], merged[y_pairs])
    ends_got = [swap(ends_sent[pairing], "gy", pairing) for pairing in range(y_pairs)]
    new_adjoint, edge_rows, norm = local_call(
        functools.partial(collide_kernel, (x_pairs, y_pairs, z_pairs)),
        "collide",
        [adjoint, design, solid_mask, port_label, *x_got[::-1], *z_got],
        [adjoint.shape, (max(y_pairs, 1), len(velocities), levels, lanes), (rows, lanes)],
        scratch=[pltpu.VMEM(adjoint.shape, jnp.float32), pltpu.SemaphoreType.DMA((groups,))],
        far_out=(0,),
        cost=pl.CostEstimate(
            flops=8000 * math.prod(adjoint.shape), bytes_accessed=4000000, transcendentals=0
        ),
    )
    (column,) = local_call(
        functools.partial(extend_kernel, y_pairs),
        "add_y_faces",
        [*y_got, *y_sent, *ends_got, *ends_sent, middle, norm],
        [(rows, lanes)],
    )
    if z_pairs == 1:
        other = swap(column, "depth", 0)
    else:
        other = lax.psum(column, "depth") - column
    if y_pairs:
        (new_adjoint,) = local_call(
            functools.partial(row_kernel, y_pairs),
            "add_y_rows",
            [new_adjoint, edge_rows, design, solid_mask, port_label, *y_got, *ends_got],
            [adjoint.shape],
            scratch=[
                pltpu.VMEM((y_pairs, len(velocities), levels, tile, lanes), jnp.float32),
                pltpu.SemaphoreType.DMA((y_pairs,)),
            ],
            far=(0,),
            far_out=(0,),
            aliases={0: 0},
        )
    (sensitivity,) = local_call(
        filter_kernel, "add_depth", [column, other], [(rows, lanes)]
    )
    return (new_adjoint, sensitivity)


def solution(mesh):
    in_specs = (
        P(None, "depth", "gy", "gx"),
        P(None, "depth", "gy", "gx"),
        P("gy", "gx"),
        P("depth", "gy", "gx"),
        P("depth", "gy", "gx"),
    )
    out_specs = (P(None, "depth", "gy", "gx"), P("gy", "gx"))
    return jax.shard_map(
        on_device, mesh=mesh, in_specs=in_specs, out_specs=out_specs, check_vma=False
    )
```

```python
import functools
import math

import jax
import jax.numpy as jnp
from jax import lax
from jax.experimental import pallas as pl
from jax.experimental.pallas import tpu as pltpu
from jax.sharding import PartitionSpec as P

velocities = (
    (0, 0, 0),
    (1, 0, 0),
    (-1, 0, 0),
    (0, 1, 0),
    (0, -1, 0),
    (0, 0, 1),
    (0, 0, -1),
    (1, 1, 0),
    (-1, -1, 0),
    (1, -1, 0),
    (-1, 1, 0),
    (1, 0, 1),
    (-1, 0, -1),
    (1, 0, -1),
    (-1, 0, 1),
    (0, 1, 1),
    (0, -1, -1),
    (0, 1, -1),
    (0, -1, 1),
)
lattice_weights = (1.0 / 3.0,) + (1.0 / 18.0,) * 6 + (1.0 / 36.0,) * 12
opposite = (0, 2, 1, 4, 3, 6, 5, 8, 7, 10, 9, 12, 11, 14, 13, 16, 15, 18, 17)
relax_rate = 1.25
damp_top = 0.5
cone_radius = 5.0
filter_reach = 4
wide = filter_reach + 1
tile = 8
level_group = 3
laterals = ((0, 0), (1, 0), (-1, 0), (0, 1), (0, -1))
lateral_weights = (1.0 / 18.0,) + (1.0 / 36.0,) * 4
kinds = len(laterals) + 3
both_ends = 2 * wide


def spot(kind):
    return 2 * kind + 1 if kind < kinds // 2 else 2 * kind - kinds


def x_lane(level, kind):
    return (level + 1) * tile + tile // 2 + spot(kind)


def crossing(axis, sign):
    others = [other for other in range(3) if other != axis]
    return [
        next(
            number
            for number, vector in enumerate(velocities)
            if vector[axis] == sign and (vector[others[0]], vector[others[1]]) == lateral
        )
        for lateral in laterals
    ]


def cone(offset_y, offset_x):
    return max(0.0, cone_radius - math.sqrt(offset_y * offset_y + offset_x * offset_x))


def pairings(axis):
    return range(min(lax.axis_size(axis) - 1, 2))


def swap(array, axis, pairing):
    size, cores = (lax.axis_size(axis), lax.axis_size("depth"))
    pairs = []
    for low in range(pairing, size - 1, 2):
        pairs += [(low, low + 1), (low + 1, low)]
    alone = [place for place in range(size) if place not in dict(pairs)]
    if axis == "depth" or cores % 2 != 0 or not alone:
        return lax.ppermute(array, axis, pairs)
    full = [(a * cores + core, b * cores + core) for a, b in pairs for core in range(cores)]
    for place in alone:
        full += [(place * cores + core, place * cores + (core ^ 1)) for core in range(cores)]
    return lax.ppermute(array, (axis, "depth"), full)


def partner_after(axis, pairing):
    return lax.rem(lax.axis_index(axis) + pairing, 2) == 0


def partners(axis, pairing):
    place, after = (lax.axis_index(axis), partner_after(axis, pairing))
    none_before, none_after = (place == 0, place == lax.axis_size(axis) - 1)
    return (
        jnp.logical_not(jnp.logical_or(after, none_before)),
        jnp.logical_and(after, jnp.logical_not(none_after)),
    )


def present(axis, pairing, array):
    before, after = partners(axis, pairing)
    return pick(jnp.logical_or(before, after), array, jnp.zeros_like(array))


def pick(flag, yes, no):
    return lax.select(flag, yes, no)


def turn(array, shift, axis):
    shift = shift % array.shape[axis]
    return array if shift == 0 else pltpu.roll(array, shift, axis)


def lanes_of(shape):
    return lax.broadcasted_iota(jnp.int32, shape, len(shape) - 1)


def rows_of(shape):
    return lax.broadcasted_iota(jnp.int32, shape, len(shape) - 2)


def halves(axis, arrays):
    before, after = 0.0, 0.0
    for pairing, array in enumerate(arrays):
        is_before, is_after = partners(axis, pairing)
        none = jnp.zeros_like(array)
        before = before + pick(is_before, array, none)
        after = after + pick(is_after, array, none)
    return (before, after)


def depth_plane(adjoint, halo, number, level):
    levels = adjoint.shape[1]
    if 0 <= level < levels:
        return adjoint[number, level]
    sign = 1 if level == levels else -1
    side = halo[1] if sign > 0 else halo[0]
    return side[crossing(2, sign).index(number)]


def gain_of(momentum, scale, solid, port, level):
    kept = (solid[level] == 0) & (port[level] != 1)
    factor = jnp.where(kept, scale, 0.0)
    return [factor * momentum[part, level] for part in range(3)]


def along_x(plane, step):
    lane = lanes_of(plane.shape)
    edge = plane.shape[-1] - 1 if step > 0 else 0
    return jnp.where(lane == edge, 0.0, turn(plane, -step, 1))


def along_y(plane, step):
    row = rows_of(plane.shape)
    edge = plane.shape[-2] - 1 if step > 0 else 0
    return jnp.where(row == edge, 0.0, turn(plane, -step, 0))


def own_moment(take):
    heavy, light = (1.0 / 18.0, 1.0 / 36.0)
    p = {
        number: take(number, vector[2]) for number, vector in enumerate(velocities) if number != 0
    }
    for number in (7, 8, 9, 10):
        p[number] = along_y(p[number], velocities[number][1])
    right_x = along_x(heavy * p[1] + light * ((p[7] + p[9]) + (p[11] + p[13])), 1)
    left_x = along_x(heavy * p[2] + light * ((p[8] + p[10]) + (p[12] + p[14])), -1)
    right_y = along_x(light * (p[7] - p[9]), 1)
    left_y = along_x(light * (p[10] - p[8]), -1)
    right_z = along_x(light * (p[11] - p[13]), 1)
    left_z = along_x(light * (p[14] - p[12]), -1)
    lower_y = along_y(heavy * p[3] + light * (p[15] + p[17]), 1)
    upper_y = along_y(heavy * p[4] + light * (p[16] + p[18]), -1)
    lower_z = along_y(light * (p[15] - p[17]), 1)
    upper_z = along_y(light * (p[18] - p[16]), -1)
    moment_x = right_x - left_x
    moment_y = (lower_y - upper_y) + (right_y + left_y)
    moment_z = heavy * (p[5] - p[6]) + ((right_z + left_z) + (lower_z + upper_z))
    return (moment_x, moment_y, moment_z)


def groups_of(levels):
    return [(low, min(low + level_group, levels)) for low in range(0, levels, level_group)]


def run_all(copies):
    for copy in copies:
        copy.start()
    for copy in copies:
        copy.wait()


def face_kernel(z_pairs, adjoint, *refs):
    outs, sems = (refs[:z_pairs], refs[z_pairs])
    copies = []
    for pairing in range(z_pairs):
        after = partner_after("depth", pairing)
        level = jnp.where(after, adjoint.shape[1] - 1, 0)
        for kind, numbers in enumerate(zip(crossing(2, -1), crossing(2, 1))):
            number = jnp.where(after, numbers[0], numbers[1])
            source, target = (adjoint.at[number, level], outs[pairing].at[kind])
            copies.append(pltpu.make_async_copy(source, target, sems.at[len(copies)]))
    run_all(copies)


def pack_kernel(counts, adjoint, momentum, design, solid, port, *refs):
    x_pairs, y_pairs = counts
    x_out, refs = (refs[:x_pairs], refs[x_pairs:])
    y_out, refs = (refs[:y_pairs], refs[y_pairs:])
    own_out, edge_gain = refs
    levels, rows, lanes = adjoint.shape[1:]
    slots = lanes // tile
    assert levels + 3 <= slots == 2 * tile and 2 * filter_reach <= tile
    scale = 6.0 * damp_top / ((1.0 + design[...]) * (1.0 + design[...]))
    lane = lanes_of((rows, lanes))
    for pairing in range(y_pairs):
        y_out[pairing][...] = jnp.zeros(y_out[pairing].shape, jnp.float32)
    total = jnp.zeros((rows, lanes), jnp.float32)
    joint = [jnp.zeros((rows, lanes), jnp.float32) for half in range(2)]
    for level in range(levels):
        gain = gain_of(momentum, scale, solid, port, level)
        moment = own_moment(
            lambda number, step: adjoint[number, level + step]
            if 0 <= level + step < levels
            else jnp.zeros((rows, lanes), jnp.float32)
        )
        total = total + (gain[0] * moment[0] + gain[1] * moment[1] + gain[2] * moment[2])
        for side, edge in enumerate((0, levels - 1)):
            if level == edge:
                for part in range(3):
                    edge_gain[side, part] = gain[part]
        for pairing in range(y_pairs):
            after = partner_after("gy", pairing)
            for part in range(3):
                place = (len(laterals) + part) * slots + level
                y_out[pairing][place : place + 1, :] = pick(
                    after, gain[part][rows - 1 : rows], gain[part][0:1]
                )
        for kind in range(kinds):
            if kind < len(laterals):
                first = adjoint[crossing(0, 1)[kind], level]
                last = adjoint[crossing(0, -1)[kind], level]
                plane = jnp.where(lane == lanes - 1, last, first)
            else:
                plane = gain[kind - len(laterals)]
            half, place = (kind // (kinds // 2), x_lane(level, kind) // 2 * 2)
            chosen = lane // 2 == place // 2
            joint[half] = jnp.where(chosen, turn(plane, place + 1, 1), joint[half])
    for pairing in range(y_pairs):
        after = partner_after("gy", pairing)
        for kind in range(len(laterals)):
            last, first = (crossing(1, -1)[kind], crossing(1, 1)[kind])
            y_out[pairing][kind * slots : kind * slots + levels, :] = pick(
                after, adjoint[last, :, rows - 1, :], adjoint[first, :, 0, :]
            )
    own_out[...] = total
    odd = lane % 2 == 1
    first_pack = jnp.where(odd, joint[0], turn(joint[1], -1, 1))
    last_pack = jnp.where(odd, turn(joint[0], 1, 1), joint[1])
    for pairing in range(x_pairs):
        x_out[pairing][...] = pick(partner_after("gx", pairing), last_pack, first_pack)


def depth_kernel(counts, levels, *refs):
    x_pairs, y_pairs, z_pairs = counts
    z_got, refs = (refs[:z_pairs], refs[z_pairs:])
    x_pack, refs = (refs[:x_pairs], refs[x_pairs:])
    y_pack, refs = (refs[:y_pairs], refs[y_pairs:])
    own, edge_gain, refs = (*refs[:2], refs[2:])
    x_out, refs = (refs[:x_pairs], refs[x_pairs:])
    y_out, own_out = (refs[:y_pairs], refs[y_pairs])
    rows, lanes = own.shape
    slots = lanes // tile
    halo = halves("depth", [got[...] for got in z_got])
    lane = lanes_of((rows, lanes))
    total = own[...]
    if z_pairs:
        for side, sign in enumerate((-1, 1)):
            gain = [edge_gain[side, part] for part in range(3)]
            for kind, (step_x_, step_y_) in enumerate(laterals):
                plane = halo[side][kind]
                pull = sign * gain[2]
                if step_x_ != 0:
                    plane = along_x(plane, step_x_)
                    pull = pull + step_x_ * gain[0]
                if step_y_ != 0:
                    plane = along_y(plane, step_y_)
                    pull = pull + step_y_ * gain[1]
                total = total + lateral_weights[kind] * plane * pull
    own_out[...] = total
    beyond = ((3, levels, 1), (4, -1, 0))
    for pairing in range(y_pairs):
        after = partner_after("gy", pairing)
        y_out[pairing][0 : kinds * slots, :] = y_pack[pairing][...]
        y_out[pairing][kinds * slots :, :] = pick(after, total[rows - tile :], total[0:tile])
        if z_pairs:
            for kind, level, side in beyond:
                planes = crossing(2, 1 if side else -1)
                last, first = (
                    halo[side][planes.index(crossing(1, sign)[kind])] for sign in (-1, 1)
                )
                place = kind * slots + level % slots
                y_out[pairing][place : place + 1, :] = pick(
                    after, last[rows - 1 : rows], first[0:1]
                )
    chosen = (lane < filter_reach) | (lane >= lanes - filter_reach)
    sums = jnp.where(chosen, total, 0.0)
    packs = []
    for edge_shift, sign in ((0, 1), (1, -1)):
        pack = sums
        if z_pairs:
            for kind, level, side in beyond:
                planes = crossing(2, 1 if side else -1)
                plane = halo[side][planes.index(crossing(0, sign)[kind])]
                place = x_lane(level, kind)
                pack = jnp.where(lane == place, turn(plane, place + edge_shift, 1), pack)
        packs.append(pack)
    for pairing in range(x_pairs):
        after = partner_after("gx", pairing)
        x_out[pairing][0:rows, :] = x_pack[pairing][...] + pick(after, packs[1], packs[0])
    lane = lanes_of((tile, lanes))
    for y_pairing in range(y_pairs):
        first, last = (jnp.zeros((tile, lanes), jnp.float32) for side in range(2))
        for kind in range(kinds):
            line = y_out[y_pairing][kind * slots : (kind + 1) * slots, :]
            upper, lower = (line[0:tile], line[tile:])
            place = kind * both_ends
            low = (lane >= place) & (lane < place + wide)
            high = (lane >= place + wide) & (lane < place + both_ends)
            upper = turn(upper, place + wide, 1)
            last = jnp.where(low, upper, jnp.where(high, turn(lower, place + both_ends, 1), last))
            first = jnp.where(high, upper, jnp.where(low, turn(lower, place, 1), first))
        base = rows + y_pairing * tile
        for pairing in range(x_pairs):
            after = partner_after("gx", pairing)
            x_out[pairing][base : base + tile, :] = pick(after, last, first)


def cross_x(levels, faces, gains, sign):
    rows = faces.shape[0]
    lane, row = (lanes_of(faces.shape), rows_of(faces.shape))
    first = x_lane(0, 0) - spot(0)
    gain = [turn(gains, -spot(len(laterals) + part), 1) for part in range(3)]
    terms = []
    for kind, (step_y, step_z) in enumerate(laterals):
        source = turn(faces, -spot(kind) - tile * step_z, 1)
        pull = sign * gain[0]
        if step_y != 0:
            edge = rows - 1 if step_y > 0 else 0
            source = jnp.where(row == edge, 0.0, turn(source, -step_y, 0))
            pull = pull + step_y * gain[1]
        if step_z != 0:
            pull = pull + step_z * gain[2]
        terms.append(lateral_weights[kind] * source * pull)
    used = (lane % tile == first % tile) & (lane >= first) & (lane < first + tile * levels)
    return jnp.sum(jnp.where(used, tree_sum(terms), 0.0), axis=1, keepdims=True)


def middle_kernel(counts, levels, *refs):
    x_pairs, y_pairs = counts
    x_got, refs = (refs[:x_pairs][::-1], refs[x_pairs:])
    x_sent, refs = (refs[:x_pairs], refs[x_pairs:])
    own, refs = (refs[0], refs[1:])
    y_out, middle = (refs[:y_pairs], refs[y_pairs])
    rows, lanes = own.shape
    slots = lanes // tile
    lane = lanes_of((rows, lanes))
    main = own[...]
    side, beside = (jnp.zeros((rows, lanes), jnp.float32) for part in range(2))
    free = spare_lanes(lanes)
    within = free + 2 * tile
    got_left, got_right = halves("gx", [got[0:rows, :] for got in x_got])
    sent_left, sent_right = halves("gx", [sent[0:rows, :] for sent in x_sent])
    if x_pairs:
        there_left = cross_x(levels, sent_left, got_left, 1)
        there_right = cross_x(levels, sent_right, got_right, -1)
        here_left = cross_x(levels, got_left, sent_left, -1)
        here_right = cross_x(levels, got_right, sent_right, 1)
        main = main + jnp.where(lane == 0, here_left, 0.0)
        main = main + jnp.where(lane == lanes - 1, here_right, 0.0)
        sums = jnp.where(lane < filter_reach, got_right, got_left)
        side = jnp.where(lane == 0, there_right, jnp.where(lane == lanes - 1, there_left, 0.0))
        chosen = (lane < filter_reach) | (lane >= lanes - filter_reach)
        side = side + jnp.where(chosen, sums, 0.0)
        beside = jnp.where(lane == free, there_right, 0.0)
        beside = beside + jnp.where(lane == free - 1, there_left, 0.0)
        beside = beside + jnp.where(lane == within, here_left, 0.0)
        beside = beside + jnp.where(lane == within - 1, here_right, 0.0)
        chosen = (lane >= free - filter_reach) & (lane < free + filter_reach)
        beside = beside + jnp.where(chosen, turn(sums, free, 1), 0.0)
    middle[0] = main
    middle[1] = side
    lane = lanes_of((slots, lanes))
    for pairing in range(y_pairs):
        after = partner_after("gy", pairing)
        out = y_out[pairing]
        ends = jnp.zeros((slots, lanes), jnp.float32)
        if x_pairs:
            base = rows + pairing * tile
            left, right = halves("gx", [got[base : base + tile, :] for got in x_got])
            low = lane[0:tile] % both_ends < wide
            upper = jnp.where(low, left, right)
            lower = jnp.where(low, turn(left, -wide, 1), turn(right, wide, 1))
            ends = jnp.concatenate([upper, lower], axis=0)
        ends = jnp.where(lane < kinds * both_ends, ends, 0.0)
        out[0:tile, :] = ends[0:tile] + pick(after, beside[rows - tile :], beside[0:tile])
        out[tile:slots, :] = ends[tile:]


def spare_lanes(lanes):
    assert kinds * both_ends + 4 * tile <= lanes and lanes & (lanes - 1) == 0
    return kinds * both_ends + tile


def step_x(line, ends, kind, step):
    lanes = line.shape[-1]
    main = turn(line, -step, 1)
    side = turn(ends, -kind * both_ends - wide - step, 1)
    if step == 0:
        return (main, side)
    edge = lanes_of(line.shape) == (lanes - 1 if step > 0 else 0)
    return (jnp.where(edge, side, main), jnp.where(edge, main, side))


def cross_y(faces, gains, sign):
    (lines, ends), (gain_lines, gain_ends) = (faces, gains)
    gain = [
        step_x(gain_lines[len(laterals) + part], gain_ends, len(laterals) + part, 0)
        for part in range(3)
    ]
    total_main, total_side = (0.0, 0.0)
    for kind, (lateral_x, lateral_z) in enumerate(laterals):
        main, side = step_x(lines[kind], ends, kind, lateral_x)
        main, side = (turn(main, -lateral_z, 0), turn(side, -lateral_z, 0))
        pull_main, pull_side = (sign * gain[1][0], sign * gain[1][1])
        if lateral_x != 0:
            pull_main = pull_main + lateral_x * gain[0][0]
            pull_side = pull_side + lateral_x * gain[0][1]
        if lateral_z != 0:
            pull_main = pull_main + lateral_z * gain[2][0]
            pull_side = pull_side + lateral_z * gain[2][1]
        total_main = total_main + lateral_weights[kind] * main * pull_main
        total_side = total_side + lateral_weights[kind] * side * pull_side
    return (
        jnp.sum(total_main, axis=0, keepdims=True),
        jnp.sum(total_side, axis=0, keepdims=True),
    )


def face_lines(lines, ends, slots):
    return (
        [lines[kind * slots : (kind + 1) * slots] for kind in range(kinds)],
        ends[0:slots],
    )


def extend_kernel(y_pairs, *refs):
    y_got, refs = (refs[:y_pairs], refs[y_pairs:])
    y_sent, refs = (refs[:y_pairs], refs[y_pairs:])
    ends_got, refs = (refs[:y_pairs], refs[y_pairs:])
    ends_sent, refs = (refs[:y_pairs], refs[y_pairs:])
    middle, norm, out = refs
    rows, lanes = middle.shape[1:]
    slots = lanes // tile
    row, row_tile, lane_tile = (
        rows_of((rows, lanes)),
        rows_of((tile, lanes)),
        lanes_of((tile, lanes)),
    )
    own = [middle[0], middle[1]]
    before = [jnp.zeros((tile, lanes), jnp.float32) for part in range(2)]
    after = [jnp.zeros((tile, lanes), jnp.float32) for part in range(2)]
    for pairing in range(y_pairs):
        flag = partner_after("gy", pairing)
        sign = jnp.where(flag, 1.0, -1.0)
        got_lines = present("gy", pairing, y_got[pairing][...])
        got_ends = present("gy", pairing, ends_got[pairing][...])
        got = face_lines(got_lines, got_ends, slots)
        sent = face_lines(y_sent[pairing][...], ends_sent[pairing][...], slots)
        there = cross_y(sent, got, -sign)
        here = cross_y(got, sent, sign)
        edge_here = jnp.where(flag, rows - 1, 0)
        edge_there = jnp.where(flag, 0, tile - 1)
        for part in range(2):
            if part == 0:
                within = turn(got_ends[0:tile], -spare_lanes(lanes) - 2 * tile, 1)
                edge = (lane_tile == 0) | (lane_tile == lanes - 1)
                sums = got_lines[kinds * slots :] + jnp.where(edge, within, 0.0)
            else:
                sums = turn(got_ends[0:tile], -spare_lanes(lanes), 1)
            sums = sums + jnp.where(row_tile == edge_there, there[part], 0.0)
            none = jnp.zeros_like(sums)
            before[part] = before[part] + pick(flag, none, sums)
            after[part] = after[part] + pick(flag, sums, none)
            own[part] = own[part] + jnp.where(row == edge_here, here[part], 0.0)
    main, side = (
        jnp.concatenate([before[part], own[part], after[part]], axis=0) for part in range(2)
    )
    out[...] = cone_sum(main, side, rows) * norm[...]


def cone_sum(main, side, rows):
    lanes = main.shape[-1]
    lane = lanes_of(main.shape)
    pairs = [main]
    for offset in range(1, filter_reach + 1):
        up = jnp.where(lane < lanes - offset, turn(main, -offset, 1), turn(side, -offset, 1))
        down = jnp.where(lane >= offset, turn(main, offset, 1), turn(side, offset, 1))
        pairs.append(up + down)
    terms = []
    for offset in range(filter_reach + 1):
        weights = [cone(offset, distance) for distance in range(filter_reach + 1)]
        weighted = tree_sum([weight * pair for weight, pair in zip(weights, pairs) if weight > 0.0])
        for step in sorted({offset, -offset}):
            terms.append(turn(weighted, -step, 0)[tile : tile + rows])
    return tree_sum(terms)


def tree_sum(terms):
    while len(terms) > 1:
        terms = [sum(terms[place + 1 : place + 2], terms[place]) for place in range(0, len(terms), 2)]
    return terms[0]


def filter_kernel(mine, other, out):
    out[...] = mine[...] + other[...]


def filter_norm(rows, lanes):
    shape = (rows + 2 * tile, lanes)
    row, lane = (rows_of(shape), lanes_of(shape))
    place = lax.axis_index("gy") * rows + row - tile
    inside = jnp.where((place >= 0) & (place < lax.axis_size("gy") * rows), 1.0, 0.0)
    left = (lax.axis_index("gx") > 0).astype(jnp.float32)
    right = (lax.axis_index("gx") < lax.axis_size("gx") - 1).astype(jnp.float32)
    beside = inside * jnp.where(lane < lanes // 2, right, left)
    return 1.0 / cone_sum(inside, beside, rows)


def collide_kernel(counts, adjoint, design, solid, port, *refs):
    x_pairs, y_pairs, z_pairs = counts
    x_got, refs = (refs[:x_pairs][::-1], refs[x_pairs:])
    z_got, refs = (refs[:z_pairs], refs[z_pairs:])
    far, edge_rows, norm, out, sems = refs
    levels, rows, lanes = adjoint.shape[1:]
    slots = lanes // tile
    halo_z = halves("depth", [got[...] for got in z_got])
    halo_x = halves("gx", [got[0:rows, :] for got in x_got])
    damping = damp_top * (1.0 - design[...]) / (1.0 + design[...])
    rate = 3.0 * (relax_rate - damping)
    lane = lanes_of((rows, lanes))
    copies = []
    for level in range(levels):
        pulled = []
        for number, (step_x_, step_y_, step_z_) in enumerate(velocities):
            source = level + step_z_
            if z_pairs or 0 <= source < levels:
                plane = depth_plane(adjoint, halo_z, number, source)
            else:
                plane = jnp.zeros((rows, lanes), jnp.float32)
            if step_x_ != 0:
                edge = lanes - 1 if step_x_ > 0 else 0
                column = 0.0
                if x_pairs:
                    kind = crossing(0, step_x_).index(number)
                    side = halo_x[1 if step_x_ > 0 else 0]
                    column = turn(side, edge - x_lane(source, kind), 1)
                plane = jnp.where(lane == edge, column, turn(plane, -step_x_, 1))
            if step_y_ != 0:
                plane = along_y(plane, step_y_)
            pulled.append(plane)
        zeroth, moment = sums_of(pulled)
        base = relax_rate * zeroth
        scaled = [rate * part for part in moment]
        fluid, inlet = (solid[level] == 0, port[level] == 1)
        outflow = jnp.where(port[level] == 2, 1.0, 0.0)
        for number, vector in enumerate(velocities):
            updated = base + (1.0 - relax_rate) * pulled[number]
            if number > 0:
                updated = updated + along(vector, scaled)
            updated = jnp.where(fluid, updated, pulled[opposite[number]])
            updated = jnp.where(inlet, 0.0, updated)
            if vector[0] != 0:
                updated = updated + vector[0] * outflow
            out[number, level] = updated
        for place, (low, high) in enumerate(groups_of(levels)):
            if level == high - 1:
                copy = pltpu.make_async_copy(
                    out.at[:, low:high], far.at[:, low:high], sems.at[place]
                )
                copy.start()
                copies.append(copy)
    for pairing in range(y_pairs):
        after = partner_after("gy", pairing)
        for number in range(len(velocities)):
            edge_rows[pairing, number] = pick(after, out[number, :, rows - 1, :], out[number, :, 0, :])
    norm[...] = filter_norm(rows, lanes)
    for copy in copies:
        copy.wait()


def along(vector, parts):
    total = 0.0
    for component, part in zip(vector, parts):
        if component > 0:
            total = total + part
        if component < 0:
            total = total - part
    return total


def sums_of(pulled):
    heavy, light = (lattice_weights[1], lattice_weights[7])
    both, gap = ({}, {})
    for number in range(1, len(velocities), 2):
        both[number] = pulled[number] + pulled[number + 1]
        gap[number] = pulled[number] - pulled[number + 1]
    zeroth = lattice_weights[0] * pulled[0] + heavy * ((both[1] + both[3]) + both[5])
    zeroth = zeroth + light * (((both[7] + both[9]) + (both[11] + both[13])) + (both[15] + both[17]))
    moment = (
        heavy * gap[1] + light * ((gap[7] + gap[9]) + (gap[11] + gap[13])),
        heavy * gap[3] + light * ((gap[7] - gap[9]) + (gap[15] + gap[17])),
        heavy * gap[5] + light * ((gap[11] - gap[13]) + (gap[15] - gap[17])),
    )
    return (zeroth, moment)


def row_kernel(y_pairs, new, edge_rows, design, solid, port, *refs):
    y_got, refs = (refs[:y_pairs], refs[y_pairs:])
    ends_got, (far, out, sems) = (refs[:y_pairs], refs[y_pairs:])
    levels, rows, lanes = solid.shape
    slots = lanes // tile
    copies = []
    for pairing in range(y_pairs):
        after = partner_after("gy", pairing)
        sign = jnp.where(after, 1.0, -1.0)
        got = present("gy", pairing, y_got[pairing][...])
        ends = present("gy", pairing, ends_got[pairing][0:slots, :])
        extra, moment = ({}, [0.0, 0.0, 0.0])
        zeroth = 0.0
        for kind, (lateral_x, lateral_z) in enumerate(laterals):
            line = got[kind * slots : (kind + 1) * slots]
            if lateral_x != 0:
                line = step_x(line, ends, kind, lateral_x)[0]
            line = turn(line, -lateral_z, 0)[0:levels]
            none = jnp.zeros_like(line)
            extra[crossing(1, 1)[kind]] = pick(after, line, none)
            extra[crossing(1, -1)[kind]] = pick(after, none, line)
            weighted = lateral_weights[kind] * line
            zeroth = zeroth + weighted
            moment[0] = moment[0] + lateral_x * weighted
            moment[2] = moment[2] + lateral_z * weighted
        moment[1] = sign * zeroth
        edge_design = pick(after, design[rows - 1 : rows, :], design[0:1, :])
        damping = damp_top * (1.0 - edge_design) / (1.0 + edge_design)
        rate = 3.0 * (relax_rate - damping)
        fluid = pick(after, solid[:, rows - 1, :], solid[:, 0, :]) == 0
        inlet = pick(after, port[:, rows - 1, :], port[:, 0, :]) == 1
        scaled = [rate * part for part in moment]
        base = relax_rate * zeroth
        for number, vector in enumerate(velocities):
            added = base
            if number > 0:
                added = added + along(vector, scaled)
            if number in extra:
                added = added + (1.0 - relax_rate) * extra[number]
            added = jnp.where(fluid, added, extra.get(opposite[number], 0.0))
            added = jnp.where(inlet, 0.0, added)
            out[pairing, number, :, 0, :] = edge_rows[pairing, number] + added
        place = jnp.where(after, rows - 1, 0)
        copies.append(
            pltpu.make_async_copy(
                out.at[pairing, :, :, 0:1, :], far.at[:, :, pl.ds(place, 1), :], sems.at[pairing]
            )
        )
        copies[-1].start()
    for copy in copies:
        copy.wait()


def local_call(body, name, operands, out_shapes, scratch=(), far=(), far_out=(), aliases=None, room=16, cost=None):
    near_spec = pl.BlockSpec(memory_space=pltpu.VMEM)
    far_spec = pl.BlockSpec(memory_space=pltpu.HBM)
    shapes = [
        jax.ShapeDtypeStruct(shape, jnp.float32) if isinstance(shape, tuple) else shape
        for shape in out_shapes
    ]
    return pl.pallas_call(
        body,
        out_shape=shapes,
        in_specs=[far_spec if place in far else near_spec for place in range(len(operands))],
        out_specs=[far_spec if place in far_out else near_spec for place in range(len(shapes))],
        scratch_shapes=list(scratch),
        input_output_aliases=aliases or {},
        compiler_params=pltpu.CompilerParams(vmem_limit_bytes=room * 1024 * 1024),
        name=name,
        cost_estimate=cost,
    )(*operands)


def on_device(adjoint, momentum, design, solid_mask, port_label):
    levels, rows, lanes = adjoint.shape[1:]
    slots = lanes // tile
    groups = len(groups_of(levels))
    x_pairs, y_pairs, z_pairs = (len(pairings(axis)) for axis in ("gx", "gy", "depth"))
    z_got = []
    if z_pairs:
        faces = local_call(
            functools.partial(face_kernel, z_pairs),
            "depth_faces",
            [pltpu.with_memory_space_constraint(adjoint, pltpu.HBM)],
            [pltpu.VMEM((len(laterals), rows, lanes), jnp.float32)] * z_pairs,
            scratch=[pltpu.SemaphoreType.DMA((z_pairs * len(laterals),))],
            far=(0,),
            cost=pl.CostEstimate(flops=2000 * math.prod(adjoint.shape), bytes_accessed=100000, transcendentals=0),
        )
        z_got = [swap(face, "depth", pairing) for pairing, face in enumerate(faces)]
    packed = local_call(
        functools.partial(pack_kernel, (x_pairs, y_pairs)),
        "pack_faces",
        [adjoint, momentum, design, solid_mask, port_label],
        [(rows, lanes)] * x_pairs
        + [(kinds * slots, lanes)] * y_pairs
        + [(rows, lanes), (2, 3, rows, lanes)],
    )
    filled = local_call(
        functools.partial(depth_kernel, (x_pairs, y_pairs, z_pairs), levels),
        "add_z_faces",
        [*z_got, *packed],
        [(rows + y_pairs * tile, lanes)] * x_pairs
        + [(kinds * slots + tile, lanes)] * y_pairs
        + [(rows, lanes)],
    )
    x_sent, y_sent, own = (
        filled[:x_pairs],
        filled[x_pairs : x_pairs + y_pairs],
        filled[x_pairs + y_pairs],
    )
    y_got = [swap(y_sent[pairing], "gy", pairing) for pairing in range(y_pairs)]
    x_got = [None] * x_pairs
    for pairing in reversed(range(x_pairs)):
        x_got[pairing] = swap(x_sent[pairing], "gx", pairing)
    merged = local_call(
        functools.partial(middle_kernel, (x_pairs, y_pairs), levels),
        "add_x_faces",
        [*x_got[::-1], *x_sent, own],
        [(slots, lanes)] * y_pairs + [(2, rows, lanes)],
    )
    ends_sent, middle = (merged[:y_pairs], merged[y_pairs])
    ends_got = [swap(ends_sent[pairing], "gy", pairing) for pairing in range(y_pairs)]
    new_adjoint, edge_rows, norm = local_call(
        functools.partial(collide_kernel, (x_pairs, y_pairs, z_pairs)),
        "collide",
        [adjoint, design, solid_mask, port_label, *x_got[::-1], *z_got],
        [adjoint.shape, (max(y_pairs, 1), len(velocities), levels, lanes), (rows, lanes)],
        scratch=[pltpu.VMEM(adjoint.shape, jnp.float32), pltpu.SemaphoreType.DMA((groups,))],
        far_out=(0,),
        cost=pl.CostEstimate(
            flops=8000 * math.prod(adjoint.shape), bytes_accessed=4000000, transcendentals=0
        ),
    )
    (column,) = local_call(
        functools.partial(extend_kernel, y_pairs),
        "add_y_faces",
        [*y_got, *y_sent, *ends_got, *ends_sent, middle, norm],
        [(rows, lanes)],
    )
    if z_pairs == 1:
        other = swap(column, "depth", 0)
    else:
        other = lax.psum(column, "depth") - column
    if y_pairs:
        (new_adjoint,) = local_call(
            functools.partial(row_kernel, y_pairs),
            "add_y_rows",
            [new_adjoint, edge_rows, design, solid_mask, port_label, *y_got, *ends_got],
            [adjoint.shape],
            scratch=[
                pltpu.VMEM((y_pairs, len(velocities), levels, tile, lanes), jnp.float32),
                pltpu.SemaphoreType.DMA((y_pairs,)),
            ],
            far=(0,),
            far_out=(0,),
            aliases={0: 0},
        )
    (sensitivity,) = local_call(
        filter_kernel, "add_depth", [column, other], [(rows, lanes)]
    )
    return (new_adjoint, sensitivity)


def solution(mesh):
    in_specs = (
        P(None, "depth", "gy", "gx"),
        P(None, "depth", "gy", "gx"),
        P("gy", "gx"),
        P("depth", "gy", "gx"),
        P("depth", "gy", "gx"),
    )
    out_specs = (P(None, "depth", "gy", "gx"), P("gy", "gx"))
    return jax.shard_map(
        on_device, mesh=mesh, in_specs=in_specs, out_specs=out_specs, check_vma=False
    )
```

```python
import functools
import math

import jax
import jax.numpy as jnp
from jax import lax
from jax.experimental import pallas as pl
from jax.experimental.pallas import tpu as pltpu
from jax.sharding import PartitionSpec as P

velocities = (
    (0, 0, 0),
    (1, 0, 0),
    (-1, 0, 0),
    (0, 1, 0),
    (0, -1, 0),
    (0, 0, 1),
    (0, 0, -1),
    (1, 1, 0),
    (-1, -1, 0),
    (1, -1, 0),
    (-1, 1, 0),
    (1, 0, 1),
    (-1, 0, -1),
    (1, 0, -1),
    (-1, 0, 1),
    (0, 1, 1),
    (0, -1, -1),
    (0, 1, -1),
    (0, -1, 1),
)
lattice_weights = (1.0 / 3.0,) + (1.0 / 18.0,) * 6 + (1.0 / 36.0,) * 12
opposite = (0, 2, 1, 4, 3, 6, 5, 8, 7, 10, 9, 12, 11, 14, 13, 16, 15, 18, 17)
relax_rate = 1.25
damp_top = 0.5
cone_radius = 5.0
filter_reach = 4
wide = filter_reach + 1
tile = 8
level_group = 3
laterals = ((0, 0), (1, 0), (-1, 0), (0, 1), (0, -1))
lateral_weights = (1.0 / 18.0,) + (1.0 / 36.0,) * 4
kinds = len(laterals) + 3
both_ends = 2 * wide


def spot(kind):
    return 2 * kind + 1 if kind < kinds // 2 else 2 * kind - kinds


def x_lane(level, kind):
    return (level + 1) * tile + tile // 2 + spot(kind)


def crossing(axis, sign):
    others = [other for other in range(3) if other != axis]
    return [
        next(
            number
            for number, vector in enumerate(velocities)
            if vector[axis] == sign and (vector[others[0]], vector[others[1]]) == lateral
        )
        for lateral in laterals
    ]


def cone(offset_y, offset_x):
    return max(0.0, cone_radius - math.sqrt(offset_y * offset_y + offset_x * offset_x))


def pairings(axis):
    return range(min(lax.axis_size(axis) - 1, 2))


def swap(array, axis, pairing):
    size, cores = (lax.axis_size(axis), lax.axis_size("depth"))
    pairs = []
    for low in range(pairing, size - 1, 2):
        pairs += [(low, low + 1), (low + 1, low)]
    alone = [place for place in range(size) if place not in dict(pairs)]
    if axis == "depth" or cores % 2 != 0 or not alone:
        return lax.ppermute(array, axis, pairs)
    full = [(a * cores + core, b * cores + core) for a, b in pairs for core in range(cores)]
    for place in alone:
        full += [(place * cores + core, place * cores + (core ^ 1)) for core in range(cores)]
    return lax.ppermute(array, (axis, "depth"), full)


def partner_after(axis, pairing):
    return lax.rem(lax.axis_index(axis) + pairing, 2) == 0


def partners(axis, pairing):
    place, after = (lax.axis_index(axis), partner_after(axis, pairing))
    none_before, none_after = (place == 0, place == lax.axis_size(axis) - 1)
    return (
        jnp.logical_not(jnp.logical_or(after, none_before)),
        jnp.logical_and(after, jnp.logical_not(none_after)),
    )


def present(axis, pairing, array):
    before, after = partners(axis, pairing)
    return pick(jnp.logical_or(before, after), array, jnp.zeros_like(array))


def pick(flag, yes, no):
    return lax.select(flag, yes, no)


def turn(array, shift, axis):
    shift = shift % array.shape[axis]
    return array if shift == 0 else pltpu.roll(array, shift, axis)


def lanes_of(shape):
    return lax.broadcasted_iota(jnp.int32, shape, len(shape) - 1)


def rows_of(shape):
    return lax.broadcasted_iota(jnp.int32, shape, len(shape) - 2)


def halves(axis, arrays):
    before, after = 0.0, 0.0
    for pairing, array in enumerate(arrays):
        is_before, is_after = partners(axis, pairing)
        none = jnp.zeros_like(array)
        before = before + pick(is_before, array, none)
        after = after + pick(is_after, array, none)
    return (before, after)


def depth_plane(adjoint, halo, number, level):
    levels = adjoint.shape[1]
    if 0 <= level < levels:
        return adjoint[number, level]
    sign = 1 if level == levels else -1
    side = halo[1] if sign > 0 else halo[0]
    return side[crossing(2, sign).index(number)]


def gain_of(momentum, scale, solid, port, level):
    kept = (solid[level] == 0) & (port[level] != 1)
    factor = jnp.where(kept, scale, 0.0)
    return [factor * momentum[part, level] for part in range(3)]


def along_x(plane, step):
    lane = lanes_of(plane.shape)
    edge = plane.shape[-1] - 1 if step > 0 else 0
    return jnp.where(lane == edge, 0.0, turn(plane, -step, 1))


def along_y(plane, step):
    row = rows_of(plane.shape)
    edge = plane.shape[-2] - 1 if step > 0 else 0
    return jnp.where(row == edge, 0.0, turn(plane, -step, 0))


def own_moment(take):
    heavy, light = (1.0 / 18.0, 1.0 / 36.0)
    p = {
        number: take(number, vector[2]) for number, vector in enumerate(velocities) if number != 0
    }
    for number in (7, 8, 9, 10):
        p[number] = along_y(p[number], velocities[number][1])
    right_x = along_x(heavy * p[1] + light * ((p[7] + p[9]) + (p[11] + p[13])), 1)
    left_x = along_x(heavy * p[2] + light * ((p[8] + p[10]) + (p[12] + p[14])), -1)
    right_y = along_x(light * (p[7] - p[9]), 1)
    left_y = along_x(light * (p[10] - p[8]), -1)
    right_z = along_x(light * (p[11] - p[13]), 1)
    left_z = along_x(light * (p[14] - p[12]), -1)
    lower_y = along_y(heavy * p[3] + light * (p[15] + p[17]), 1)
    upper_y = along_y(heavy * p[4] + light * (p[16] + p[18]), -1)
    lower_z = along_y(light * (p[15] - p[17]), 1)
    upper_z = along_y(light * (p[18] - p[16]), -1)
    moment_x = right_x - left_x
    moment_y = (lower_y - upper_y) + (right_y + left_y)
    moment_z = heavy * (p[5] - p[6]) + ((right_z + left_z) + (lower_z + upper_z))
    return (moment_x, moment_y, moment_z)


def groups_of(levels):
    return [(low, min(low + level_group, levels)) for low in range(0, levels, level_group)]


def run_all(copies):
    for copy in copies:
        copy.start()
    for copy in copies:
        copy.wait()


def face_kernel(z_pairs, adjoint, *refs):
    outs, sems = (refs[:z_pairs], refs[z_pairs])
    copies = []
    for pairing in range(z_pairs):
        after = partner_after("depth", pairing)
        level = jnp.where(after, adjoint.shape[1] - 1, 0)
        for kind, numbers in enumerate(zip(crossing(2, -1), crossing(2, 1))):
            number = jnp.where(after, numbers[0], numbers[1])
            source, target = (adjoint.at[number, level], outs[pairing].at[kind])
            copies.append(pltpu.make_async_copy(source, target, sems.at[len(copies)]))
    run_all(copies)


def pack_kernel(counts, adjoint, momentum, design, solid, port, *refs):
    x_pairs, y_pairs = counts
    x_out, refs = (refs[:x_pairs], refs[x_pairs:])
    y_out, refs = (refs[:y_pairs], refs[y_pairs:])
    own_out, edge_gain = refs
    levels, rows, lanes = adjoint.shape[1:]
    slots = lanes // tile
    assert levels + 3 <= slots == 2 * tile and 2 * filter_reach <= tile
    scale = 6.0 * damp_top / ((1.0 + design[...]) * (1.0 + design[...]))
    lane = lanes_of((rows, lanes))
    for pairing in range(y_pairs):
        y_out[pairing][...] = jnp.zeros(y_out[pairing].shape, jnp.float32)
    total = jnp.zeros((rows, lanes), jnp.float32)
    joint = [jnp.zeros((rows, lanes), jnp.float32) for half in range(2)]
    for level in range(levels):
        gain = gain_of(momentum, scale, solid, port, level)
        moment = own_moment(
            lambda number, step: adjoint[number, level + step]
            if 0 <= level + step < levels
            else jnp.zeros((rows, lanes), jnp.float32)
        )
        total = total + (gain[0] * moment[0] + gain[1] * moment[1] + gain[2] * moment[2])
        for side, edge in enumerate((0, levels - 1)):
            if level == edge:
                for part in range(3):
                    edge_gain[side, part] = gain[part]
        for pairing in range(y_pairs):
            after = partner_after("gy", pairing)
            for part in range(3):
                place = (len(laterals) + part) * slots + level
                y_out[pairing][place : place + 1, :] = pick(
                    after, gain[part][rows - 1 : rows], gain[part][0:1]
                )
        for kind in range(kinds):
            if kind < len(laterals):
                first = adjoint[crossing(0, 1)[kind], level]
                last = adjoint[crossing(0, -1)[kind], level]
                plane = jnp.where(lane == lanes - 1, last, first)
            else:
                plane = gain[kind - len(laterals)]
            half, place = (kind // (kinds // 2), x_lane(level, kind) // 2 * 2)
            chosen = lane // 2 == place // 2
            joint[half] = jnp.where(chosen, turn(plane, place + 1, 1), joint[half])
    for pairing in range(y_pairs):
        after = partner_after("gy", pairing)
        for kind in range(len(laterals)):
            last, first = (crossing(1, -1)[kind], crossing(1, 1)[kind])
            step = laterals[kind][1]
            low, high = (max(step, 0), levels + min(step, 0))
            base = kind * slots - step
            y_out[pairing][base + low : base + high, :] = pick(
                after, adjoint[last, low:high, rows - 1, :], adjoint[first, low:high, 0, :]
            )
    own_out[...] = total
    odd = lane % 2 == 1
    first_pack = jnp.where(odd, joint[0], turn(joint[1], -1, 1))
    last_pack = jnp.where(odd, turn(joint[0], 1, 1), joint[1])
    for pairing in range(x_pairs):
        x_out[pairing][...] = pick(partner_after("gx", pairing), last_pack, first_pack)


def depth_kernel(counts, levels, *refs):
    x_pairs, y_pairs, z_pairs = counts
    z_got, refs = (refs[:z_pairs], refs[z_pairs:])
    x_pack, refs = (refs[:x_pairs], refs[x_pairs:])
    y_pack, refs = (refs[:y_pairs], refs[y_pairs:])
    own, edge_gain, refs = (*refs[:2], refs[2:])
    x_out, refs = (refs[:x_pairs], refs[x_pairs:])
    y_out, own_out = (refs[:y_pairs], refs[y_pairs])
    rows, lanes = own.shape
    slots = lanes // tile
    halo = halves("depth", [got[...] for got in z_got])
    lane = lanes_of((rows, lanes))
    total = own[...]
    if z_pairs:
        for side, sign in enumerate((-1, 1)):
            gain = [edge_gain[side, part] for part in range(3)]
            for kind, (step_x_, step_y_) in enumerate(laterals):
                plane = halo[side][kind]
                pull = sign * gain[2]
                if step_x_ != 0:
                    plane = along_x(plane, step_x_)
                    pull = pull + step_x_ * gain[0]
                if step_y_ != 0:
                    plane = along_y(plane, step_y_)
                    pull = pull + step_y_ * gain[1]
                total = total + lateral_weights[kind] * plane * pull
    own_out[...] = total
    beyond = ((3, levels, 1), (4, -1, 0))
    for pairing in range(y_pairs):
        after = partner_after("gy", pairing)
        y_out[pairing][0 : kinds * slots, :] = y_pack[pairing][...]
        y_out[pairing][kinds * slots :, :] = pick(after, total[rows - tile :], total[0:tile])
        if z_pairs:
            for kind, level, side in beyond:
                planes = crossing(2, 1 if side else -1)
                last, first = (
                    halo[side][planes.index(crossing(1, sign)[kind])] for sign in (-1, 1)
                )
                place = kind * slots + level - laterals[kind][1]
                y_out[pairing][place : place + 1, :] = pick(
                    after, last[rows - 1 : rows], first[0:1]
                )
    chosen = (lane < filter_reach) | (lane >= lanes - filter_reach)
    sums = jnp.where(chosen, total, 0.0)
    packs = []
    for edge_shift, sign in ((0, 1), (1, -1)):
        pack = sums
        if z_pairs:
            for kind, level, side in beyond:
                planes = crossing(2, 1 if side else -1)
                plane = halo[side][planes.index(crossing(0, sign)[kind])]
                place = x_lane(level, kind)
                pack = jnp.where(lane == place, turn(plane, place + edge_shift, 1), pack)
        packs.append(pack)
    for pairing in range(x_pairs):
        after = partner_after("gx", pairing)
        x_out[pairing][0:rows, :] = x_pack[pairing][...] + pick(after, packs[1], packs[0])
    lane = lanes_of((tile, lanes))
    for y_pairing in range(y_pairs):
        first, last = (jnp.zeros((tile, lanes), jnp.float32) for side in range(2))
        for kind in range(kinds):
            line = y_out[y_pairing][kind * slots : (kind + 1) * slots, :]
            upper, lower = (line[0:tile], line[tile:])
            place = kind * both_ends
            low = (lane >= place) & (lane < place + wide)
            high = (lane >= place + wide) & (lane < place + both_ends)
            upper = turn(upper, place + wide, 1)
            last = jnp.where(low, upper, jnp.where(high, turn(lower, place + both_ends, 1), last))
            first = jnp.where(high, upper, jnp.where(low, turn(lower, place, 1), first))
        base = rows + y_pairing * tile
        for pairing in range(x_pairs):
            after = partner_after("gx", pairing)
            x_out[pairing][base : base + tile, :] = pick(after, last, first)


def cross_x(levels, faces, gains, sign):
    rows = faces.shape[0]
    lane, row = (lanes_of(faces.shape), rows_of(faces.shape))
    first = x_lane(0, 0) - spot(0)
    gain = [turn(gains, -spot(len(laterals) + part), 1) for part in range(3)]
    terms = []
    for kind, (step_y, step_z) in enumerate(laterals):
        source = turn(faces, -spot(kind) - tile * step_z, 1)
        pull = sign * gain[0]
        if step_y != 0:
            edge = rows - 1 if step_y > 0 else 0
            source = jnp.where(row == edge, 0.0, turn(source, -step_y, 0))
            pull = pull + step_y * gain[1]
        if step_z != 0:
            pull = pull + step_z * gain[2]
        terms.append(lateral_weights[kind] * source * pull)
    used = (lane % tile == first % tile) & (lane >= first) & (lane < first + tile * levels)
    return jnp.sum(jnp.where(used, tree_sum(terms), 0.0), axis=1, keepdims=True)


def middle_kernel(counts, levels, *refs):
    x_pairs, y_pairs = counts
    x_got, refs = (refs[:x_pairs][::-1], refs[x_pairs:])
    x_sent, refs = (refs[:x_pairs], refs[x_pairs:])
    own, refs = (refs[0], refs[1:])
    y_out, middle = (refs[:y_pairs], refs[y_pairs])
    rows, lanes = own.shape
    slots = lanes // tile
    lane = lanes_of((rows, lanes))
    main = own[...]
    side, beside = (jnp.zeros((rows, lanes), jnp.float32) for part in range(2))
    free = spare_lanes(lanes)
    within = free + 2 * tile
    got_left, got_right = halves("gx", [got[0:rows, :] for got in x_got])
    sent_left, sent_right = halves("gx", [sent[0:rows, :] for sent in x_sent])
    if x_pairs:
        there_left = cross_x(levels, sent_left, got_left, 1)
        there_right = cross_x(levels, sent_right, got_right, -1)
        here_left = cross_x(levels, got_left, sent_left, -1)
        here_right = cross_x(levels, got_right, sent_right, 1)
        main = main + jnp.where(lane == 0, here_left, 0.0)
        main = main + jnp.where(lane == lanes - 1, here_right, 0.0)
        sums = jnp.where(lane < filter_reach, got_right, got_left)
        side = jnp.where(lane == 0, there_right, jnp.where(lane == lanes - 1, there_left, 0.0))
        chosen = (lane < filter_reach) | (lane >= lanes - filter_reach)
        side = side + jnp.where(chosen, sums, 0.0)
        beside = jnp.where(lane == free, there_right, 0.0)
        beside = beside + jnp.where(lane == free - 1, there_left, 0.0)
        beside = beside + jnp.where(lane == within, here_left, 0.0)
        beside = beside + jnp.where(lane == within - 1, here_right, 0.0)
        chosen = (lane >= free - filter_reach) & (lane < free + filter_reach)
        beside = beside + jnp.where(chosen, turn(sums, free, 1), 0.0)
    middle[0] = main
    middle[1] = side
    lane = lanes_of((slots, lanes))
    for pairing in range(y_pairs):
        after = partner_after("gy", pairing)
        out = y_out[pairing]
        ends = jnp.zeros((slots, lanes), jnp.float32)
        if x_pairs:
            base = rows + pairing * tile
            left, right = halves("gx", [got[base : base + tile, :] for got in x_got])
            low = lane[0:tile] % both_ends < wide
            upper = jnp.where(low, left, right)
            lower = jnp.where(low, turn(left, -wide, 1), turn(right, wide, 1))
            ends = jnp.concatenate([upper, lower], axis=0)
        ends = jnp.where(lane < kinds * both_ends, ends, 0.0)
        out[0:tile, :] = ends[0:tile] + pick(after, beside[rows - tile :], beside[0:tile])
        out[tile:slots, :] = ends[tile:]


def spare_lanes(lanes):
    assert kinds * both_ends + 4 * tile <= lanes and lanes & (lanes - 1) == 0
    return kinds * both_ends + tile


def step_x(line, ends, kind, step):
    lanes = line.shape[-1]
    main = turn(line, -step, 1)
    side = turn(ends, -kind * both_ends - wide - step, 1)
    if step == 0:
        return (main, side)
    edge = lanes_of(line.shape) == (lanes - 1 if step > 0 else 0)
    return (jnp.where(edge, side, main), jnp.where(edge, main, side))


def cross_y(faces, gains, sign):
    (lines, ends), (gain_lines, gain_ends) = (faces, gains)
    gain = [
        step_x(gain_lines[len(laterals) + part], gain_ends, len(laterals) + part, 0)
        for part in range(3)
    ]
    total_main, total_side = (0.0, 0.0)
    for kind, (lateral_x, lateral_z) in enumerate(laterals):
        main, side = step_x(lines[kind], ends, kind, lateral_x)
        pull_main, pull_side = (sign * gain[1][0], sign * gain[1][1])
        if lateral_x != 0:
            pull_main = pull_main + lateral_x * gain[0][0]
            pull_side = pull_side + lateral_x * gain[0][1]
        if lateral_z != 0:
            pull_main = pull_main + lateral_z * gain[2][0]
            pull_side = pull_side + lateral_z * gain[2][1]
        total_main = total_main + lateral_weights[kind] * main * pull_main
        total_side = total_side + lateral_weights[kind] * side * pull_side
    return (
        jnp.sum(total_main, axis=0, keepdims=True),
        jnp.sum(total_side, axis=0, keepdims=True),
    )


def face_lines(lines, ends, slots):
    return (
        [lines[kind * slots : (kind + 1) * slots] for kind in range(kinds)],
        ends[0:slots],
    )


def extend_kernel(y_pairs, *refs):
    y_got, refs = (refs[:y_pairs], refs[y_pairs:])
    y_sent, refs = (refs[:y_pairs], refs[y_pairs:])
    ends_got, refs = (refs[:y_pairs], refs[y_pairs:])
    ends_sent, refs = (refs[:y_pairs], refs[y_pairs:])
    middle, norm, out = refs
    rows, lanes = middle.shape[1:]
    slots = lanes // tile
    row, row_tile, lane_tile = (
        rows_of((rows, lanes)),
        rows_of((tile, lanes)),
        lanes_of((tile, lanes)),
    )
    own = [middle[0], middle[1]]
    before = [jnp.zeros((tile, lanes), jnp.float32) for part in range(2)]
    after = [jnp.zeros((tile, lanes), jnp.float32) for part in range(2)]
    for pairing in range(y_pairs):
        flag = partner_after("gy", pairing)
        sign = jnp.where(flag, 1.0, -1.0)
        got_lines = present("gy", pairing, y_got[pairing][...])
        got_ends = present("gy", pairing, ends_got[pairing][...])
        got = face_lines(got_lines, got_ends, slots)
        sent = face_lines(y_sent[pairing][...], ends_sent[pairing][...], slots)
        there = cross_y(sent, got, -sign)
        here = cross_y(got, sent, sign)
        edge_here = jnp.where(flag, rows - 1, 0)
        edge_there = jnp.where(flag, 0, tile - 1)
        for part in range(2):
            if part == 0:
                within = turn(got_ends[0:tile], -spare_lanes(lanes) - 2 * tile, 1)
                edge = (lane_tile == 0) | (lane_tile == lanes - 1)
                sums = got_lines[kinds * slots :] + jnp.where(edge, within, 0.0)
            else:
                sums = turn(got_ends[0:tile], -spare_lanes(lanes), 1)
            sums = sums + jnp.where(row_tile == edge_there, there[part], 0.0)
            none = jnp.zeros_like(sums)
            before[part] = before[part] + pick(flag, none, sums)
            after[part] = after[part] + pick(flag, sums, none)
            own[part] = own[part] + jnp.where(row == edge_here, here[part], 0.0)
    main, side = (
        jnp.concatenate([before[part], own[part], after[part]], axis=0) for part in range(2)
    )
    out[...] = cone_sum(main, side, rows) * norm[...]


def cone_sum(main, side, rows):
    lanes = main.shape[-1]
    lane = lanes_of(main.shape)
    pairs = [main]
    for offset in range(1, filter_reach + 1):
        up = jnp.where(lane < lanes - offset, turn(main, -offset, 1), turn(side, -offset, 1))
        down = jnp.where(lane >= offset, turn(main, offset, 1), turn(side, offset, 1))
        pairs.append(up + down)
    terms = []
    for offset in range(filter_reach + 1):
        weights = [cone(offset, distance) for distance in range(filter_reach + 1)]
        weighted = tree_sum([weight * pair for weight, pair in zip(weights, pairs) if weight > 0.0])
        for step in sorted({offset, -offset}):
            terms.append(turn(weighted, -step, 0)[tile : tile + rows])
    return tree_sum(terms)


def tree_sum(terms):
    while len(terms) > 1:
        terms = [sum(terms[place + 1 : place + 2], terms[place]) for place in range(0, len(terms), 2)]
    return terms[0]


def filter_kernel(mine, other, out):
    out[...] = mine[...] + other[...]


def filter_norm(rows, lanes):
    shape = (rows + 2 * tile, lanes)
    row, lane = (rows_of(shape), lanes_of(shape))
    place = lax.axis_index("gy") * rows + row - tile
    inside = jnp.where((place >= 0) & (place < lax.axis_size("gy") * rows), 1.0, 0.0)
    left = (lax.axis_index("gx") > 0).astype(jnp.float32)
    right = (lax.axis_index("gx") < lax.axis_size("gx") - 1).astype(jnp.float32)
    beside = inside * jnp.where(lane < lanes // 2, right, left)
    return 1.0 / cone_sum(inside, beside, rows)


def collide_kernel(counts, adjoint, design, solid, port, *refs):
    x_pairs, y_pairs, z_pairs = counts
    x_got, refs = (refs[:x_pairs][::-1], refs[x_pairs:])
    z_got, refs = (refs[:z_pairs], refs[z_pairs:])
    far, edge_rows, norm, out, sems = refs
    levels, rows, lanes = adjoint.shape[1:]
    slots = lanes // tile
    halo_z = halves("depth", [got[...] for got in z_got])
    halo_x = halves("gx", [got[0:rows, :] for got in x_got])
    damping = damp_top * (1.0 - design[...]) / (1.0 + design[...])
    rate = 3.0 * (relax_rate - damping)
    lane = lanes_of((rows, lanes))
    copies = []
    for level in range(levels):
        pulled = []
        for number, (step_x_, step_y_, step_z_) in enumerate(velocities):
            source = level + step_z_
            if z_pairs or 0 <= source < levels:
                plane = depth_plane(adjoint, halo_z, number, source)
            else:
                plane = jnp.zeros((rows, lanes), jnp.float32)
            if step_x_ != 0:
                edge = lanes - 1 if step_x_ > 0 else 0
                column = 0.0
                if x_pairs:
                    kind = crossing(0, step_x_).index(number)
                    side = halo_x[1 if step_x_ > 0 else 0]
                    column = turn(side, edge - x_lane(source, kind), 1)
                plane = jnp.where(lane == edge, column, turn(plane, -step_x_, 1))
            if step_y_ != 0:
                plane = along_y(plane, step_y_)
            pulled.append(plane)
        zeroth, moment = sums_of(pulled)
        base = relax_rate * zeroth
        scaled = [rate * part for part in moment]
        fluid, inlet = (solid[level] == 0, port[level] == 1)
        outflow = jnp.where(port[level] == 2, 1.0, 0.0)
        for number, vector in enumerate(velocities):
            updated = base + (1.0 - relax_rate) * pulled[number]
            if number > 0:
                updated = updated + along(vector, scaled)
            updated = jnp.where(fluid, updated, pulled[opposite[number]])
            updated = jnp.where(inlet, 0.0, updated)
            if vector[0] != 0:
                updated = updated + vector[0] * outflow
            out[number, level] = updated
        for place, (low, high) in enumerate(groups_of(levels)):
            if level == high - 1:
                copy = pltpu.make_async_copy(
                    out.at[:, low:high], far.at[:, low:high], sems.at[place]
                )
                copy.start()
                copies.append(copy)
    for pairing in range(y_pairs):
        after = partner_after("gy", pairing)
        for number in range(len(velocities)):
            edge_rows[pairing, number] = pick(after, out[number, :, rows - 1, :], out[number, :, 0, :])
    norm[...] = filter_norm(rows, lanes)
    for copy in copies:
        copy.wait()


def along(vector, parts):
    total = 0.0
    for component, part in zip(vector, parts):
        if component > 0:
            total = total + part
        if component < 0:
            total = total - part
    return total


def sums_of(pulled):
    heavy, light = (lattice_weights[1], lattice_weights[7])
    both, gap = ({}, {})
    for number in range(1, len(velocities), 2):
        both[number] = pulled[number] + pulled[number + 1]
        gap[number] = pulled[number] - pulled[number + 1]
    zeroth = lattice_weights[0] * pulled[0] + heavy * ((both[1] + both[3]) + both[5])
    zeroth = zeroth + light * (((both[7] + both[9]) + (both[11] + both[13])) + (both[15] + both[17]))
    moment = (
        heavy * gap[1] + light * ((gap[7] + gap[9]) + (gap[11] + gap[13])),
        heavy * gap[3] + light * ((gap[7] - gap[9]) + (gap[15] + gap[17])),
        heavy * gap[5] + light * ((gap[11] - gap[13]) + (gap[15] - gap[17])),
    )
    return (zeroth, moment)


def row_kernel(y_pairs, new, edge_rows, design, solid, port, *refs):
    y_got, refs = (refs[:y_pairs], refs[y_pairs:])
    ends_got, (far, out, sems) = (refs[:y_pairs], refs[y_pairs:])
    levels, rows, lanes = solid.shape
    slots = lanes // tile
    copies = []
    for pairing in range(y_pairs):
        after = partner_after("gy", pairing)
        sign = jnp.where(after, 1.0, -1.0)
        got = present("gy", pairing, y_got[pairing][...])
        ends = present("gy", pairing, ends_got[pairing][0:slots, :])
        extra, moment = ({}, [0.0, 0.0, 0.0])
        zeroth = 0.0
        for kind, (lateral_x, lateral_z) in enumerate(laterals):
            line = got[kind * slots : (kind + 1) * slots]
            if lateral_x != 0:
                line = step_x(line, ends, kind, lateral_x)[0]
            line = line[0:levels]
            none = jnp.zeros_like(line)
            extra[crossing(1, 1)[kind]] = pick(after, line, none)
            extra[crossing(1, -1)[kind]] = pick(after, none, line)
            weighted = lateral_weights[kind] * line
            zeroth = zeroth + weighted
            moment[0] = moment[0] + lateral_x * weighted
            moment[2] = moment[2] + lateral_z * weighted
        moment[1] = sign * zeroth
        edge_design = pick(after, design[rows - 1 : rows, :], design[0:1, :])
        damping = damp_top * (1.0 - edge_design) / (1.0 + edge_design)
        rate = 3.0 * (relax_rate - damping)
        fluid = pick(after, solid[:, rows - 1, :], solid[:, 0, :]) == 0
        inlet = pick(after, port[:, rows - 1, :], port[:, 0, :]) == 1
        scaled = [rate * part for part in moment]
        base = relax_rate * zeroth
        for number, vector in enumerate(velocities):
            added = base
            if number > 0:
                added = added + along(vector, scaled)
            if number in extra:
                added = added + (1.0 - relax_rate) * extra[number]
            added = jnp.where(fluid, added, extra.get(opposite[number], 0.0))
            added = jnp.where(inlet, 0.0, added)
            out[pairing, number, :, 0, :] = edge_rows[pairing, number] + added
        place = jnp.where(after, rows - 1, 0)
        copies.append(
            pltpu.make_async_copy(
                out.at[pairing, :, :, 0:1, :], far.at[:, :, pl.ds(place, 1), :], sems.at[pairing]
            )
        )
        copies[-1].start()
    for copy in copies:
        copy.wait()


def local_call(body, name, operands, out_shapes, scratch=(), far=(), far_out=(), aliases=None, room=16, cost=None):
    near_spec = pl.BlockSpec(memory_space=pltpu.VMEM)
    far_spec = pl.BlockSpec(memory_space=pltpu.HBM)
    shapes = [
        jax.ShapeDtypeStruct(shape, jnp.float32) if isinstance(shape, tuple) else shape
        for shape in out_shapes
    ]
    return pl.pallas_call(
        body,
        out_shape=shapes,
        in_specs=[far_spec if place in far else near_spec for place in range(len(operands))],
        out_specs=[far_spec if place in far_out else near_spec for place in range(len(shapes))],
        scratch_shapes=list(scratch),
        input_output_aliases=aliases or {},
        compiler_params=pltpu.CompilerParams(vmem_limit_bytes=room * 1024 * 1024),
        name=name,
        cost_estimate=cost,
    )(*operands)


def on_device(adjoint, momentum, design, solid_mask, port_label):
    levels, rows, lanes = adjoint.shape[1:]
    slots = lanes // tile
    groups = len(groups_of(levels))
    x_pairs, y_pairs, z_pairs = (len(pairings(axis)) for axis in ("gx", "gy", "depth"))
    z_got = []
    if z_pairs:
        faces = local_call(
            functools.partial(face_kernel, z_pairs),
            "depth_faces",
            [pltpu.with_memory_space_constraint(adjoint, pltpu.HBM)],
            [pltpu.VMEM((len(laterals), rows, lanes), jnp.float32)] * z_pairs,
            scratch=[pltpu.SemaphoreType.DMA((z_pairs * len(laterals),))],
            far=(0,),
            cost=pl.CostEstimate(flops=2000 * math.prod(adjoint.shape), bytes_accessed=100000, transcendentals=0),
        )
        z_got = [swap(face, "depth", pairing) for pairing, face in enumerate(faces)]
    packed = local_call(
        functools.partial(pack_kernel, (x_pairs, y_pairs)),
        "pack_faces",
        [adjoint, momentum, design, solid_mask, port_label],
        [(rows, lanes)] * x_pairs
        + [(kinds * slots, lanes)] * y_pairs
        + [(rows, lanes), (2, 3, rows, lanes)],
    )
    filled = local_call(
        functools.partial(depth_kernel, (x_pairs, y_pairs, z_pairs), levels),
        "add_z_faces",
        [*z_got, *packed],
        [(rows + y_pairs * tile, lanes)] * x_pairs
        + [(kinds * slots + tile, lanes)] * y_pairs
        + [(rows, lanes)],
    )
    x_sent, y_sent, own = (
        filled[:x_pairs],
        filled[x_pairs : x_pairs + y_pairs],
        filled[x_pairs + y_pairs],
    )
    y_got = [swap(y_sent[pairing], "gy", pairing) for pairing in range(y_pairs)]
    x_got = [None] * x_pairs
    for pairing in reversed(range(x_pairs)):
        x_got[pairing] = swap(x_sent[pairing], "gx", pairing)
    merged = local_call(
        functools.partial(middle_kernel, (x_pairs, y_pairs), levels),
        "add_x_faces",
        [*x_got[::-1], *x_sent, own],
        [(slots, lanes)] * y_pairs + [(2, rows, lanes)],
    )
    ends_sent, middle = (merged[:y_pairs], merged[y_pairs])
    ends_got = [swap(ends_sent[pairing], "gy", pairing) for pairing in range(y_pairs)]
    new_adjoint, edge_rows, norm = local_call(
        functools.partial(collide_kernel, (x_pairs, y_pairs, z_pairs)),
        "collide",
        [adjoint, design, solid_mask, port_label, *x_got[::-1], *z_got],
        [adjoint.shape, (max(y_pairs, 1), len(velocities), levels, lanes), (rows, lanes)],
        scratch=[pltpu.VMEM(adjoint.shape, jnp.float32), pltpu.SemaphoreType.DMA((groups,))],
        far_out=(0,),
        cost=pl.CostEstimate(
            flops=8000 * math.prod(adjoint.shape), bytes_accessed=4000000, transcendentals=0
        ),
    )
    (column,) = local_call(
        functools.partial(extend_kernel, y_pairs),
        "add_y_faces",
        [*y_got, *y_sent, *ends_got, *ends_sent, middle, norm],
        [(rows, lanes)],
    )
    if z_pairs == 1:
        other = swap(column, "depth", 0)
    else:
        other = lax.psum(column, "depth") - column
    if y_pairs:
        (new_adjoint,) = local_call(
            functools.partial(row_kernel, y_pairs),
            "add_y_rows",
            [new_adjoint, edge_rows, design, solid_mask, port_label, *y_got, *ends_got],
            [adjoint.shape],
            scratch=[
                pltpu.VMEM((y_pairs, len(velocities), levels, tile, lanes), jnp.float32),
                pltpu.SemaphoreType.DMA((y_pairs,)),
            ],
            far=(0,),
            far_out=(0,),
            aliases={0: 0},
        )
    (sensitivity,) = local_call(
        filter_kernel, "add_depth", [column, other], [(rows, lanes)]
    )
    return (new_adjoint, sensitivity)


def solution(mesh):
    in_specs = (
        P(None, "depth", "gy", "gx"),
        P(None, "depth", "gy", "gx"),
        P("gy", "gx"),
        P("depth", "gy", "gx"),
        P("depth", "gy", "gx"),
    )
    out_specs = (P(None, "depth", "gy", "gx"), P("gy", "gx"))
    return jax.shard_map(
        on_device, mesh=mesh, in_specs=in_specs, out_specs=out_specs, check_vma=False
    )
```

```python
import functools
import math

import jax
import jax.numpy as jnp
from jax import lax
from jax.experimental import pallas as pl
from jax.experimental.pallas import tpu as pltpu
from jax.sharding import PartitionSpec as P

velocities = (
    (0, 0, 0),
    (1, 0, 0),
    (-1, 0, 0),
    (0, 1, 0),
    (0, -1, 0),
    (0, 0, 1),
    (0, 0, -1),
    (1, 1, 0),
    (-1, -1, 0),
    (1, -1, 0),
    (-1, 1, 0),
    (1, 0, 1),
    (-1, 0, -1),
    (1, 0, -1),
    (-1, 0, 1),
    (0, 1, 1),
    (0, -1, -1),
    (0, 1, -1),
    (0, -1, 1),
)
lattice_weights = (1.0 / 3.0,) + (1.0 / 18.0,) * 6 + (1.0 / 36.0,) * 12
opposite = (0, 2, 1, 4, 3, 6, 5, 8, 7, 10, 9, 12, 11, 14, 13, 16, 15, 18, 17)
relax_rate = 1.25
damp_top = 0.5
cone_radius = 5.0
filter_reach = 4
wide = filter_reach + 1
tile = 8
level_group = 3
laterals = ((0, 0), (1, 0), (-1, 0), (0, 1), (0, -1))
lateral_weights = (1.0 / 18.0,) + (1.0 / 36.0,) * 4
kinds = len(laterals) + 3
both_ends = 2 * wide


def spot(kind):
    return 2 * kind + 1 if kind < kinds // 2 else 2 * kind - kinds


def x_lane(level, kind):
    return (level + 1) * tile + tile // 2 + spot(kind)


def crossing(axis, sign):
    others = [other for other in range(3) if other != axis]
    return [
        next(
            number
            for number, vector in enumerate(velocities)
            if vector[axis] == sign and (vector[others[0]], vector[others[1]]) == lateral
        )
        for lateral in laterals
    ]


def cone(offset_y, offset_x):
    return max(0.0, cone_radius - math.sqrt(offset_y * offset_y + offset_x * offset_x))


def pairings(axis):
    return range(min(lax.axis_size(axis) - 1, 2))


def swap(array, axis, pairing):
    size, cores = (lax.axis_size(axis), lax.axis_size("depth"))
    pairs = []
    for low in range(pairing, size - 1, 2):
        pairs += [(low, low + 1), (low + 1, low)]
    alone = [place for place in range(size) if place not in dict(pairs)]
    if axis == "depth" or cores % 2 != 0 or not alone:
        return lax.ppermute(array, axis, pairs)
    full = [(a * cores + core, b * cores + core) for a, b in pairs for core in range(cores)]
    for place in alone:
        full += [(place * cores + core, place * cores + (core ^ 1)) for core in range(cores)]
    return lax.ppermute(array, (axis, "depth"), full)


def partner_after(axis, pairing):
    return lax.rem(lax.axis_index(axis) + pairing, 2) == 0


def partners(axis, pairing):
    place, after = (lax.axis_index(axis), partner_after(axis, pairing))
    none_before, none_after = (place == 0, place == lax.axis_size(axis) - 1)
    return (
        jnp.logical_not(jnp.logical_or(after, none_before)),
        jnp.logical_and(after, jnp.logical_not(none_after)),
    )


def present(axis, pairing, array):
    before, after = partners(axis, pairing)
    return pick(jnp.logical_or(before, after), array, jnp.zeros_like(array))


def pick(flag, yes, no):
    return lax.select(flag, yes, no)


def turn(array, shift, axis):
    shift = shift % array.shape[axis]
    return array if shift == 0 else pltpu.roll(array, shift, axis)


def lanes_of(shape):
    return lax.broadcasted_iota(jnp.int32, shape, len(shape) - 1)


def rows_of(shape):
    return lax.broadcasted_iota(jnp.int32, shape, len(shape) - 2)


def halves(axis, arrays):
    before, after = 0.0, 0.0
    for pairing, array in enumerate(arrays):
        is_before, is_after = partners(axis, pairing)
        none = jnp.zeros_like(array)
        before = before + pick(is_before, array, none)
        after = after + pick(is_after, array, none)
    return (before, after)


def depth_plane(adjoint, halo, number, level):
    levels = adjoint.shape[1]
    if 0 <= level < levels:
        return adjoint[number, level]
    sign = 1 if level == levels else -1
    side = halo[1] if sign > 0 else halo[0]
    return side[crossing(2, sign).index(number)]


def gain_of(momentum, scale, solid, port, level):
    kept = (solid[level] == 0) & (port[level] != 1)
    factor = jnp.where(kept, scale, 0.0)
    return [factor * momentum[part, level] for part in range(3)]


def along_x(plane, step):
    lane = lanes_of(plane.shape)
    edge = plane.shape[-1] - 1 if step > 0 else 0
    return jnp.where(lane == edge, 0.0, turn(plane, -step, 1))


def along_y(plane, step):
    row = rows_of(plane.shape)
    edge = plane.shape[-2] - 1 if step > 0 else 0
    return jnp.where(row == edge, 0.0, turn(plane, -step, 0))


def own_moment(take):
    heavy = lattice_weights[1] / lattice_weights[7]
    p = {
        number: take(number, vector[2]) for number, vector in enumerate(velocities) if number != 0
    }
    for number in (7, 8, 9, 10):
        p[number] = along_y(p[number], velocities[number][1])
    right_x = along_x(heavy * p[1] + ((p[7] + p[9]) + (p[11] + p[13])), 1)
    left_x = along_x(heavy * p[2] + ((p[8] + p[10]) + (p[12] + p[14])), -1)
    right_y = along_x((p[7] - p[9]), 1)
    left_y = along_x((p[10] - p[8]), -1)
    right_z = along_x((p[11] - p[13]), 1)
    left_z = along_x((p[14] - p[12]), -1)
    lower_y = along_y(heavy * p[3] + (p[15] + p[17]), 1)
    upper_y = along_y(heavy * p[4] + (p[16] + p[18]), -1)
    lower_z = along_y((p[15] - p[17]), 1)
    upper_z = along_y((p[18] - p[16]), -1)
    moment_x = right_x - left_x
    moment_y = (lower_y - upper_y) + (right_y + left_y)
    moment_z = heavy * (p[5] - p[6]) + ((right_z + left_z) + (lower_z + upper_z))
    return (moment_x, moment_y, moment_z)


def groups_of(levels):
    return [(low, min(low + level_group, levels)) for low in range(0, levels, level_group)]


def run_all(copies):
    for copy in copies:
        copy.start()
    for copy in copies:
        copy.wait()


def face_kernel(z_pairs, adjoint, *refs):
    outs, sems = (refs[:z_pairs], refs[z_pairs])
    copies = []
    for pairing in range(z_pairs):
        after = partner_after("depth", pairing)
        level = jnp.where(after, adjoint.shape[1] - 1, 0)
        for kind, numbers in enumerate(zip(crossing(2, -1), crossing(2, 1))):
            number = jnp.where(after, numbers[0], numbers[1])
            source, target = (adjoint.at[number, level], outs[pairing].at[kind])
            copies.append(pltpu.make_async_copy(source, target, sems.at[len(copies)]))
    run_all(copies)


def pack_kernel(counts, adjoint, momentum, design, solid, port, *refs):
    x_pairs, y_pairs = counts
    x_out, refs = (refs[:x_pairs], refs[x_pairs:])
    y_out, refs = (refs[:y_pairs], refs[y_pairs:])
    own_out, edge_gain = refs
    levels, rows, lanes = adjoint.shape[1:]
    slots = lanes // tile
    assert levels + 3 <= slots == 2 * tile and 2 * filter_reach <= tile
    scale = 6.0 * damp_top / ((1.0 + design[...]) * (1.0 + design[...]))
    lane = lanes_of((rows, lanes))
    for pairing in range(y_pairs):
        y_out[pairing][...] = jnp.zeros(y_out[pairing].shape, jnp.float32)
    total = jnp.zeros((rows, lanes), jnp.float32)
    joint = [jnp.zeros((rows, lanes), jnp.float32) for half in range(2)]
    for level in range(levels):
        gain = gain_of(momentum, scale, solid, port, level)
        moment = own_moment(
            lambda number, step: adjoint[number, level + step]
            if 0 <= level + step < levels
            else jnp.zeros((rows, lanes), jnp.float32)
        )
        total = total + (gain[0] * moment[0] + gain[1] * moment[1] + gain[2] * moment[2])
        for side, edge in enumerate((0, levels - 1)):
            if level == edge:
                for part in range(3):
                    edge_gain[side, part] = gain[part]
        for pairing in range(y_pairs):
            after = partner_after("gy", pairing)
            for part in range(3):
                place = (len(laterals) + part) * slots + level
                y_out[pairing][place : place + 1, :] = pick(
                    after, gain[part][rows - 1 : rows], gain[part][0:1]
                )
        for kind in range(kinds):
            if kind < len(laterals):
                first = adjoint[crossing(0, 1)[kind], level]
                last = adjoint[crossing(0, -1)[kind], level]
                plane = jnp.where(lane == lanes - 1, last, first)
            else:
                plane = gain[kind - len(laterals)]
            half, place = (kind // (kinds // 2), x_lane(level, kind) // 2 * 2)
            chosen = lane // 2 == place // 2
            joint[half] = jnp.where(chosen, turn(plane, place + 1, 1), joint[half])
    for pairing in range(y_pairs):
        after = partner_after("gy", pairing)
        for kind in range(len(laterals)):
            last, first = (crossing(1, -1)[kind], crossing(1, 1)[kind])
            step = laterals[kind][1]
            low, high = (max(step, 0), levels + min(step, 0))
            base = kind * slots - step
            y_out[pairing][base + low : base + high, :] = pick(
                after, adjoint[last, low:high, rows - 1, :], adjoint[first, low:high, 0, :]
            )
    own_out[...] = lattice_weights[7] * total
    odd = lane % 2 == 1
    first_pack = jnp.where(odd, joint[0], turn(joint[1], -1, 1))
    last_pack = jnp.where(odd, turn(joint[0], 1, 1), joint[1])
    for pairing in range(x_pairs):
        x_out[pairing][...] = pick(partner_after("gx", pairing), last_pack, first_pack)


def depth_kernel(counts, levels, *refs):
    x_pairs, y_pairs, z_pairs = counts
    z_got, refs = (refs[:z_pairs], refs[z_pairs:])
    x_pack, refs = (refs[:x_pairs], refs[x_pairs:])
    y_pack, refs = (refs[:y_pairs], refs[y_pairs:])
    own, edge_gain, refs = (*refs[:2], refs[2:])
    x_out, refs = (refs[:x_pairs], refs[x_pairs:])
    y_out, own_out = (refs[:y_pairs], refs[y_pairs])
    rows, lanes = own.shape
    slots = lanes // tile
    halo = halves("depth", [got[...] for got in z_got])
    lane = lanes_of((rows, lanes))
    total = own[...]
    if z_pairs:
        for side, sign in enumerate((-1, 1)):
            gain = [edge_gain[side, part] for part in range(3)]
            for kind, (step_x_, step_y_) in enumerate(laterals):
                plane = halo[side][kind]
                pull = sign * gain[2]
                if step_x_ != 0:
                    plane = along_x(plane, step_x_)
                    pull = pull + step_x_ * gain[0]
                if step_y_ != 0:
                    plane = along_y(plane, step_y_)
                    pull = pull + step_y_ * gain[1]
                total = total + lateral_weights[kind] * plane * pull
    own_out[...] = total
    beyond = ((3, levels, 1), (4, -1, 0))
    for pairing in range(y_pairs):
        after = partner_after("gy", pairing)
        y_out[pairing][0 : kinds * slots, :] = y_pack[pairing][...]
        y_out[pairing][kinds * slots :, :] = pick(after, total[rows - tile :], total[0:tile])
        if z_pairs:
            for kind, level, side in beyond:
                planes = crossing(2, 1 if side else -1)
                last, first = (
                    halo[side][planes.index(crossing(1, sign)[kind])] for sign in (-1, 1)
                )
                place = kind * slots + level - laterals[kind][1]
                y_out[pairing][place : place + 1, :] = pick(
                    after, last[rows - 1 : rows], first[0:1]
                )
    chosen = (lane < filter_reach) | (lane >= lanes - filter_reach)
    sums = jnp.where(chosen, total, 0.0)
    packs = []
    for edge_shift, sign in ((0, 1), (1, -1)):
        pack = sums
        if z_pairs:
            for kind, level, side in beyond:
                planes = crossing(2, 1 if side else -1)
                plane = halo[side][planes.index(crossing(0, sign)[kind])]
                place = x_lane(level, kind)
                pack = jnp.where(lane == place, turn(plane, place + edge_shift, 1), pack)
        packs.append(pack)
    for pairing in range(x_pairs):
        after = partner_after("gx", pairing)
        x_out[pairing][0:rows, :] = x_pack[pairing][...] + pick(after, packs[1], packs[0])
    lane = lanes_of((tile, lanes))
    for y_pairing in range(y_pairs):
        first, last = (jnp.zeros((tile, lanes), jnp.float32) for side in range(2))
        for kind in range(kinds):
            line = y_out[y_pairing][kind * slots : (kind + 1) * slots, :]
            upper, lower = (line[0:tile], line[tile:])
            place = kind * both_ends
            low = (lane >= place) & (lane < place + wide)
            high = (lane >= place + wide) & (lane < place + both_ends)
            upper = turn(upper, place + wide, 1)
            last = jnp.where(low, upper, jnp.where(high, turn(lower, place + both_ends, 1), last))
            first = jnp.where(high, upper, jnp.where(low, turn(lower, place, 1), first))
        base = rows + y_pairing * tile
        for pairing in range(x_pairs):
            after = partner_after("gx", pairing)
            x_out[pairing][base : base + tile, :] = pick(after, last, first)


def cross_x(levels, faces, gains, sign):
    rows = faces.shape[0]
    lane, row = (lanes_of(faces.shape), rows_of(faces.shape))
    first = x_lane(0, 0) - spot(0)
    gain = [turn(gains, -spot(len(laterals) + part), 1) for part in range(3)]
    terms = []
    for kind, (step_y, step_z) in enumerate(laterals):
        source = turn(faces, -spot(kind) - tile * step_z, 1)
        pull = sign * gain[0]
        if step_y != 0:
            edge = rows - 1 if step_y > 0 else 0
            source = jnp.where(row == edge, 0.0, turn(source, -step_y, 0))
            pull = pull + step_y * gain[1]
        if step_z != 0:
            pull = pull + step_z * gain[2]
        terms.append(lateral_weights[kind] * source * pull)
    used = (lane % tile == first % tile) & (lane >= first) & (lane < first + tile * levels)
    return jnp.sum(jnp.where(used, tree_sum(terms), 0.0), axis=1, keepdims=True)


def middle_kernel(counts, levels, *refs):
    x_pairs, y_pairs = counts
    x_got, refs = (refs[:x_pairs][::-1], refs[x_pairs:])
    x_sent, refs = (refs[:x_pairs], refs[x_pairs:])
    own, refs = (refs[0], refs[1:])
    y_out, middle = (refs[:y_pairs], refs[y_pairs])
    rows, lanes = own.shape
    slots = lanes // tile
    lane = lanes_of((rows, lanes))
    main = own[...]
    side, beside = (jnp.zeros((rows, lanes), jnp.float32) for part in range(2))
    free = spare_lanes(lanes)
    within = free + 2 * tile
    got_left, got_right = halves("gx", [got[0:rows, :] for got in x_got])
    sent_left, sent_right = halves("gx", [sent[0:rows, :] for sent in x_sent])
    if x_pairs:
        there_left = cross_x(levels, sent_left, got_left, 1)
        there_right = cross_x(levels, sent_right, got_right, -1)
        here_left = cross_x(levels, got_left, sent_left, -1)
        here_right = cross_x(levels, got_right, sent_right, 1)
        main = main + jnp.where(lane == 0, here_left, 0.0)
        main = main + jnp.where(lane == lanes - 1, here_right, 0.0)
        sums = jnp.where(lane < filter_reach, got_right, got_left)
        side = jnp.where(lane == 0, there_right, jnp.where(lane == lanes - 1, there_left, 0.0))
        chosen = (lane < filter_reach) | (lane >= lanes - filter_reach)
        side = side + jnp.where(chosen, sums, 0.0)
        beside = jnp.where(lane == free, there_right, 0.0)
        beside = beside + jnp.where(lane == free - 1, there_left, 0.0)
        beside = beside + jnp.where(lane == within, here_left, 0.0)
        beside = beside + jnp.where(lane == within - 1, here_right, 0.0)
        chosen = (lane >= free - filter_reach) & (lane < free + filter_reach)
        beside = beside + jnp.where(chosen, turn(sums, free, 1), 0.0)
    middle[0] = main
    middle[1] = side
    lane = lanes_of((slots, lanes))
    for pairing in range(y_pairs):
        after = partner_after("gy", pairing)
        out = y_out[pairing]
        ends = jnp.zeros((slots, lanes), jnp.float32)
        if x_pairs:
            base = rows + pairing * tile
            left, right = halves("gx", [got[base : base + tile, :] for got in x_got])
            low = lane[0:tile] % both_ends < wide
            upper = jnp.where(low, left, right)
            lower = jnp.where(low, turn(left, -wide, 1), turn(right, wide, 1))
            ends = jnp.concatenate([upper, lower], axis=0)
        ends = jnp.where(lane < kinds * both_ends, ends, 0.0)
        out[0:tile, :] = ends[0:tile] + pick(after, beside[rows - tile :], beside[0:tile])
        out[tile:slots, :] = ends[tile:]


def spare_lanes(lanes):
    assert kinds * both_ends + 4 * tile <= lanes and lanes & (lanes - 1) == 0
    return kinds * both_ends + tile


def step_x(line, ends, kind, step):
    lanes = line.shape[-1]
    main = turn(line, -step, 1)
    side = turn(ends, -kind * both_ends - wide - step, 1)
    if step == 0:
        return (main, side)
    edge = lanes_of(line.shape) == (lanes - 1 if step > 0 else 0)
    return (jnp.where(edge, side, main), jnp.where(edge, main, side))


def cross_y(faces, gains, sign):
    (lines, ends), (gain_lines, gain_ends) = (faces, gains)
    gain = [
        step_x(gain_lines[len(laterals) + part], gain_ends, len(laterals) + part, 0)
        for part in range(3)
    ]
    total_main, total_side = (0.0, 0.0)
    for kind, (lateral_x, lateral_z) in enumerate(laterals):
        main, side = step_x(lines[kind], ends, kind, lateral_x)
        pull_main, pull_side = (sign * gain[1][0], sign * gain[1][1])
        if lateral_x != 0:
            pull_main = pull_main + lateral_x * gain[0][0]
            pull_side = pull_side + lateral_x * gain[0][1]
        if lateral_z != 0:
            pull_main = pull_main + lateral_z * gain[2][0]
            pull_side = pull_side + lateral_z * gain[2][1]
        total_main = total_main + lateral_weights[kind] * main * pull_main
        total_side = total_side + lateral_weights[kind] * side * pull_side
    return (
        jnp.sum(total_main, axis=0, keepdims=True),
        jnp.sum(total_side, axis=0, keepdims=True),
    )


def face_lines(lines, ends, slots):
    return (
        [lines[kind * slots : (kind + 1) * slots] for kind in range(kinds)],
        ends[0:slots],
    )


def extend_kernel(y_pairs, *refs):
    y_got, refs = (refs[:y_pairs], refs[y_pairs:])
    y_sent, refs = (refs[:y_pairs], refs[y_pairs:])
    ends_got, refs = (refs[:y_pairs], refs[y_pairs:])
    ends_sent, refs = (refs[:y_pairs], refs[y_pairs:])
    middle, norm, out = refs
    rows, lanes = middle.shape[1:]
    slots = lanes // tile
    row, row_tile, lane_tile = (
        rows_of((rows, lanes)),
        rows_of((tile, lanes)),
        lanes_of((tile, lanes)),
    )
    own = [middle[0], middle[1]]
    before = [jnp.zeros((tile, lanes), jnp.float32) for part in range(2)]
    after = [jnp.zeros((tile, lanes), jnp.float32) for part in range(2)]
    for pairing in range(y_pairs):
        flag = partner_after("gy", pairing)
        sign = jnp.where(flag, 1.0, -1.0)
        got_lines = present("gy", pairing, y_got[pairing][...])
        got_ends = present("gy", pairing, ends_got[pairing][...])
        got = face_lines(got_lines, got_ends, slots)
        sent = face_lines(y_sent[pairing][...], ends_sent[pairing][...], slots)
        there = cross_y(sent, got, -sign)
        here = cross_y(got, sent, sign)
        edge_here = jnp.where(flag, rows - 1, 0)
        edge_there = jnp.where(flag, 0, tile - 1)
        for part in range(2):
            if part == 0:
                within = turn(got_ends[0:tile], -spare_lanes(lanes) - 2 * tile, 1)
                edge = (lane_tile == 0) | (lane_tile == lanes - 1)
                sums = got_lines[kinds * slots :] + jnp.where(edge, within, 0.0)
            else:
                sums = turn(got_ends[0:tile], -spare_lanes(lanes), 1)
            sums = sums + jnp.where(row_tile == edge_there, there[part], 0.0)
            none = jnp.zeros_like(sums)
            before[part] = before[part] + pick(flag, none, sums)
            after[part] = after[part] + pick(flag, sums, none)
            own[part] = own[part] + jnp.where(row == edge_here, here[part], 0.0)
    main, side = (
        jnp.concatenate([before[part], own[part], after[part]], axis=0) for part in range(2)
    )
    out[...] = cone_sum(main, side, rows) * norm[...]


def cone_sum(main, side, rows):
    lanes = main.shape[-1]
    lane = lanes_of(main.shape)
    pairs = [main]
    for offset in range(1, filter_reach + 1):
        up = jnp.where(lane < lanes - offset, turn(main, -offset, 1), turn(side, -offset, 1))
        down = jnp.where(lane >= offset, turn(main, offset, 1), turn(side, offset, 1))
        pairs.append(up + down)
    terms = []
    for offset in range(filter_reach + 1):
        weights = [cone(offset, distance) for distance in range(filter_reach + 1)]
        weighted = tree_sum([weight * pair for weight, pair in zip(weights, pairs) if weight > 0.0])
        for step in sorted({offset, -offset}):
            terms.append(turn(weighted, -step, 0)[tile : tile + rows])
    return tree_sum(terms)


def tree_sum(terms):
    while len(terms) > 1:
        terms = [sum(terms[place + 1 : place + 2], terms[place]) for place in range(0, len(terms), 2)]
    return terms[0]


def filter_kernel(mine, other, out):
    out[...] = mine[...] + other[...]


def filter_norm(rows, lanes):
    shape = (rows + 2 * tile, lanes)
    row, lane = (rows_of(shape), lanes_of(shape))
    place = lax.axis_index("gy") * rows + row - tile
    inside = jnp.where((place >= 0) & (place < lax.axis_size("gy") * rows), 1.0, 0.0)
    left = (lax.axis_index("gx") > 0).astype(jnp.float32)
    right = (lax.axis_index("gx") < lax.axis_size("gx") - 1).astype(jnp.float32)
    beside = inside * jnp.where(lane < lanes // 2, right, left)
    return 1.0 / cone_sum(inside, beside, rows)


def collide_kernel(counts, adjoint, design, solid, port, *refs):
    x_pairs, y_pairs, z_pairs = counts
    x_got, refs = (refs[:x_pairs][::-1], refs[x_pairs:])
    z_got, refs = (refs[:z_pairs], refs[z_pairs:])
    far, edge_rows, norm, out, sems = refs
    levels, rows, lanes = adjoint.shape[1:]
    slots = lanes // tile
    halo_z = halves("depth", [got[...] for got in z_got])
    halo_x = halves("gx", [got[0:rows, :] for got in x_got])
    damping = damp_top * (1.0 - design[...]) / (1.0 + design[...])
    rate = 3.0 * (relax_rate - damping)
    lane = lanes_of((rows, lanes))
    copies = []
    for level in range(levels):
        pulled = []
        for number, (step_x_, step_y_, step_z_) in enumerate(velocities):
            source = level + step_z_
            if z_pairs or 0 <= source < levels:
                plane = depth_plane(adjoint, halo_z, number, source)
            else:
                plane = jnp.zeros((rows, lanes), jnp.float32)
            if step_x_ != 0:
                edge = lanes - 1 if step_x_ > 0 else 0
                column = 0.0
                if x_pairs:
                    kind = crossing(0, step_x_).index(number)
                    side = halo_x[1 if step_x_ > 0 else 0]
                    column = turn(side, edge - x_lane(source, kind), 1)
                plane = jnp.where(lane == edge, column, turn(plane, -step_x_, 1))
            if step_y_ != 0:
                plane = along_y(plane, step_y_)
            pulled.append(plane)
        zeroth, moment = sums_of(pulled)
        base = relax_rate * zeroth
        scaled = [rate * part for part in moment]
        fluid, inlet = (solid[level] == 0, port[level] == 1)
        outflow = jnp.where(port[level] == 2, 1.0, 0.0)
        for number, vector in enumerate(velocities):
            updated = base + (1.0 - relax_rate) * pulled[number]
            if number > 0:
                updated = updated + along(vector, scaled)
            updated = jnp.where(fluid, updated, pulled[opposite[number]])
            updated = jnp.where(inlet, 0.0, updated)
            if vector[0] != 0:
                updated = updated + vector[0] * outflow
            out[number, level] = updated
        for place, (low, high) in enumerate(groups_of(levels)):
            if level == high - 1:
                copy = pltpu.make_async_copy(
                    out.at[:, low:high], far.at[:, low:high], sems.at[place]
                )
                copy.start()
                copies.append(copy)
    for pairing in range(y_pairs):
        after = partner_after("gy", pairing)
        for number in range(len(velocities)):
            edge_rows[pairing, number] = pick(after, out[number, :, rows - 1, :], out[number, :, 0, :])
    norm[...] = filter_norm(rows, lanes)
    for copy in copies:
        copy.wait()


def along(vector, parts):
    total = 0.0
    for component, part in zip(vector, parts):
        if component > 0:
            total = total + part
        if component < 0:
            total = total - part
    return total


def sums_of(pulled):
    heavy, light = (lattice_weights[1], lattice_weights[7])
    both, gap = ({}, {})
    for number in range(1, len(velocities), 2):
        both[number] = pulled[number] + pulled[number + 1]
        gap[number] = pulled[number] - pulled[number + 1]
    zeroth = lattice_weights[0] * pulled[0] + heavy * ((both[1] + both[3]) + both[5])
    zeroth = zeroth + light * (((both[7] + both[9]) + (both[11] + both[13])) + (both[15] + both[17]))
    moment = (
        heavy * gap[1] + light * ((gap[7] + gap[9]) + (gap[11] + gap[13])),
        heavy * gap[3] + light * ((gap[7] - gap[9]) + (gap[15] + gap[17])),
        heavy * gap[5] + light * ((gap[11] - gap[13]) + (gap[15] - gap[17])),
    )
    return (zeroth, moment)


def row_kernel(y_pairs, new, edge_rows, design, solid, port, *refs):
    y_got, refs = (refs[:y_pairs], refs[y_pairs:])
    ends_got, (far, out, sems) = (refs[:y_pairs], refs[y_pairs:])
    levels, rows, lanes = solid.shape
    slots = lanes // tile
    copies = []
    for pairing in range(y_pairs):
        after = partner_after("gy", pairing)
        sign = jnp.where(after, 1.0, -1.0)
        got = present("gy", pairing, y_got[pairing][...])
        ends = present("gy", pairing, ends_got[pairing][0:slots, :])
        extra, moment = ({}, [0.0, 0.0, 0.0])
        zeroth = 0.0
        for kind, (lateral_x, lateral_z) in enumerate(laterals):
            line = got[kind * slots : (kind + 1) * slots]
            if lateral_x != 0:
                line = step_x(line, ends, kind, lateral_x)[0]
            line = line[0:levels]
            none = jnp.zeros_like(line)
            extra[crossing(1, 1)[kind]] = pick(after, line, none)
            extra[crossing(1, -1)[kind]] = pick(after, none, line)
            weighted = lateral_weights[kind] * line
            zeroth = zeroth + weighted
            moment[0] = moment[0] + lateral_x * weighted
            moment[2] = moment[2] + lateral_z * weighted
        moment[1] = sign * zeroth
        edge_design = pick(after, design[rows - 1 : rows, :], design[0:1, :])
        damping = damp_top * (1.0 - edge_design) / (1.0 + edge_design)
        rate = 3.0 * (relax_rate - damping)
        fluid = pick(after, solid[:, rows - 1, :], solid[:, 0, :]) == 0
        inlet = pick(after, port[:, rows - 1, :], port[:, 0, :]) == 1
        scaled = [rate * part for part in moment]
        base = relax_rate * zeroth
        for number, vector in enumerate(velocities):
            added = base
            if number > 0:
                added = added + along(vector, scaled)
            if number in extra:
                added = added + (1.0 - relax_rate) * extra[number]
            added = jnp.where(fluid, added, extra.get(opposite[number], 0.0))
            added = jnp.where(inlet, 0.0, added)
            out[pairing, number, :, 0, :] = edge_rows[pairing, number] + added
        place = jnp.where(after, rows - 1, 0)
        copies.append(
            pltpu.make_async_copy(
                out.at[pairing, :, :, 0:1, :], far.at[:, :, pl.ds(place, 1), :], sems.at[pairing]
            )
        )
        copies[-1].start()
    for copy in copies:
        copy.wait()


def local_call(body, name, operands, out_shapes, scratch=(), far=(), far_out=(), aliases=None, room=16, cost=None):
    near_spec = pl.BlockSpec(memory_space=pltpu.VMEM)
    far_spec = pl.BlockSpec(memory_space=pltpu.HBM)
    shapes = [
        jax.ShapeDtypeStruct(shape, jnp.float32) if isinstance(shape, tuple) else shape
        for shape in out_shapes
    ]
    return pl.pallas_call(
        body,
        out_shape=shapes,
        in_specs=[far_spec if place in far else near_spec for place in range(len(operands))],
        out_specs=[far_spec if place in far_out else near_spec for place in range(len(shapes))],
        scratch_shapes=list(scratch),
        input_output_aliases=aliases or {},
        compiler_params=pltpu.CompilerParams(vmem_limit_bytes=room * 1024 * 1024),
        name=name,
        cost_estimate=cost,
    )(*operands)


def on_device(adjoint, momentum, design, solid_mask, port_label):
    levels, rows, lanes = adjoint.shape[1:]
    slots = lanes // tile
    groups = len(groups_of(levels))
    x_pairs, y_pairs, z_pairs = (len(pairings(axis)) for axis in ("gx", "gy", "depth"))
    z_got = []
    if z_pairs:
        faces = local_call(
            functools.partial(face_kernel, z_pairs),
            "depth_faces",
            [pltpu.with_memory_space_constraint(adjoint, pltpu.HBM)],
            [pltpu.VMEM((len(laterals), rows, lanes), jnp.float32)] * z_pairs,
            scratch=[pltpu.SemaphoreType.DMA((z_pairs * len(laterals),))],
            far=(0,),
            cost=pl.CostEstimate(flops=2000 * math.prod(adjoint.shape), bytes_accessed=100000, transcendentals=0),
        )
        z_got = [swap(face, "depth", pairing) for pairing, face in enumerate(faces)]
    packed = local_call(
        functools.partial(pack_kernel, (x_pairs, y_pairs)),
        "pack_faces",
        [adjoint, momentum, design, solid_mask, port_label],
        [(rows, lanes)] * x_pairs
        + [(kinds * slots, lanes)] * y_pairs
        + [(rows, lanes), (2, 3, rows, lanes)],
    )
    filled = local_call(
        functools.partial(depth_kernel, (x_pairs, y_pairs, z_pairs), levels),
        "add_z_faces",
        [*z_got, *packed],
        [(rows + y_pairs * tile, lanes)] * x_pairs
        + [(kinds * slots + tile, lanes)] * y_pairs
        + [(rows, lanes)],
    )
    x_sent, y_sent, own = (
        filled[:x_pairs],
        filled[x_pairs : x_pairs + y_pairs],
        filled[x_pairs + y_pairs],
    )
    y_got = [swap(y_sent[pairing], "gy", pairing) for pairing in range(y_pairs)]
    x_got = [None] * x_pairs
    for pairing in reversed(range(x_pairs)):
        x_got[pairing] = swap(x_sent[pairing], "gx", pairing)
    merged = local_call(
        functools.partial(middle_kernel, (x_pairs, y_pairs), levels),
        "add_x_faces",
        [*x_got[::-1], *x_sent, own],
        [(slots, lanes)] * y_pairs + [(2, rows, lanes)],
    )
    ends_sent, middle = (merged[:y_pairs], merged[y_pairs])
    ends_got = [swap(ends_sent[pairing], "gy", pairing) for pairing in range(y_pairs)]
    new_adjoint, edge_rows, norm = local_call(
        functools.partial(collide_kernel, (x_pairs, y_pairs, z_pairs)),
        "collide",
        [adjoint, design, solid_mask, port_label, *x_got[::-1], *z_got],
        [adjoint.shape, (max(y_pairs, 1), len(velocities), levels, lanes), (rows, lanes)],
        scratch=[pltpu.VMEM(adjoint.shape, jnp.float32), pltpu.SemaphoreType.DMA((groups,))],
        far_out=(0,),
        cost=pl.CostEstimate(
            flops=8000 * math.prod(adjoint.shape), bytes_accessed=4000000, transcendentals=0
        ),
    )
    (column,) = local_call(
        functools.partial(extend_kernel, y_pairs),
        "add_y_faces",
        [*y_got, *y_sent, *ends_got, *ends_sent, middle, norm],
        [(rows, lanes)],
    )
    if z_pairs == 1:
        other = swap(column, "depth", 0)
    else:
        other = lax.psum(column, "depth") - column
    if y_pairs:
        (new_adjoint,) = local_call(
            functools.partial(row_kernel, y_pairs),
            "add_y_rows",
            [new_adjoint, edge_rows, design, solid_mask, port_label, *y_got, *ends_got],
            [adjoint.shape],
            scratch=[
                pltpu.VMEM((y_pairs, len(velocities), levels, tile, lanes), jnp.float32),
                pltpu.SemaphoreType.DMA((y_pairs,)),
            ],
            far=(0,),
            far_out=(0,),
            aliases={0: 0},
        )
    (sensitivity,) = local_call(
        filter_kernel, "add_depth", [column, other], [(rows, lanes)]
    )
    return (new_adjoint, sensitivity)


def solution(mesh):
    in_specs = (
        P(None, "depth", "gy", "gx"),
        P(None, "depth", "gy", "gx"),
        P("gy", "gx"),
        P("depth", "gy", "gx"),
        P("depth", "gy", "gx"),
    )
    out_specs = (P(None, "depth", "gy", "gx"), P("gy", "gx"))
    return jax.shard_map(
        on_device, mesh=mesh, in_specs=in_specs, out_specs=out_specs, check_vma=False
    )
```
